32 devices in a mesh: cuts: 4 (over z), group: 8 (over y, x, core).
Axes of the slice: x: 2, y: 2, z: 4, core: 2. Of those that a mesh axis runs over, the one named last changes fastest.
Arguments:
- radiation: float32 [32, 2, 128, 128], P(('cuts', 'group')), may hold values from -6 to 6
- phases: float32 [32, 16, 128], P(('cuts', 'group')), may hold values from -3.140625 to 3.140625
- energy: float32 [32, 16, 128], P(('cuts', 'group')), may hold values from -5 to 5
- pixels: int32 [32, 16, 128], P(('cuts', 'group')), may hold values from 0 to 16383
- destination: int32 [32, 16], P(('cuts', 'group')), may hold values from 0 to 3, as said below
- propagator: float32 [2, 128, 128], replicated, may hold values from -1 to 1
- transmit: float32 [2, 32], replicated, may hold values from -1 to 1
Outputs:
- radiation_out: float32 [32, 2, 128, 128], P(('cuts', 'group'))
The draws below stay inside these ranges and needn't reach their ends.
Inputs may be any that keep to these rules, and one draw needn't show every extreme that they name: `destination`: the blocks of one slice go to exactly 2 different cuts, 8 blocks to each; in every draw some cut receives 8 blocks from every slice of the same position within a cut.
All inputs are finite; a program needn't handle non-finite values.
Results may differ from the reference program's by a relative error of at most 0.0011.
Values sent between devices are 32-bit elements; how exact they have to be, the bound alone decides.
No kernel may reach another device: no remote copies, remote signals or barrier semaphores. Data moves between devices by JAX's collectives and lax.ppermute only.
A program may use at most 64 MiB of HBM per device.

```python
import math
import jax
import jax.numpy as jnp
from jax import lax

GRID = 128
BLOCK = 128
BLOCKS = 16
STEPS = 2
SLICES = 32
SEND_CAP = 8
HOT_CUTS = 1
N_CUTS = 4
N_GROUP = 8


def draw_destination(key, part):
    key_offset, key_score, key_order = jax.random.split(key, 3)
    cut_ids = jnp.arange(N_CUTS, dtype=jnp.int32)
    offset = jax.random.randint(key_offset, (), 0, N_CUTS)
    hot_mask = ((cut_ids - offset) % N_CUTS < HOT_CUTS).astype(jnp.int32)
    base_score = jax.random.randint(key_score, (SLICES, N_CUTS), 0, 1000)
    score = (base_score + 1000 * hot_mask[None, :]) * N_CUTS + cut_ids[None, :]
    ranking = jnp.argsort(-score, axis=1)
    picked = ranking[:, :BLOCKS // SEND_CAP]
    order_key = jax.random.randint(key_order, (SLICES, BLOCKS), 0, 1 << 20) * BLOCKS + jnp.arange(BLOCKS, dtype=jnp.int32)[None, :]
    shuffle = jnp.argsort(order_key, axis=1)
    chosen = jnp.take_along_axis(picked, shuffle // SEND_CAP, axis=1)
    return chosen.astype(jnp.int32)


def draw_propagator(key, part):
    key_real, key_imag = jax.random.split(key, 2)
    amplitude = 0.52 / math.sqrt(GRID)
    real_part = jax.random.uniform(key_real, (GRID, GRID), jnp.float32, -amplitude, amplitude)
    imag_part = jax.random.uniform(key_imag, (GRID, GRID), jnp.float32, -amplitude, amplitude)
    real_part = real_part + 0.8 * jnp.eye(GRID, dtype=jnp.float32)
    return jnp.stack([real_part, imag_part])


def plant(array, rng, smallest, largest):
    longest = array.shape.index(max(array.shape))
    spots = []
    for shift in (0, 1):
        where = [jax.random.randint(jax.random.fold_in(rng, axis), (), 0, length) for axis, length in enumerate(array.shape)]
        where[longest] = (where[longest] + shift) % array.shape[longest]
        spots.append(tuple(where))
    return array.at[spots[0]].set(smallest).at[spots[1]].set(largest)


def levels(stream_key, extent, pieces, low, top_value):
    def one(dim, shards_of):
        heights = jax.random.uniform(jax.random.fold_in(jax.random.fold_in(stream_key, 6), dim), (shards_of,), jnp.float32, low / len(pieces), top_value / len(pieces))
        return jnp.repeat(jnp.exp(heights), extent[dim] // shards_of).reshape((-1,) + (1,) * (len(extent) - dim - 1))

    level = one(*pieces[0])
    for cut in pieces[1:]:
        level = level * one(*cut)
    return level


def centred(rng, dims, width, most, cuts=(), held_as=jnp.bfloat16):
    result = width * jax.random.normal(rng, dims, jnp.float32)
    if cuts:
        result = result * levels(rng, dims, cuts, -0.22, 0.18)
    return jnp.clip(result, -most, most).astype(held_as)


def setup_inputs(seed: int = 0) -> dict:
    streams_of = jax.random.split(jax.random.key(seed), 8)
    return {
        "radiation": centred(streams_of[0], (SLICES, 2, GRID, GRID), 1.0, 6.0, ((0, 32),), jnp.float32),
        "phases": jnp.clip(jax.random.uniform(streams_of[1], (SLICES, BLOCKS, BLOCK), jnp.float32, -3.140625, 3.140625), -3.140625, 3.140625),
        "energy": centred(streams_of[2], (SLICES, BLOCKS, BLOCK), 1.0, 5.0, ((0, 32),), jnp.float32),
        "pixels": plant(jax.random.randint(streams_of[3], (SLICES, BLOCKS, BLOCK), 0, GRID * GRID), jax.random.fold_in(streams_of[3], 1), 0, (GRID * GRID) - 1).astype(jnp.int32),
        "destination": draw_destination(jax.random.fold_in(streams_of[7], 71), 0),
        "propagator": draw_propagator(jax.random.fold_in(streams_of[7], 71), 0),
        "transmit": jnp.clip(jax.random.uniform(streams_of[6], (2, SLICES), jnp.float32, -1.0, 1.0), -1.0, 1.0),
    }


KICK_RATE = 0.5
PHASE_RATE = 1.0
EMIT_RATE = 0.5


def rounded(values):
    low_values = values.astype(jnp.bfloat16)
    low_values = lax.optimization_barrier(low_values)
    return low_values.astype(jnp.float32)


def diffract(real_part, imag_part, propagator):
    highest = lax.Precision.HIGHEST
    left_real = jnp.einsum("ij,sjk->sik", propagator[0], real_part, precision=highest) - jnp.einsum("ij,sjk->sik", propagator[1], imag_part, precision=highest)
    left_imag = jnp.einsum("ij,sjk->sik", propagator[0], imag_part, precision=highest) + jnp.einsum("ij,sjk->sik", propagator[1], real_part, precision=highest)
    out_real = jnp.einsum("sik,lk->sil", left_real, propagator[0], precision=highest) - jnp.einsum("sik,lk->sil", left_imag, propagator[1], precision=highest)
    out_imag = jnp.einsum("sik,lk->sil", left_real, propagator[1], precision=highest) + jnp.einsum("sik,lk->sil", left_imag, propagator[0], precision=highest)
    return out_real, out_imag


def undulate(real_part, imag_part, phases, energy, home, row_index, col_index, propagator):
    real_low = rounded(real_part)
    imag_low = rounded(imag_part)
    read_real = real_low[home, row_index, col_index]
    read_imag = imag_low[home, row_index, col_index]
    energy = energy - KICK_RATE * (read_real * jnp.cos(phases) - read_imag * jnp.sin(phases))
    phases = phases + PHASE_RATE * energy
    weight_real = rounded(jnp.cos(phases))
    weight_imag = rounded(-jnp.sin(phases))
    source_real = jnp.zeros_like(real_part).at[home, row_index, col_index].add(weight_real)
    source_imag = jnp.zeros_like(imag_part).at[home, row_index, col_index].add(weight_imag)
    real_part = real_part + EMIT_RATE * source_real
    imag_part = imag_part + EMIT_RATE * source_imag
    real_part, imag_part = diffract(real_part, imag_part, propagator)
    zero_slice = jnp.zeros_like(real_part[:1])
    real_part = jnp.concatenate([zero_slice, real_part[:-1]], axis=0)
    imag_part = jnp.concatenate([zero_slice, imag_part[:-1]], axis=0)
    return real_part, imag_part, phases, energy


def reference(radiation, phases, energy, pixels, destination, propagator, transmit):
    slice_count = radiation.shape[0]
    grid_size = radiation.shape[-1]
    real_part = radiation[:, 0]
    imag_part = radiation[:, 1]
    flat_phase = phases.reshape(-1)
    flat_energy = energy.reshape(-1)
    flat_pixel = pixels.reshape(-1)
    row_index = (flat_pixel // grid_size).astype(jnp.int32)
    col_index = (flat_pixel % grid_size).astype(jnp.int32)
    slice_ids = jnp.arange(slice_count, dtype=jnp.int32)
    home = jnp.broadcast_to(slice_ids[:, None, None], pixels.shape).reshape(-1)
    for step_index in range(STEPS):
        real_part, imag_part, flat_phase, flat_energy = undulate(real_part, imag_part, flat_phase, flat_energy, home, row_index, col_index, propagator)
    complex_field = real_part + 1j * imag_part
    gain = transmit[0] + 1j * transmit[1]
    filtered = jnp.fft.ifft(jnp.fft.fft(complex_field, axis=0) * gain[:, None, None], axis=0)
    real_part = jnp.real(filtered)
    imag_part = jnp.imag(filtered)
    new_home = destination[:, :, None] * N_GROUP + (slice_ids % N_GROUP)[:, None, None]
    home = jnp.broadcast_to(new_home, pixels.shape).reshape(-1).astype(jnp.int32)
    for step_index in range(STEPS):
        real_part, imag_part, flat_phase, flat_energy = undulate(real_part, imag_part, flat_phase, flat_energy, home, row_index, col_index, propagator)
    return jnp.stack([real_part, imag_part], axis=1)
```

```python
import functools
import math

import jax
import jax.numpy as jnp
from jax import lax
from jax.experimental import pallas as pl
from jax.experimental.pallas import tpu as pltpu
from jax.sharding import PartitionSpec as P

STEPS = 2

KICK_RATE = 0.5
PHASE_RATE = 1.0
EMIT_RATE = 0.5

AXES = ("cuts", "group")
F32 = jnp.float32
BF16 = jnp.bfloat16
VMEM_LIMIT = 48 * 1024 * 1024


def dot(left, right, left_dim, right_dim):
    dims = (((left_dim,), (right_dim,)), ((), ()))
    return lax.dot_general(left, right, dims, preferred_element_type=F32)


def exact_dot(left, right):
    return jnp.dot(left, right, precision=lax.Precision.HIGHEST, preferred_element_type=F32)


def split(value):
    high = value.astype(BF16)
    return high, (value - high.astype(F32)).astype(BF16)


def diffract(real, imag, propagator):
    size = real.shape[0]
    prop_real, prop_imag = propagator[0], propagator[1]
    form = jnp.concatenate(
        [
            jnp.concatenate([prop_real, -prop_imag], axis=1),
            jnp.concatenate([prop_imag, prop_real], axis=1),
        ],
        axis=0,
    )
    form_high, form_low = split(form)
    high, low = split(jnp.concatenate([real, imag], axis=1))
    both = dot(jnp.concatenate([high, low], axis=0), form_high, 1, 1)
    right = both[:size] + both[size:] + dot(high, form_low, 1, 1)
    high, low = split(jnp.concatenate([right[:, :size], right[:, size:]], axis=0))
    both = dot(form_high, jnp.concatenate([high, low], axis=1), 1, 0)
    out = both[:, :size] + both[:, size:] + dot(form_low, high, 1, 0)
    return out[:size], out[size:]


def cells(pixels, grid):
    shift = grid.bit_length() - 1
    if grid == 1 << shift:
        return lax.shift_right_arithmetic(pixels, shift), pixels & (grid - 1)
    return pixels // grid, pixels % grid


def chunks(blocks):
    width = 2 if blocks % 2 == 0 else 1
    return [(start, width) for start in range(0, blocks, width)]


def lanes(array, start, width):
    return jnp.concatenate([array[start + k : start + k + 1] for k in range(width)], axis=1)


def hits(ids, grid):
    return lax.broadcasted_iota(jnp.int32, (grid, ids.shape[1]), 0) == ids


def kick(real, imag, phases, energy, pixels, read_ref):
    grid = real.shape[0]
    blocks, size = phases.shape
    low = jnp.concatenate([real, imag], axis=1).astype(BF16)
    row, col = cells(pixels, grid)
    for start, width in chunks(blocks):
        row_hot = jnp.where(hits(lanes(row, start, width), grid), 1.0, 0.0).astype(BF16)
        picked = dot(low, row_hot, 0, 0)
        col_hit = hits(lanes(col, start, width), grid)
        for part in range(2):
            value = picked[part * grid : (part + 1) * grid]
            value = jnp.sum(jnp.where(col_hit, value, 0.0), axis=0, keepdims=True)
            for k in range(width):
                read_ref[part, start + k : start + k + 1, :] = value[:, k * size : (k + 1) * size]
    read_real = read_ref[0, :blocks, :]
    read_imag = read_ref[1, :blocks, :]
    energy = energy - KICK_RATE * (read_real * jnp.cos(phases) - read_imag * jnp.sin(phases))
    return phases + PHASE_RATE * energy, energy


def emit(real, imag, phases, pixels, row_ref, spread_ref):
    grid = real.shape[0]
    blocks, size = phases.shape
    row, col = cells(pixels, grid)
    weight_real = jnp.cos(phases)
    weight_imag = -jnp.sin(phases)
    for start, width in chunks(blocks):
        where = pl.ds(start * size, width * size)
        row_ref[:, where] = jnp.where(hits(lanes(row, start, width), grid), 1.0, 0.0).astype(BF16)
        col_hit = hits(lanes(col, start, width), grid)
        for part, weight in ((0, weight_real), (1, weight_imag)):
            value = jnp.where(col_hit, lanes(weight, start, width), 0.0)
            spread_ref[part * grid : (part + 1) * grid, where] = value.astype(BF16)
    span = blocks * size
    source = dot(row_ref[:, :span], spread_ref[:, :span], 1, 1)
    return real + EMIT_RATE * source[:, :grid], imag + EMIT_RATE * source[:, grid:]


def position():
    return lax.axis_index("cuts") * lax.axis_size("group") + lax.axis_index("group")


def kept_unless(index):
    return jnp.where(position() == index, 0.0, 1.0).astype(F32)


def kick_kernel(field, phases, energy, pixels, out, read_ref):
    blocks = phases.shape[0]
    new_phases, new_energy = kick(field[0], field[1], phases[...], energy[...], pixels[...], read_ref)
    out[0:blocks, :] = new_phases
    out[blocks : 2 * blocks, :] = new_energy
    out[2 * blocks : 3 * blocks, :] = pixels[...].astype(F32)


def radiate_kernel(count, field, state, propagator, out, row_ref, spread_ref):
    blocks = state.shape[0] // 3
    pixels = state[2 * blocks : 3 * blocks, :].astype(jnp.int32)
    real, imag = emit(field[0], field[1], state[0:blocks, :], pixels, row_ref, spread_ref)
    real, imag = diffract(real, imag, propagator)
    keep = kept_unless(count - 1)
    out[0] = real * keep
    out[1] = imag * keep


def second_kernel(count, rows, field, state, propagator, out, state_out, read_ref, row_ref, spread_ref):
    blocks = state.shape[0] // 3
    real, imag = field[0], field[1]
    grid = real.shape[0]
    pixels = state[2 * blocks : 3 * blocks, :].astype(jnp.int32)
    phases, energy = kick(real, imag, state[0:blocks, :], state[blocks : 2 * blocks, :], pixels, read_ref)
    state_out[0:blocks, :] = phases
    state_out[blocks : 2 * blocks, :] = energy
    state_out[2 * blocks : 3 * blocks, :] = state[2 * blocks : 3 * blocks, :]
    real, imag = emit(real, imag, phases, pixels, row_ref, spread_ref)
    real, imag = diffract(real, imag, propagator)
    keep = kept_unless(count - 2)
    real, imag = real * keep, imag * keep
    if rows:
        for part in range(grid // rows):
            out[part, 0:rows, :] = real[part * rows : (part + 1) * rows]
            out[part, rows : 2 * rows, :] = imag[part * rows : (part + 1) * rows]
    else:
        out[0] = real
        out[1] = imag


def matrix_kernel(transmit, cos_out, sin_out, cos_in, sin_in, out):
    count = cos_in.shape[0]
    gain_real, gain_imag = transmit[0:1, :], transmit[1:2, :]
    for which in range(2):
        cosine, sine = cos_out[which], sin_out[which]
        real = cosine * gain_real - sine * gain_imag
        imag = cosine * gain_imag + sine * gain_real
        full_real = exact_dot(real, cos_in[...]) + exact_dot(imag, sin_in[...])
        full_imag = exact_dot(imag, cos_in[...]) - exact_dot(real, sin_in[...])
        base = 2 * which * count
        out[base : base + count, :] = jnp.concatenate([full_real, -full_imag], axis=1)
        out[base + count : base + 2 * count, :] = jnp.concatenate([full_imag, full_real], axis=1)


def filter_kernel(rows, matrix, data, out):
    count = data.shape[0] // (2 * rows)
    size = data.shape[1]
    stacked = jnp.concatenate(
        [
            jnp.concatenate(
                [data[pl.ds(part * rows + j, count, stride=2 * rows), :] for part in range(2)], axis=0
            )
            for j in range(rows)
        ],
        axis=1,
    )
    result = exact_dot(matrix[...], stacked)
    for kind in range(4):
        for j in range(rows):
            out[pl.ds(kind * rows + j, count, stride=4 * rows), :] = result[
                kind * count : (kind + 1) * count, j * size : (j + 1) * size
            ]


def pick_kernel(cuts, groups, cap, near, destination, states, out, buffer, slots, sems):
    total = cuts * groups
    blocks = buffer.shape[2] // 3
    me = position()
    copies = []
    homes = []
    for which in range(2):
        home = lax.rem(me + (total - 2 + which), total)
        homes.append(home)
        for cut in range(cuts):
            source = cut * groups + lax.rem(home, groups)
            if near:
                held = states.at[lax.div(lax.rem(source + 2 - which, total), groups), which]
            else:
                held = states.at[lax.rem(source + total - 1, total)]
            copy = pltpu.make_async_copy(held, buffer.at[which, cut], sems.at[which, cut])
            copy.start()
            copies.append(copy)
    for copy in copies:
        copy.wait()
    capacity = cuts * cap
    for which in range(2):
        home = homes[which]
        wanted = lax.div(home, groups)
        place = lax.rem(home, groups)
        used = 0
        for cut in range(cuts):
            for block in range(blocks):
                for kind in range(3):
                    slots[which, kind, pl.ds(used, 1), :] = buffer[
                        which, cut, kind * blocks + block : kind * blocks + block + 1, :
                    ]
                goes = destination[(cut * groups + place) * blocks + block] == wanted
                used = used + jnp.where(goes, 1, 0)
        filled = lax.broadcasted_iota(jnp.int32, (capacity, out.shape[3]), 0) < used
        for kind, empty in ((0, 0.0), (1, 0.0), (2, -1.0)):
            out[which, kind] = jnp.where(filled, slots[which, kind, 0:capacity, :], empty)


def last_kernel(rows, fields, state, propagator, out, field_ref, read_ref, row_ref, spread_ref):
    grid = propagator.shape[1]
    if rows:
        for part in range(grid // rows):
            for kind in range(4):
                field_ref[kind, part * rows : (part + 1) * rows, :] = fields[
                    part, kind * rows : (kind + 1) * rows, :
                ]
    else:
        for kind in range(4):
            field_ref[kind] = fields[kind]
    first_pixels = state[0, 2].astype(jnp.int32)
    next_pixels = state[1, 2].astype(jnp.int32)
    real, imag = field_ref[0], field_ref[1]
    phases, _ = kick(real, imag, state[0, 0], state[0, 1], first_pixels, read_ref.at[0])
    real, imag = emit(real, imag, phases, first_pixels, row_ref, spread_ref)
    phases, energy = kick(field_ref[2], field_ref[3], state[1, 0], state[1, 1], next_pixels, read_ref.at[1])
    real, imag = diffract(real, imag, propagator)
    keep = kept_unless(1)
    real, imag = real * keep, imag * keep
    phases, _ = kick(real, imag, phases, energy, next_pixels, read_ref.at[0])
    real, imag = emit(real, imag, phases, next_pixels, row_ref, spread_ref)
    real, imag = diffract(real, imag, propagator)
    keep = kept_unless(0)
    out[0] = real * keep
    out[1] = imag * keep


def call(kernel, out_shape, scratch, flops, args, memory=None):
    memory = memory or {}
    specs = [pl.BlockSpec(memory_space=memory.get(k, pltpu.VMEM)) for k in range(len(args))]
    return pl.pallas_call(
        kernel,
        out_shape=out_shape,
        in_specs=specs,
        out_specs=jax.tree.map(lambda _: pl.BlockSpec(memory_space=pltpu.VMEM), out_shape),
        scratch_shapes=scratch,
        compiler_params=pltpu.CompilerParams(vmem_limit_bytes=VMEM_LIMIT),
        cost_estimate=pl.CostEstimate(flops=flops, bytes_accessed=1 << 19, transcendentals=0),
    )(*args)


def time_tables(count):
    times = jnp.arange(count, dtype=jnp.int32)
    outs = [angle_table((times + (count - lag)) % count, times, count) for lag in (4, 3)]
    cos_out = jnp.stack([cosine for cosine, _ in outs]) / count
    sin_out = jnp.stack([sine for _, sine in outs]) / count
    return (cos_out, sin_out, *angle_table(times, times, count))


def angle_table(first_ids, second_ids, total_slices):
    product = first_ids[:, None] * second_ids[None, :] % total_slices
    angle = product.astype(F32) * (2.0 * math.pi / total_slices)
    return jnp.cos(angle), jnp.sin(angle)


def filter_any(field, transmit, count):
    grid = field.shape[1]
    span = grid * grid
    share = -(-span // count)
    flat = jnp.pad(field.reshape(2, span), ((0, 0), (0, share * count - span)))
    parts = flat.reshape(2, count, share).transpose(1, 0, 2)
    got = lax.all_to_all(parts, AXES, split_axis=0, concat_axis=0, tiled=True)
    got = jnp.roll(got, 2, axis=0)
    real, imag = got[:, 0], got[:, 1]
    times = jnp.arange(count, dtype=jnp.int32)
    cosine, sine = angle_table(times, times, count)
    spec_real = exact_dot(cosine, real) + exact_dot(sine, imag)
    spec_imag = exact_dot(cosine, imag) - exact_dot(sine, real)
    gain_real, gain_imag = transmit[0][:, None], transmit[1][:, None]
    shaped_real = gain_real * spec_real - gain_imag * spec_imag
    shaped_imag = gain_real * spec_imag + gain_imag * spec_real
    back_real = (exact_dot(cosine, shaped_real) - exact_dot(sine, shaped_imag)) / count
    back_imag = (exact_dot(cosine, shaped_imag) + exact_dot(sine, shaped_real)) / count
    back = jnp.stack([back_real, back_imag], axis=1)
    sent = jnp.stack([jnp.roll(back, 2, axis=0), jnp.roll(back, 1, axis=0)], axis=1)
    fields = lax.all_to_all(sent, AXES, split_axis=0, concat_axis=0, tiled=True)
    fields = fields.transpose(1, 2, 0, 3).reshape(4, share * count)[:, :span]
    return fields.reshape(4, grid, grid)


def on_device(radiation, phases, energy, pixels, destination, propagator, transmit):
    cuts, groups = lax.axis_size("cuts"), lax.axis_size("group")
    count = cuts * groups
    grid = radiation.shape[-1]
    blocks, size = phases.shape[1:]
    cap = max(2, 2 * blocks // cuts)
    rows = grid // count if grid % count == 0 and (2 * grid // count) % 8 == 0 else 0
    field = radiation[0]
    shape = lambda *dims: jax.ShapeDtypeStruct(dims, F32)
    read = lambda number: pltpu.VMEM((2, number, size), F32)
    hot = lambda number: [pltpu.VMEM((grid, number * size), BF16), pltpu.VMEM((2 * grid, number * size), BF16)]
    pass_flops = 4 * blocks * size * grid * grid
    prop_flops = 48 * grid**3

    everywhere = lax.all_gather(destination[0], AXES, tiled=True)
    state = call(
        kick_kernel, shape(3 * blocks, size), [read(blocks)], pass_flops,
        (field, phases[0], energy[0], pixels[0]),
    )
    route = [((i + 1) % count, i) for i in range(count)]
    behind = lax.ppermute(state, AXES, route)
    field = call(
        functools.partial(radiate_kernel, count), shape(2, grid, grid), hot(blocks), pass_flops + prop_flops,
        (field, state, propagator),
    )
    part_shape = shape(count, 2 * rows, grid) if rows else shape(2, grid, grid)
    field, state = call(
        functools.partial(second_kernel, count, rows), (part_shape, shape(3 * blocks, size)),
        [read(blocks)] + hot(blocks), 2 * pass_flops + prop_flops,
        (field, behind, propagator),
    )
    if rows:
        matrix = call(
            matrix_kernel, shape(4 * count, 2 * count), [], 1 << 20, (transmit, *time_tables(count))
        )
        data = lax.all_to_all(field, AXES, split_axis=0, concat_axis=0, tiled=True)
        states = lax.all_gather(state, AXES)
        sent = call(
            functools.partial(filter_kernel, rows), shape(count * 4 * rows, grid), [], 1 << 24,
            (matrix, data.reshape(count * 2 * rows, grid)),
        )
        fields = lax.all_to_all(
            sent.reshape(count, 4 * rows, grid), AXES, split_axis=0, concat_axis=0, tiled=True
        )
    else:
        shifted = [
            lax.ppermute(state, AXES, [(i, (i + ahead) % count) for i in range(count)]) for ahead in (3, 2)
        ]
        states = lax.all_gather(jnp.stack(shifted), "cuts")
        fields = filter_any(field, transmit, count)
    capacity = cuts * cap
    picked = call(
        functools.partial(pick_kernel, cuts, groups, cap, not rows), shape(2, 3, capacity, size),
        [
            pltpu.VMEM((2, cuts, 3 * blocks, size), F32),
            pltpu.VMEM((2, 3, capacity + 8, size), F32),
            pltpu.SemaphoreType.DMA((2, cuts)),
        ],
        1 << 20, (everywhere, states), {0: pltpu.SMEM, 1: pl.ANY},
    )
    out = call(
        functools.partial(last_kernel, rows), shape(2, grid, grid),
        [pltpu.VMEM((4, grid, grid), F32), pltpu.VMEM((2, 2, capacity, size), F32)] + hot(capacity),
        10 * pass_flops + 2 * prop_flops, (fields, picked, propagator),
    )
    return out[None]


def solution(mesh):
    return jax.shard_map(
        on_device,
        mesh=mesh,
        in_specs=(
            P(("cuts", "group"), None, None, None),
            P(("cuts", "group"), None, None),
            P(("cuts", "group"), None, None),
            P(("cuts", "group"), None, None),
            P(("cuts", "group"), None),
            P(),
            P(),
        ),
        out_specs=P(("cuts", "group"), None, None, None),
        check_vma=False,
    )
```

```python
import functools
import math

import jax
import jax.numpy as jnp
from jax import lax
from jax.experimental import pallas as pl
from jax.experimental.pallas import tpu as pltpu
from jax.sharding import PartitionSpec as P

KICK_RATE = 0.5
PHASE_RATE = 1.0
EMIT_RATE = 0.5

AXES = ("cuts", "group")
F32 = jnp.float32
BF16 = jnp.bfloat16
VMEM_LIMIT = 48 * 1024 * 1024
WHOLE_VMEM = 60 * 1024 * 1024


def dot(left, right, left_dim, right_dim):
    dims = (((left_dim,), (right_dim,)), ((), ()))
    return lax.dot_general(left, right, dims, preferred_element_type=F32)


def exact_dot(left, right):
    return jnp.dot(left, right, precision=lax.Precision.HIGHEST, preferred_element_type=F32)


def split(value):
    high = value.astype(BF16)
    return high, (value - high.astype(F32)).astype(BF16)


def diffract(real, imag, propagator):
    size = real.shape[0]
    prop_real, prop_imag = propagator[0], propagator[1]
    form = jnp.concatenate(
        [
            jnp.concatenate([prop_real, -prop_imag], axis=1),
            jnp.concatenate([prop_imag, prop_real], axis=1),
        ],
        axis=0,
    )
    form_high, form_low = split(form)
    high, low = split(jnp.concatenate([real, imag], axis=1))
    both = dot(jnp.concatenate([high, low], axis=0), form_high, 1, 1)
    right = both[:size] + both[size:] + dot(high, form_low, 1, 1)
    high, low = split(jnp.concatenate([right[:, :size], right[:, size:]], axis=0))
    both = dot(form_high, jnp.concatenate([high, low], axis=1), 1, 0)
    out = both[:, :size] + both[:, size:] + dot(form_low, high, 1, 0)
    return out[:size], out[size:]


def cells(pixels, grid):
    shift = grid.bit_length() - 1
    if grid == 1 << shift:
        return lax.shift_right_arithmetic(pixels, shift), pixels & (grid - 1)
    return pixels // grid, pixels % grid


def chunks(blocks):
    width = 2 if blocks % 2 == 0 else 1
    return [(start, width) for start in range(0, blocks, width)]


def lanes(array, start, width):
    return jnp.concatenate([array[start + k : start + k + 1] for k in range(width)], axis=1)


def hits(ids, grid):
    return lax.broadcasted_iota(jnp.int32, (grid, ids.shape[1]), 0) == ids


def kick(real, imag, phases, energy, pixels, read_ref):
    grid = real.shape[0]
    blocks, size = phases.shape
    low = jnp.concatenate([real, imag], axis=1).astype(BF16)
    row, col = cells(pixels, grid)
    for start, width in chunks(blocks):
        row_hot = jnp.where(hits(lanes(row, start, width), grid), 1.0, 0.0).astype(BF16)
        picked = dot(low, row_hot, 0, 0)
        col_hit = hits(lanes(col, start, width), grid)
        for part in range(2):
            value = picked[part * grid : (part + 1) * grid]
            value = jnp.sum(jnp.where(col_hit, value, 0.0), axis=0, keepdims=True)
            for k in range(width):
                read_ref[part, start + k : start + k + 1, :] = value[:, k * size : (k + 1) * size]
    read_real = read_ref[0, :blocks, :]
    read_imag = read_ref[1, :blocks, :]
    energy = energy - KICK_RATE * (read_real * jnp.cos(phases) - read_imag * jnp.sin(phases))
    return phases + PHASE_RATE * energy, energy


def emit(real, imag, phases, pixels, row_ref, spread_ref):
    grid = real.shape[0]
    blocks, size = phases.shape
    row, col = cells(pixels, grid)
    weight_real = jnp.cos(phases)
    weight_imag = -jnp.sin(phases)
    for start, width in chunks(blocks):
        where = pl.ds(start * size, width * size)
        row_ref[:, where] = jnp.where(hits(lanes(row, start, width), grid), 1.0, 0.0).astype(BF16)
        col_hit = hits(lanes(col, start, width), grid)
        for part, weight in ((0, weight_real), (1, weight_imag)):
            value = jnp.where(col_hit, lanes(weight, start, width), 0.0)
            spread_ref[part * grid : (part + 1) * grid, where] = value.astype(BF16)
    span = blocks * size
    source = dot(row_ref[:, :span], spread_ref[:, :span], 1, 1)
    return real + EMIT_RATE * source[:, :grid], imag + EMIT_RATE * source[:, grid:]


def position():
    return lax.axis_index("cuts") * lax.axis_size("group") + lax.axis_index("group")


def kept_unless(index):
    return jnp.where(position() == index, 0.0, 1.0).astype(F32)


def kick_kernel(field_hbm, phases_hbm, energy_hbm, pixels_hbm, dest_hbm, out, field, phases, energy, pixels, dest, read_ref, sems):
    blocks = phases.shape[0]
    pairs = ((dest_hbm, dest), (field_hbm, field), (pixels_hbm, pixels), (phases_hbm, phases), (energy_hbm, energy))
    copies = [pltpu.make_async_copy(source, target, sems.at[k]) for k, (source, target) in enumerate(pairs)]
    for copy in copies:
        copy.start()
    for copy in copies:
        copy.wait()
    new_phases, new_energy = kick(field[0], field[1], phases[...], energy[...], pixels[...], read_ref)
    goals = [dest[0, block] for block in range(blocks)]
    ranks = [0] * blocks
    for later in range(blocks):
        for earlier in range(later):
            first = (goals[earlier] <= goals[later]).astype(jnp.int32)
            ranks[later] = ranks[later] + first
            ranks[earlier] = ranks[earlier] + (1 - first)
    whole = pixels[...].astype(F32)
    for block in range(blocks):
        for kind, value in enumerate((new_phases, new_energy, whole)):
            out[pl.ds(kind * blocks + ranks[block], 1), :] = value[block : block + 1, :]
        goal = jnp.full((1, out.shape[1]), goals[block].astype(F32), F32)
        out[pl.ds(3 * blocks + ranks[block], 1), :] = goal


def radiate_kernel(count, field, state, propagator, out, row_ref, spread_ref):
    blocks = state.shape[0] // 4
    pixels = state[2 * blocks : 3 * blocks, :].astype(jnp.int32)
    real, imag = emit(field[0], field[1], state[0:blocks, :], pixels, row_ref, spread_ref)
    real, imag = diffract(real, imag, propagator)
    keep = kept_unless(count - 1)
    out[0] = real * keep
    out[1] = imag * keep


def second_kernel(count, rows, cap, field, state, propagator, out, *rest):
    sends = rest[:-3]
    read_ref, row_ref, spread_ref = rest[-3:]
    blocks = state.shape[0] // 4
    real, imag = field[0], field[1]
    grid = real.shape[0]
    pixels = state[2 * blocks : 3 * blocks, :].astype(jnp.int32)
    phases, energy = kick(real, imag, state[0:blocks, :], state[blocks : 2 * blocks, :], pixels, read_ref)
    cuts = len(sends)
    source = lax.rem(position() + 1, count)
    cut = lax.div(source, count // cuts)
    kinds = (phases, energy, state[2 * blocks : 3 * blocks, :])
    for ahead, send in enumerate(sends):
        wanted = lax.rem(cut + ahead, cuts).astype(F32)
        chunk = [jnp.zeros((cap, phases.shape[1]), F32)] * 2 + [jnp.full((cap, phases.shape[1]), -1.0, F32)]
        for start in range(0, blocks, cap):
            goes = state[3 * blocks + start : 3 * blocks + start + cap, :] == wanted
            chunk = [jnp.where(goes, kind[start : start + cap], old) for kind, old in zip(kinds, chunk)]
        for kind in range(3):
            send[kind * cap : (kind + 1) * cap, :] = chunk[kind]
    real, imag = emit(real, imag, phases, pixels, row_ref, spread_ref)
    real, imag = diffract(real, imag, propagator)
    keep = kept_unless(count - 2)
    real, imag = real * keep, imag * keep
    if rows:
        for part in range(grid // rows):
            out[part, 0:rows, :] = real[part * rows : (part + 1) * rows]
            out[part, rows : 2 * rows, :] = imag[part * rows : (part + 1) * rows]
    else:
        out[0] = real
        out[1] = imag


def matrix_kernel(transmit, cos_out, sin_out, cos_in, sin_in, out):
    count = cos_in.shape[0]
    gain_real, gain_imag = transmit[0:1, :], transmit[1:2, :]
    for which in range(2):
        cosine, sine = cos_out[which], sin_out[which]
        real = cosine * gain_real - sine * gain_imag
        imag = cosine * gain_imag + sine * gain_real
        full_real = exact_dot(real, cos_in[...]) + exact_dot(imag, sin_in[...])
        full_imag = exact_dot(imag, cos_in[...]) - exact_dot(real, sin_in[...])
        base = 2 * which * count
        form = jnp.concatenate(
            [
                jnp.concatenate([full_real, -full_imag], axis=1),
                jnp.concatenate([full_imag, full_real], axis=1),
            ],
            axis=0,
        )
        high, low = split(form)
        out[base : base + 2 * count, :] = jnp.concatenate([high, high, low], axis=1)


def filter_kernel(rows, matrix, data, out):
    count = data.shape[0] // (2 * rows)
    size = data.shape[1]
    stacked = jnp.concatenate(
        [
            jnp.concatenate(
                [data[pl.ds(part * rows + j, count, stride=2 * rows), :] for part in range(2)], axis=0
            )
            for j in range(rows)
        ],
        axis=1,
    )
    high, low = split(stacked)
    result = dot(matrix[...], jnp.concatenate([high, low, high], axis=0), 1, 0)
    for kind in range(4):
        for j in range(rows):
            out[pl.ds(kind * rows + j, count, stride=4 * rows), :] = result[
                kind * count : (kind + 1) * count, j * size : (j + 1) * size
            ]


def joined(chunks_in):
    cap = chunks_in[0].shape[0] // 3
    kinds = [
        jnp.concatenate([chunk[kind * cap : (kind + 1) * cap, :] for chunk in chunks_in], axis=0)
        for kind in range(3)
    ]
    return kinds[0], kinds[1], kinds[2].astype(jnp.int32)


def last_kernel(rows, fields, propagator, *rest):
    out, field_ref, read_ref, row_ref, spread_ref = rest[-5:]
    half = (len(rest) - 5) // 2
    first_phases, first_energy, first_pixels = joined(rest[:half])
    phases, energy, next_pixels = joined(rest[half : 2 * half])
    grid = propagator.shape[1]
    if rows:
        for part in range(grid // rows):
            for kind in range(4):
                field_ref[kind, part * rows : (part + 1) * rows, :] = fields[
                    part, kind * rows : (kind + 1) * rows, :
                ]
    else:
        for kind in range(4):
            field_ref[kind] = fields[kind]
    real, imag = field_ref[0], field_ref[1]
    first_phases, _ = kick(real, imag, first_phases, first_energy, first_pixels, read_ref.at[0])
    real, imag = emit(real, imag, first_phases, first_pixels, row_ref, spread_ref)
    phases, energy = kick(field_ref[2], field_ref[3], phases, energy, next_pixels, read_ref.at[1])
    real, imag = diffract(real, imag, propagator)
    keep = kept_unless(1)
    real, imag = real * keep, imag * keep
    phases, _ = kick(real, imag, phases, energy, next_pixels, read_ref.at[0])
    real, imag = emit(real, imag, phases, next_pixels, row_ref, spread_ref)
    real, imag = diffract(real, imag, propagator)
    keep = kept_unless(0)
    out[0] = real * keep
    out[1] = imag * keep


def call(kernel, out_shape, scratch, flops, args, memory=pltpu.VMEM, limit=VMEM_LIMIT):
    specs = [pl.BlockSpec(memory_space=memory)] * len(args)
    return pl.pallas_call(
        kernel,
        out_shape=out_shape,
        in_specs=specs,
        out_specs=jax.tree.map(lambda _: pl.BlockSpec(memory_space=pltpu.VMEM), out_shape),
        scratch_shapes=scratch,
        compiler_params=pltpu.CompilerParams(vmem_limit_bytes=limit),
        cost_estimate=pl.CostEstimate(flops=flops, bytes_accessed=1 << 19, transcendentals=0),
    )(*args)


def time_tables(count):
    times = jnp.arange(count, dtype=jnp.int32)
    outs = [angle_table((times + (count - lag)) % count, times, count) for lag in (4, 3)]
    cos_out = jnp.stack([cosine for cosine, _ in outs]) / count
    sin_out = jnp.stack([sine for _, sine in outs]) / count
    return (cos_out, sin_out, *angle_table(times, times, count))


def angle_table(first_ids, second_ids, total_slices):
    product = first_ids[:, None] * second_ids[None, :] % total_slices
    angle = product.astype(F32) * (2.0 * math.pi / total_slices)
    return jnp.cos(angle), jnp.sin(angle)


def filter_any(field, transmit, count):
    grid = field.shape[1]
    span = grid * grid
    share = -(-span // count)
    flat = jnp.pad(field.reshape(2, span), ((0, 0), (0, share * count - span)))
    parts = flat.reshape(2, count, share).transpose(1, 0, 2)
    got = lax.all_to_all(parts, AXES, split_axis=0, concat_axis=0, tiled=True)
    got = jnp.roll(got, 2, axis=0)
    real, imag = got[:, 0], got[:, 1]
    times = jnp.arange(count, dtype=jnp.int32)
    cosine, sine = angle_table(times, times, count)
    spec_real = exact_dot(cosine, real) + exact_dot(sine, imag)
    spec_imag = exact_dot(cosine, imag) - exact_dot(sine, real)
    gain_real, gain_imag = transmit[0][:, None], transmit[1][:, None]
    shaped_real = gain_real * spec_real - gain_imag * spec_imag
    shaped_imag = gain_real * spec_imag + gain_imag * spec_real
    back_real = (exact_dot(cosine, shaped_real) - exact_dot(sine, shaped_imag)) / count
    back_imag = (exact_dot(cosine, shaped_imag) + exact_dot(sine, shaped_real)) / count
    back = jnp.stack([back_real, back_imag], axis=1)
    sent = jnp.stack([jnp.roll(back, 2, axis=0), jnp.roll(back, 1, axis=0)], axis=1)
    fields = lax.all_to_all(sent, AXES, split_axis=0, concat_axis=0, tiled=True)
    fields = fields.transpose(1, 2, 0, 3).reshape(4, share * count)[:, :span]
    return fields.reshape(4, grid, grid)


def on_device(radiation, phases, energy, pixels, destination, propagator, transmit):
    cuts, groups = lax.axis_size("cuts"), lax.axis_size("group")
    count = cuts * groups
    grid = radiation.shape[-1]
    blocks, size = phases.shape[1:]
    cap = max(2, 2 * blocks // cuts)
    rows = grid // count if grid % count == 0 and (2 * grid // count) % 8 == 0 else 0
    field = radiation[0]
    shape = lambda *dims: jax.ShapeDtypeStruct(dims, F32)
    read = lambda number: pltpu.VMEM((2, number, size), F32)
    hot = lambda number: [pltpu.VMEM((grid, number * size), BF16), pltpu.VMEM((2 * grid, number * size), BF16)]
    pass_flops = 4 * blocks * size * grid * grid
    prop_flops = 48 * grid**3

    state = call(
        kick_kernel, shape(4 * blocks, size),
        [
            pltpu.VMEM((2, grid, grid), F32),
            pltpu.VMEM((blocks, size), F32),
            pltpu.VMEM((blocks, size), F32),
            pltpu.VMEM((blocks, size), jnp.int32),
            pltpu.SMEM((1, blocks), jnp.int32),
            read(blocks),
            pltpu.SemaphoreType.DMA((5,)),
        ],
        pass_flops, (field, phases[0], energy[0], pixels[0], destination), pl.ANY, WHOLE_VMEM,
    )
    route = [((i + 1) % count, i) for i in range(count)]
    behind = lax.ppermute(state, AXES, route)
    field = call(
        functools.partial(radiate_kernel, count), shape(2, grid, grid), hot(blocks), pass_flops + prop_flops,
        (field, state, propagator),
    )
    part_shape = shape(count, 2 * rows, grid) if rows else shape(2, grid, grid)
    field, *sends = call(
        functools.partial(second_kernel, count, rows, cap), (part_shape, *[shape(3 * cap, size)] * cuts),
        [read(blocks)] + hot(blocks), 2 * pass_flops + prop_flops,
        (field, behind, propagator),
    )
    chunks_in = [
        lax.ppermute(send, AXES, [(i, (i + lag + groups * ahead) % count) for i in range(count)])
        for lag in (3, 2)
        for ahead, send in enumerate(sends)
    ]
    if rows:
        matrix = call(
            matrix_kernel, jax.ShapeDtypeStruct((4 * count, 6 * count), BF16), [], 1 << 20,
            (transmit, *time_tables(count)),
        )
        data = lax.all_to_all(field, AXES, split_axis=0, concat_axis=0, tiled=True)
        sent = call(
            functools.partial(filter_kernel, rows), shape(count * 4 * rows, grid), [], 1 << 24,
            (matrix, data.reshape(count * 2 * rows, grid)),
        )
        fields = lax.all_to_all(
            sent.reshape(count, 4 * rows, grid), AXES, split_axis=0, concat_axis=0, tiled=True
        )
    else:
        fields = filter_any(field, transmit, count)
    capacity = cuts * cap
    out = call(
        functools.partial(last_kernel, rows), shape(2, grid, grid),
        [pltpu.VMEM((4, grid, grid), F32), pltpu.VMEM((2, 2, capacity, size), F32)] + hot(capacity),
        10 * pass_flops + 2 * prop_flops, (fields, propagator, *chunks_in),
    )
    return out[None]


def solution(mesh):
    return jax.shard_map(
        on_device,
        mesh=mesh,
        in_specs=(
            P(("cuts", "group"), None, None, None),
            P(("cuts", "group"), None, None),
            P(("cuts", "group"), None, None),
            P(("cuts", "group"), None, None),
            P(("cuts", "group"), None),
            P(),
            P(),
        ),
        out_specs=P(("cuts", "group"), None, None, None),
        check_vma=False,
    )
```

```python
import functools
import math

import jax
import jax.numpy as jnp
from jax import lax
from jax.experimental import pallas as pl
from jax.experimental.pallas import tpu as pltpu
from jax.sharding import PartitionSpec as P

KICK_RATE = 0.5
PHASE_RATE = 1.0
EMIT_RATE = 0.5

AXES = ("cuts", "group")
F32 = jnp.float32
BF16 = jnp.bfloat16
KINDS = 4
VMEM_LIMIT = 48 * 1024 * 1024
WHOLE_VMEM = 60 * 1024 * 1024


def dot(left, right, left_dim, right_dim):
    dims = (((left_dim,), (right_dim,)), ((), ()))
    return lax.dot_general(left, right, dims, preferred_element_type=F32)


def exact_dot(left, right):
    return jnp.dot(left, right, precision=lax.Precision.HIGHEST, preferred_element_type=F32)


def split(value):
    high = value.astype(BF16)
    return high, (value - high.astype(F32)).astype(BF16)


def diffract(real, imag, propagator):
    size = real.shape[0]
    prop_real, prop_imag = propagator[0], propagator[1]
    form = jnp.concatenate(
        [
            jnp.concatenate([prop_real, -prop_imag], axis=1),
            jnp.concatenate([prop_imag, prop_real], axis=1),
        ],
        axis=0,
    )
    form_high, form_low = split(form)
    high, low = split(jnp.concatenate([real, imag], axis=1))
    both = dot(jnp.concatenate([high, low], axis=0), form_high, 1, 1)
    right = both[:size] + both[size:] + dot(high, form_low, 1, 1)
    high, low = split(jnp.concatenate([right[:, :size], right[:, size:]], axis=0))
    both = dot(form_high, jnp.concatenate([high, low], axis=1), 1, 0)
    out = both[:, :size] + both[:, size:] + dot(form_low, high, 1, 0)
    return out[:size], out[size:]


def cells(pixels, grid):
    shift = grid.bit_length() - 1
    if grid == 1 << shift:
        return lax.shift_right_arithmetic(pixels, shift), pixels & (grid - 1)
    return pixels // grid, pixels % grid


def chunks(blocks):
    width = 2 if blocks % 2 == 0 else 1
    return [(start, width) for start in range(0, blocks, width)]


def lanes(array, start, width):
    return jnp.concatenate([array[start + k : start + k + 1] for k in range(width)], axis=1)


def hits(ids, grid):
    return lax.broadcasted_iota(jnp.int32, (grid, ids.shape[1]), 0) == ids


def kick(real, imag, phases, energy, pixels, read_ref):
    grid = real.shape[0]
    blocks, size = phases.shape
    low = jnp.concatenate([real, imag], axis=1).astype(BF16)
    row, col = cells(pixels, grid)
    for start, width in chunks(blocks):
        row_hot = jnp.where(hits(lanes(row, start, width), grid), 1.0, 0.0).astype(BF16)
        picked = dot(low, row_hot, 0, 0)
        col_hit = hits(lanes(col, start, width), grid)
        for part in range(2):
            value = picked[part * grid : (part + 1) * grid]
            value = jnp.sum(jnp.where(col_hit, value, 0.0), axis=0, keepdims=True)
            for k in range(width):
                read_ref[part, start + k : start + k + 1, :] = value[:, k * size : (k + 1) * size]
    read_real = read_ref[0, :blocks, :]
    read_imag = read_ref[1, :blocks, :]
    energy = energy - KICK_RATE * (read_real * jnp.cos(phases) - read_imag * jnp.sin(phases))
    return phases + PHASE_RATE * energy, energy


def emit(real, imag, phases, pixels, row_ref, spread_ref):
    grid = real.shape[0]
    blocks, size = phases.shape
    row, col = cells(pixels, grid)
    weight_real = jnp.cos(phases)
    weight_imag = -jnp.sin(phases)
    for start, width in chunks(blocks):
        where = pl.ds(start * size, width * size)
        row_ref[:, where] = jnp.where(hits(lanes(row, start, width), grid), 1.0, 0.0).astype(BF16)
        col_hit = hits(lanes(col, start, width), grid)
        for part, weight in ((0, weight_real), (1, weight_imag)):
            value = jnp.where(col_hit, lanes(weight, start, width), 0.0)
            spread_ref[part * grid : (part + 1) * grid, where] = value.astype(BF16)
    span = blocks * size
    source = dot(row_ref[:, :span], spread_ref[:, :span], 1, 1)
    return real + EMIT_RATE * source[:, :grid], imag + EMIT_RATE * source[:, grid:]


def position():
    return lax.axis_index("cuts") * lax.axis_size("group") + lax.axis_index("group")


def kept_unless(index):
    return jnp.where(position() == index, 0.0, 1.0).astype(F32)


def kick_kernel(field_hbm, phases_hbm, energy_hbm, pixels_hbm, dest_hbm, out, field, phases, energy, pixels, dest, read_ref, sems):
    blocks, size = phases.shape
    pairs = ((field_hbm, field), (pixels_hbm, pixels), (phases_hbm, phases), (energy_hbm, energy), (dest_hbm, dest))
    copies = [pltpu.make_async_copy(source, target, sems.at[k]) for k, (source, target) in enumerate(pairs)]
    for copy in copies:
        copy.start()
    for copy in copies:
        copy.wait()
    new_phases, new_energy = kick(field[0], field[1], phases[...], energy[...], pixels[...], read_ref)
    out[0:blocks, :] = new_phases
    out[blocks : 2 * blocks, :] = new_energy
    out[2 * blocks : 3 * blocks, :] = pixels[...].astype(F32)
    square = (blocks, blocks)
    own = lax.broadcasted_iota(jnp.int32, square, 0) == lax.broadcasted_iota(jnp.int32, square, 1)
    goals = jnp.where(own, jnp.broadcast_to(dest[0:1, :].astype(F32), square), 0.0)
    out[3 * blocks : 4 * blocks, :] = jnp.broadcast_to(jnp.sum(goals, axis=1, keepdims=True), (blocks, size))


def by_destination(kinds):
    goals = kinds[-1]
    blocks = goals.shape[0]
    place = lax.broadcasted_iota(jnp.int32, goals.shape, 0)
    rank = jnp.zeros(goals.shape, jnp.int32)
    for block in range(blocks):
        goal = goals[block : block + 1]
        ahead = (goal < goals) | ((goal == goals) & (place > block))
        rank = rank + jnp.where(ahead, 1, 0)
    ordered = [jnp.zeros(kind.shape, F32) for kind in kinds]
    for block in range(blocks):
        here = rank[block : block + 1] == place
        ordered = [jnp.where(here, kind[block : block + 1], old) for kind, old in zip(kinds, ordered)]
    return ordered


def lane_groups(values, shifts):
    size = values[0].shape[1]
    group = lax.broadcasted_iota(jnp.int32, values[0].shape, 1) // (size // len(values))
    joined_up = None
    for k, (value, shift) in enumerate(zip(values, shifts)):
        if shift % size:
            value = pltpu.roll(value, shift % size, axis=1)
        joined_up = value if joined_up is None else jnp.where(group == k, value, joined_up)
    return joined_up


def radiate_kernel(count, field, state, propagator, out, row_ref, spread_ref):
    blocks = state.shape[0] // 4
    pixels = state[2 * blocks : 3 * blocks, :].astype(jnp.int32)
    real, imag = emit(field[0], field[1], state[0:blocks, :], pixels, row_ref, spread_ref)
    real, imag = diffract(real, imag, propagator)
    keep = kept_unless(count - 1)
    out[0] = real * keep
    out[1] = imag * keep


def second_kernel(count, rows, cap, height, field, state, propagator, out, *rest):
    sends = rest[:-3]
    read_ref, row_ref, spread_ref = rest[-3:]
    blocks, size = state.shape[0] // 4, state.shape[1]
    real, imag = field[0], field[1]
    grid = real.shape[0]
    pixels = state[2 * blocks : 3 * blocks, :].astype(jnp.int32)
    phases, energy = kick(real, imag, state[0:blocks, :], state[blocks : 2 * blocks, :], pixels, read_ref)
    kinds = by_destination((phases, energy, state[2 * blocks : 3 * blocks, :], state[3 * blocks : 4 * blocks, :]))
    if height:
        pieces = len(kinds)
        width = size // pieces
        for chunk in range(blocks // cap):
            parts = [kind[chunk * cap : (chunk + 1) * cap] for kind in kinds]
            for piece in range(pieces):
                row = lane_groups(parts, [(k - piece) * width for k in range(pieces)])
                out[pl.ds(piece * cap * height + 2 * rows + chunk, cap, stride=height), :] = row
    else:
        cuts = len(sends)
        cut = lax.div(lax.rem(position() + 1, count), count // cuts)
        for ahead, send in enumerate(sends):
            wanted = lax.rem(cut + ahead, cuts).astype(F32)
            chunk = [jnp.zeros((cap, size), F32)] * 2 + [jnp.full((cap, size), -1.0, F32)]
            for start in range(0, blocks, cap):
                goes = kinds[3][start : start + cap] == wanted
                chunk = [jnp.where(goes, kind[start : start + cap], old) for kind, old in zip(kinds, chunk)]
            for kind in range(3):
                send[kind * cap : (kind + 1) * cap, :] = chunk[kind]
    real, imag = emit(real, imag, phases, pixels, row_ref, spread_ref)
    real, imag = diffract(real, imag, propagator)
    keep = kept_unless(count - 2)
    real, imag = real * keep, imag * keep
    if height:
        for part in range(grid // rows):
            base = part * height
            out[base : base + rows, :] = real[part * rows : (part + 1) * rows]
            out[base + rows : base + 2 * rows, :] = imag[part * rows : (part + 1) * rows]
    else:
        out[0] = real
        out[1] = imag


def matrix_kernel(transmit, cos_out, sin_out, cos_in, sin_in, out):
    count = cos_in.shape[0]
    gain_real, gain_imag = transmit[0:1, :], transmit[1:2, :]
    for which in range(2):
        cosine, sine = cos_out[which], sin_out[which]
        real = cosine * gain_real - sine * gain_imag
        imag = cosine * gain_imag + sine * gain_real
        full_real = exact_dot(real, cos_in[...]) + exact_dot(imag, sin_in[...])
        full_imag = exact_dot(imag, cos_in[...]) - exact_dot(real, sin_in[...])
        base = 2 * which * count
        form = jnp.concatenate(
            [
                jnp.concatenate([full_real, -full_imag], axis=1),
                jnp.concatenate([full_imag, full_real], axis=1),
            ],
            axis=0,
        )
        high, low = split(form)
        out[base : base + 2 * count, :] = jnp.concatenate([high, high, low], axis=1)


def filter_kernel(rows, cuts, chunk_count, matrix, data, out):
    count = matrix.shape[1] // 6
    height = data.shape[0] // count
    tall = out.shape[0] // count
    groups = count // cuts
    size = data.shape[1]
    stacked = jnp.concatenate(
        [
            jnp.concatenate(
                [data[pl.ds(part * rows + j, count, stride=height), :] for part in range(2)], axis=0
            )
            for j in range(rows)
        ],
        axis=1,
    )
    high, low = split(stacked)
    result = dot(matrix[...], jnp.concatenate([high, low, high], axis=0), 1, 0)
    for kind in range(4):
        for j in range(rows):
            out[pl.ds(kind * rows + j, count, stride=tall), :] = result[
                kind * count : (kind + 1) * count, j * size : (j + 1) * size
            ]
    bundles = [
        pltpu.roll(data[pl.ds(2 * rows + chunk, count, stride=height), :], 1, axis=0)
        for chunk in range(chunk_count)
    ]
    goals = [bundle[:, size - 1 : size] for bundle in bundles]
    for cut in range(cuts):
        chosen = bundles[0]
        for bundle, goal in zip(bundles[1:], goals[1:]):
            chosen = jnp.where(goal == float(cut), bundle, chosen)
        for which in range(2):
            first = cut * groups + 2 - which
            fits = min(groups, count - first)
            for source in range(cuts):
                tile = chosen[source * groups : (source + 1) * groups]
                base = 4 * rows + which * cuts + source
                out[pl.ds(first * tall + base, fits, stride=tall), :] = tile[:fits]
                for k in range(fits, groups):
                    row = (first + k - count) * tall + base
                    out[row : row + 1, :] = tile[k : k + 1]


def joined(chunks_in):
    cap = chunks_in[0].shape[0] // 3
    kinds = [
        jnp.concatenate([chunk[kind * cap : (kind + 1) * cap, :] for chunk in chunks_in], axis=0)
        for kind in range(3)
    ]
    return kinds[0], kinds[1], kinds[2].astype(jnp.int32)


def relayed(fields, rows, cuts, which, count):
    tall = fields.shape[0] // count
    size = fields.shape[1]
    width = size // KINDS
    bundles = [
        fields[pl.ds(4 * rows + which * cuts + cut, count, stride=tall), :] for cut in range(cuts)
    ]
    kinds = [lane_groups(bundles, [(cut - kind) * width for cut in range(cuts)]) for kind in range(KINDS)]
    home = lax.rem(position() + (count - 2 + which), count)
    wanted = lax.div(home, count // cuts).astype(F32)
    return kinds[0], kinds[1], jnp.where(kinds[3] == wanted, kinds[2], -1.0).astype(jnp.int32)


def last_kernel(rows, cuts, count, fields, propagator, *rest):
    out, field_ref, read_ref, row_ref, spread_ref = rest[-5:]
    chunks_in = rest[:-5]
    grid = propagator.shape[1]
    if chunks_in:
        half = len(chunks_in) // 2
        first_phases, first_energy, first_pixels = joined(chunks_in[:half])
        phases, energy, next_pixels = joined(chunks_in[half:])
        for kind in range(4):
            field_ref[kind] = fields[kind]
    else:
        first_phases, first_energy, first_pixels = relayed(fields, rows, cuts, 0, count)
        phases, energy, next_pixels = relayed(fields, rows, cuts, 1, count)
        tall = fields.shape[0] // count
        for part in range(grid // rows):
            for kind in range(4):
                base = part * tall + kind * rows
                field_ref[kind, part * rows : (part + 1) * rows, :] = fields[base : base + rows, :]
    real, imag = field_ref[0], field_ref[1]
    first_phases, _ = kick(real, imag, first_phases, first_energy, first_pixels, read_ref.at[0])
    real, imag = emit(real, imag, first_phases, first_pixels, row_ref, spread_ref)
    phases, energy = kick(field_ref[2], field_ref[3], phases, energy, next_pixels, read_ref.at[1])
    real, imag = diffract(real, imag, propagator)
    keep = kept_unless(1)
    real, imag = real * keep, imag * keep
    phases, _ = kick(real, imag, phases, energy, next_pixels, read_ref.at[0])
    real, imag = emit(real, imag, phases, next_pixels, row_ref, spread_ref)
    real, imag = diffract(real, imag, propagator)
    keep = kept_unless(0)
    out[0] = real * keep
    out[1] = imag * keep


def call(kernel, out_shape, scratch, flops, args, memory=pltpu.VMEM, limit=VMEM_LIMIT):
    specs = [pl.BlockSpec(memory_space=memory)] * len(args)
    return pl.pallas_call(
        kernel,
        out_shape=out_shape,
        in_specs=specs,
        out_specs=jax.tree.map(lambda _: pl.BlockSpec(memory_space=pltpu.VMEM), out_shape),
        scratch_shapes=scratch,
        compiler_params=pltpu.CompilerParams(vmem_limit_bytes=limit),
        cost_estimate=pl.CostEstimate(flops=flops, bytes_accessed=1 << 19, transcendentals=0),
    )(*args)


def time_tables(count):
    times = jnp.arange(count, dtype=jnp.int32)
    outs = [angle_table((times + (count - lag)) % count, times, count) for lag in (4, 3)]
    cos_out = jnp.stack([cosine for cosine, _ in outs]) / count
    sin_out = jnp.stack([sine for _, sine in outs]) / count
    return (cos_out, sin_out, *angle_table(times, times, count))


def angle_table(first_ids, second_ids, total_slices):
    product = first_ids[:, None] * second_ids[None, :] % total_slices
    angle = product.astype(F32) * (2.0 * math.pi / total_slices)
    return jnp.cos(angle), jnp.sin(angle)


def filter_any(field, transmit, count):
    grid = field.shape[1]
    span = grid * grid
    share = -(-span // count)
    flat = jnp.pad(field.reshape(2, span), ((0, 0), (0, share * count - span)))
    parts = flat.reshape(2, count, share).transpose(1, 0, 2)
    got = lax.all_to_all(parts, AXES, split_axis=0, concat_axis=0, tiled=True)
    got = jnp.roll(got, 2, axis=0)
    real, imag = got[:, 0], got[:, 1]
    times = jnp.arange(count, dtype=jnp.int32)
    cosine, sine = angle_table(times, times, count)
    spec_real = exact_dot(cosine, real) + exact_dot(sine, imag)
    spec_imag = exact_dot(cosine, imag) - exact_dot(sine, real)
    gain_real, gain_imag = transmit[0][:, None], transmit[1][:, None]
    shaped_real = gain_real * spec_real - gain_imag * spec_imag
    shaped_imag = gain_real * spec_imag + gain_imag * spec_real
    back_real = (exact_dot(cosine, shaped_real) - exact_dot(sine, shaped_imag)) / count
    back_imag = (exact_dot(cosine, shaped_imag) + exact_dot(sine, shaped_real)) / count
    back = jnp.stack([back_real, back_imag], axis=1)
    sent = jnp.stack([jnp.roll(back, 2, axis=0), jnp.roll(back, 1, axis=0)], axis=1)
    fields = lax.all_to_all(sent, AXES, split_axis=0, concat_axis=0, tiled=True)
    fields = fields.transpose(1, 2, 0, 3).reshape(4, share * count)[:, :span]
    return fields.reshape(4, grid, grid)


def on_device(radiation, phases, energy, pixels, destination, propagator, transmit):
    cuts, groups = lax.axis_size("cuts"), lax.axis_size("group")
    count = cuts * groups
    grid = radiation.shape[-1]
    blocks, size = phases.shape[1:]
    cap = max(2, 2 * blocks // cuts)
    rows = grid // count if grid % count == 0 and (2 * grid // count) % 8 == 0 else 0
    if cap * KINDS != count or cuts != KINDS or size % 128 or blocks != 2 * cap or groups % 8:
        rows = 0
    height = 2 * rows + 8 if rows else 0
    tall = 4 * rows + 8
    field = radiation[0]
    shape = lambda *dims: jax.ShapeDtypeStruct(dims, F32)
    read = lambda number: pltpu.VMEM((2, number, size), F32)
    hot = lambda number: [pltpu.VMEM((grid, number * size), BF16), pltpu.VMEM((2 * grid, number * size), BF16)]
    pass_flops = 4 * blocks * size * grid * grid
    prop_flops = 48 * grid**3

    state = call(
        kick_kernel, shape(4 * blocks, size),
        [
            pltpu.VMEM((2, grid, grid), F32),
            pltpu.VMEM((blocks, size), F32),
            pltpu.VMEM((blocks, size), F32),
            pltpu.VMEM((blocks, size), jnp.int32),
            pltpu.VMEM((1, blocks), jnp.int32),
            read(blocks),
            pltpu.SemaphoreType.DMA((5,)),
        ],
        pass_flops, (field, phases[0], energy[0], pixels[0], destination), pl.ANY, WHOLE_VMEM,
    )
    route = [((i + 1) % count, i) for i in range(count)]
    behind = lax.ppermute(state, AXES, route)
    field = call(
        functools.partial(radiate_kernel, count), shape(2, grid, grid), hot(blocks), pass_flops + prop_flops,
        (field, state, propagator),
    )
    part_shape = shape(count * height, grid) if rows else shape(2, grid, grid)
    send_shapes = [] if rows else [shape(3 * cap, size)] * cuts
    field, *sends = call(
        functools.partial(second_kernel, count, rows, cap, height), (part_shape, *send_shapes),
        [read(blocks)] + hot(blocks), 2 * pass_flops + prop_flops,
        (field, behind, propagator),
    )
    chunks_in = [
        lax.ppermute(send, AXES, [(i, (i + lag + groups * ahead) % count) for i in range(count)])
        for lag in (3, 2)
        for ahead, send in enumerate(sends)
    ]
    if rows:
        matrix = call(
            matrix_kernel, jax.ShapeDtypeStruct((4 * count, 6 * count), BF16), [], 1 << 20,
            (transmit, *time_tables(count)),
        )
        data = lax.all_to_all(
            field.reshape(count, height, grid), AXES, split_axis=0, concat_axis=0, tiled=True
        )
        sent = call(
            functools.partial(filter_kernel, rows, cuts, blocks // cap), shape(count * tall, grid), [], 1 << 24,
            (matrix, data.reshape(count * height, grid)),
        )
        fields = lax.all_to_all(
            sent.reshape(count, tall, grid), AXES, split_axis=0, concat_axis=0, tiled=True
        )
        fields = fields.reshape(count * tall, grid)
    else:
        fields = filter_any(field, transmit, count)
    capacity = cuts * cap
    out = call(
        functools.partial(last_kernel, rows, cuts, count), shape(2, grid, grid),
        [pltpu.VMEM((4, grid, grid), F32), pltpu.VMEM((2, 2, capacity, size), F32)] + hot(capacity),
        10 * pass_flops + 2 * prop_flops, (fields, propagator, *chunks_in),
    )
    return out[None]


def solution(mesh):
    return jax.shard_map(
        on_device,
        mesh=mesh,
        in_specs=(
            P(("cuts", "group"), None, None, None),
            P(("cuts", "group"), None, None),
            P(("cuts", "group"), None, None),
            P(("cuts", "group"), None, None),
            P(("cuts", "group"), None),
            P(),
            P(),
        ),
        out_specs=P(("cuts", "group"), None, None, None),
        check_vma=False,
    )
```

```python
import functools
import math

import jax
import jax.numpy as jnp
from jax import lax
from jax.experimental import pallas as pl
from jax.experimental.pallas import tpu as pltpu
from jax.sharding import PartitionSpec as P

KICK_RATE = 0.5
PHASE_RATE = 1.0
EMIT_RATE = 0.5

AXES = ("cuts", "group")
F32 = jnp.float32
BF16 = jnp.bfloat16
KINDS = 4
VMEM_LIMIT = 48 * 1024 * 1024
WHOLE_VMEM = 60 * 1024 * 1024


def dot(left, right, left_dim, right_dim):
    dims = (((left_dim,), (right_dim,)), ((), ()))
    return lax.dot_general(left, right, dims, preferred_element_type=F32)


def exact_dot(left, right):
    return jnp.dot(left, right, precision=lax.Precision.HIGHEST, preferred_element_type=F32)


def split(value):
    high = value.astype(BF16)
    return high, (value - high.astype(F32)).astype(BF16)


def diffract(real, imag, propagator):
    size = real.shape[0]
    prop_real, prop_imag = propagator[0], propagator[1]
    form = jnp.concatenate(
        [
            jnp.concatenate([prop_real, -prop_imag], axis=1),
            jnp.concatenate([prop_imag, prop_real], axis=1),
        ],
        axis=0,
    )
    form_high, form_low = split(form)
    high, low = split(jnp.concatenate([real, imag], axis=1))
    both = dot(jnp.concatenate([high, low], axis=0), form_high, 1, 1)
    right = both[:size] + both[size:] + dot(high, form_low, 1, 1)
    high, low = split(jnp.concatenate([right[:, :size], right[:, size:]], axis=0))
    both = dot(form_high, jnp.concatenate([high, low], axis=1), 1, 0)
    out = both[:, :size] + both[:, size:] + dot(form_low, high, 1, 0)
    return out[:size], out[size:]


def cells(pixels, grid):
    shift = grid.bit_length() - 1
    if grid == 1 << shift:
        return lax.shift_right_arithmetic(pixels, shift), pixels & (grid - 1)
    return pixels // grid, pixels % grid


def chunks(blocks):
    width = 2 if blocks % 2 == 0 else 1
    return [(start, width) for start in range(0, blocks, width)]


def lanes(array, start, width):
    return jnp.concatenate([array[start + k : start + k + 1] for k in range(width)], axis=1)


def hits(ids, grid):
    return lax.broadcasted_iota(jnp.int32, (grid, ids.shape[1]), 0) == ids


def kick(real, imag, phases, energy, pixels, read_ref):
    grid = real.shape[0]
    blocks, size = phases.shape
    low = jnp.concatenate([real, imag], axis=1).astype(BF16)
    row, col = cells(pixels, grid)
    for start, width in chunks(blocks):
        row_hot = jnp.where(hits(lanes(row, start, width), grid), 1.0, 0.0).astype(BF16)
        picked = dot(low, row_hot, 0, 0)
        col_hit = hits(lanes(col, start, width), grid)
        for part in range(2):
            value = picked[part * grid : (part + 1) * grid]
            value = jnp.sum(jnp.where(col_hit, value, 0.0), axis=0, keepdims=True)
            for k in range(width):
                read_ref[part, start + k : start + k + 1, :] = value[:, k * size : (k + 1) * size]
    read_real = read_ref[0, :blocks, :]
    read_imag = read_ref[1, :blocks, :]
    energy = energy - KICK_RATE * (read_real * jnp.cos(phases) - read_imag * jnp.sin(phases))
    return phases + PHASE_RATE * energy, energy


def emit(real, imag, phases, pixels, row_ref, spread_ref):
    grid = real.shape[0]
    blocks, size = phases.shape
    row, col = cells(pixels, grid)
    weight_real = jnp.cos(phases)
    weight_imag = -jnp.sin(phases)
    for start, width in chunks(blocks):
        where = pl.ds(start * size, width * size)
        row_ref[:, where] = jnp.where(hits(lanes(row, start, width), grid), 1.0, 0.0).astype(BF16)
        col_hit = hits(lanes(col, start, width), grid)
        for part, weight in ((0, weight_real), (1, weight_imag)):
            value = jnp.where(col_hit, lanes(weight, start, width), 0.0)
            spread_ref[part * grid : (part + 1) * grid, where] = value.astype(BF16)
    span = blocks * size
    source = dot(row_ref[:, :span], spread_ref[:, :span], 1, 1)
    return real + EMIT_RATE * source[:, :grid], imag + EMIT_RATE * source[:, grid:]


def position():
    return lax.axis_index("cuts") * lax.axis_size("group") + lax.axis_index("group")


def kept_unless(index):
    return jnp.where(position() == index, 0.0, 1.0).astype(F32)


def kick_kernel(field_hbm, phases_hbm, energy_hbm, pixels_hbm, dest_hbm, out, field, phases, energy, pixels, dest, read_ref, sems):
    blocks, size = phases.shape
    pairs = ((field_hbm, field), (pixels_hbm, pixels), (phases_hbm, phases), (energy_hbm, energy), (dest_hbm, dest))
    copies = [pltpu.make_async_copy(source, target, sems.at[k]) for k, (source, target) in enumerate(pairs)]
    for copy in copies:
        copy.start()
    for copy in copies:
        copy.wait()
    new_phases, new_energy = kick(field[0], field[1], phases[...], energy[...], pixels[...], read_ref)
    out[0:blocks, :] = new_phases
    out[blocks : 2 * blocks, :] = new_energy
    out[2 * blocks : 3 * blocks, :] = pixels[...].astype(F32)
    square = (blocks, blocks)
    own = lax.broadcasted_iota(jnp.int32, square, 0) == lax.broadcasted_iota(jnp.int32, square, 1)
    goals = jnp.where(own, jnp.broadcast_to(dest[0:1, :].astype(F32), square), 0.0)
    out[3 * blocks : 4 * blocks, :] = jnp.broadcast_to(jnp.sum(goals, axis=1, keepdims=True), (blocks, size))


def by_destination(kinds):
    goals = kinds[-1]
    blocks = goals.shape[0]
    place = lax.broadcasted_iota(jnp.int32, goals.shape, 0)
    rank = jnp.zeros(goals.shape, jnp.int32)
    for block in range(blocks):
        goal = goals[block : block + 1]
        ahead = (goal < goals) | ((goal == goals) & (place > block))
        rank = rank + jnp.where(ahead, 1, 0)
    ordered = [jnp.zeros(kind.shape, F32) for kind in kinds]
    for block in range(blocks):
        here = rank[block : block + 1] == place
        ordered = [jnp.where(here, kind[block : block + 1], old) for kind, old in zip(kinds, ordered)]
    return ordered


def lane_groups(values, shifts):
    size = values[0].shape[1]
    group = lax.broadcasted_iota(jnp.int32, values[0].shape, 1) // (size // len(values))
    joined_up = None
    for k, (value, shift) in enumerate(zip(values, shifts)):
        if shift % size:
            value = pltpu.roll(value, shift % size, axis=1)
        joined_up = value if joined_up is None else jnp.where(group == k, value, joined_up)
    return joined_up


def radiate_kernel(blocks, dropped, field, state, propagator, out, row_ref, spread_ref):
    pixels = state[2 * blocks : 3 * blocks, :].astype(jnp.int32)
    real, imag = emit(field[0], field[1], state[0:blocks, :], pixels, row_ref, spread_ref)
    real, imag = diffract(real, imag, propagator)
    keep = kept_unless(dropped)
    out[0] = real * keep
    out[1] = imag * keep


def second_kernel(count, rows, cap, field, state, propagator, out, *rest):
    sends = rest[:-3]
    read_ref, row_ref, spread_ref = rest[-3:]
    blocks, size = state.shape[0] // 4, state.shape[1]
    real, imag = field[0], field[1]
    grid = real.shape[0]
    pixels = state[2 * blocks : 3 * blocks, :].astype(jnp.int32)
    phases, energy = kick(real, imag, state[0:blocks, :], state[blocks : 2 * blocks, :], pixels, read_ref)
    kinds = by_destination((phases, energy, state[2 * blocks : 3 * blocks, :], state[3 * blocks : 4 * blocks, :]))
    if rows:
        pieces = len(kinds)
        width = size // pieces
        for chunk in range(blocks // cap):
            parts = [kind[chunk * cap : (chunk + 1) * cap] for kind in kinds]
            for piece in range(pieces):
                row = lane_groups(parts, [(k - piece) * width for k in range(pieces)])
                out[pl.ds(piece * cap * 3 + 2, cap, stride=3), chunk, :] = row
    else:
        cuts = len(sends)
        cut = lax.div(lax.rem(position() + 1, count), count // cuts)
        for ahead, send in enumerate(sends):
            wanted = lax.rem(cut + ahead, cuts).astype(F32)
            chunk = [jnp.zeros((cap, size), F32)] * 2 + [jnp.full((cap, size), -1.0, F32)]
            for start in range(0, blocks, cap):
                goes = kinds[3][start : start + cap] == wanted
                chunk = [jnp.where(goes, kind[start : start + cap], old) for kind, old in zip(kinds, chunk)]
            for kind in range(3):
                send[kind * cap : (kind + 1) * cap, :] = chunk[kind]
    real, imag = emit(real, imag, phases, pixels, row_ref, spread_ref)
    real, imag = diffract(real, imag, propagator)
    keep = kept_unless(count - 2)
    real, imag = real * keep, imag * keep
    if rows:
        for part in range(grid // rows):
            out[3 * part] = real[part * rows : (part + 1) * rows]
            out[3 * part + 1] = imag[part * rows : (part + 1) * rows]
    else:
        out[0] = real
        out[1] = imag


def matrix_kernel(transmit, cos_out, sin_out, cos_in, sin_in, out):
    gain_real, gain_imag = transmit[0:1, :], transmit[1:2, :]
    cosine, sine = cos_out[...], sin_out[...]
    real = cosine * gain_real - sine * gain_imag
    imag = cosine * gain_imag + sine * gain_real
    full_real = exact_dot(real, cos_in[...]) + exact_dot(imag, sin_in[...])
    full_imag = exact_dot(imag, cos_in[...]) - exact_dot(real, sin_in[...])
    form = jnp.concatenate(
        [
            jnp.concatenate([full_real, -full_imag], axis=1),
            jnp.concatenate([full_imag, full_real], axis=1),
        ],
        axis=0,
    )
    high, low = split(form)
    out[...] = jnp.concatenate([high, high, low], axis=1)


def filter_kernel(cuts, chunk_count, matrix, data, out):
    count = data.shape[0] // 3
    rows, size = data.shape[1:]
    groups = count // cuts
    stacked = jnp.concatenate(
        [
            jnp.concatenate([data[pl.ds(part, count, stride=3), j, :] for part in range(2)], axis=0)
            for j in range(rows)
        ],
        axis=1,
    )
    high, low = split(stacked)
    result = dot(matrix[...], jnp.concatenate([high, low, high], axis=0), 1, 0)
    for part in range(2):
        for j in range(rows):
            out[pl.ds(part, count, stride=3), j, :] = result[
                part * count : (part + 1) * count, j * size : (j + 1) * size
            ]
    bundles = [pltpu.roll(data[pl.ds(2, count, stride=3), chunk, :], 1, axis=0) for chunk in range(chunk_count)]
    goals = [bundle[:, size - 1 : size] for bundle in bundles]
    for cut in range(cuts):
        chosen = bundles[0]
        for bundle, goal in zip(bundles[1:], goals[1:]):
            chosen = jnp.where(goal == float(cut), bundle, chosen)
        first = cut * groups + 2
        fits = min(groups, count - first)
        for source in range(cuts):
            tile = chosen[source * groups : (source + 1) * groups]
            out[pl.ds(3 * first + 2, fits, stride=3), source, :] = tile[:fits]
            for k in range(fits, groups):
                out[3 * (first + k - count) + 2, source : source + 1, :] = tile[k : k + 1]


def joined(chunks_in):
    cap = chunks_in[0].shape[0] // 3
    kinds = [
        jnp.concatenate([chunk[kind * cap : (kind + 1) * cap, :] for chunk in chunks_in], axis=0)
        for kind in range(3)
    ]
    return kinds[0], kinds[1], kinds[2].astype(jnp.int32)


def relayed(fields, cuts):
    count = fields.shape[0] // 3
    size = fields.shape[2]
    width = size // KINDS
    bundles = [fields[pl.ds(2, count, stride=3), cut, :] for cut in range(cuts)]
    kinds = [lane_groups(bundles, [(cut - kind) * width for cut in range(cuts)]) for kind in range(KINDS)]
    wanted = lax.div(lax.rem(position() + (count - 2), count), count // cuts).astype(F32)
    return kinds[0], kinds[1], jnp.where(kinds[3] == wanted, kinds[2], -1.0).astype(jnp.int32)


def third_kernel(cuts, fields, *rest):
    out, state, read_ref = rest[-3:]
    chunks_in = rest[:-3]
    if chunks_in:
        phases, energy, pixels = joined(chunks_in)
        out[...] = fields[...]
    else:
        phases, energy, pixels = relayed(fields, cuts)
        rows = fields.shape[1]
        for part in range(fields.shape[0] // 3):
            for kind in range(2):
                out[kind, part * rows : (part + 1) * rows, :] = fields[3 * part + kind]
    phases, energy = kick(out[0], out[1], phases, energy, pixels, read_ref)
    blocks = phases.shape[0]
    state[0:blocks, :] = phases
    state[blocks : 2 * blocks, :] = energy
    state[2 * blocks : 3 * blocks, :] = pixels.astype(F32)


def fourth_kernel(field, state, propagator, out, read_ref, row_ref, spread_ref):
    blocks = state.shape[0] // 3
    pixels = state[2 * blocks : 3 * blocks, :].astype(jnp.int32)
    real, imag = field[0], field[1]
    phases, _ = kick(real, imag, state[0:blocks, :], state[blocks : 2 * blocks, :], pixels, read_ref)
    real, imag = emit(real, imag, phases, pixels, row_ref, spread_ref)
    real, imag = diffract(real, imag, propagator)
    keep = kept_unless(0)
    out[0] = real * keep
    out[1] = imag * keep


def call(kernel, out_shape, scratch, flops, args, memory=pltpu.VMEM, limit=VMEM_LIMIT):
    specs = [pl.BlockSpec(memory_space=memory)] * len(args)
    return pl.pallas_call(
        kernel,
        out_shape=out_shape,
        in_specs=specs,
        out_specs=jax.tree.map(lambda _: pl.BlockSpec(memory_space=pltpu.VMEM), out_shape),
        scratch_shapes=scratch,
        compiler_params=pltpu.CompilerParams(vmem_limit_bytes=limit),
        cost_estimate=pl.CostEstimate(flops=flops, bytes_accessed=1 << 19, transcendentals=0),
    )(*args)


def time_tables(count):
    times = jnp.arange(count, dtype=jnp.int32)
    cos_out, sin_out = angle_table((times + (count - 4)) % count, times, count)
    return (cos_out / count, sin_out / count, *angle_table(times, times, count))


def angle_table(first_ids, second_ids, total_slices):
    product = first_ids[:, None] * second_ids[None, :] % total_slices
    angle = product.astype(F32) * (2.0 * math.pi / total_slices)
    return jnp.cos(angle), jnp.sin(angle)


def filter_any(field, transmit, count):
    grid = field.shape[1]
    span = grid * grid
    share = -(-span // count)
    flat = jnp.pad(field.reshape(2, span), ((0, 0), (0, share * count - span)))
    parts = flat.reshape(2, count, share).transpose(1, 0, 2)
    got = lax.all_to_all(parts, AXES, split_axis=0, concat_axis=0, tiled=True)
    got = jnp.roll(got, 2, axis=0)
    real, imag = got[:, 0], got[:, 1]
    times = jnp.arange(count, dtype=jnp.int32)
    cosine, sine = angle_table(times, times, count)
    spec_real = exact_dot(cosine, real) + exact_dot(sine, imag)
    spec_imag = exact_dot(cosine, imag) - exact_dot(sine, real)
    gain_real, gain_imag = transmit[0][:, None], transmit[1][:, None]
    shaped_real = gain_real * spec_real - gain_imag * spec_imag
    shaped_imag = gain_real * spec_imag + gain_imag * spec_real
    back_real = (exact_dot(cosine, shaped_real) - exact_dot(sine, shaped_imag)) / count
    back_imag = (exact_dot(cosine, shaped_imag) + exact_dot(sine, shaped_real)) / count
    back = jnp.stack([back_real, back_imag], axis=1)
    sent = jnp.roll(back, 2, axis=0)
    fields = lax.all_to_all(sent, AXES, split_axis=0, concat_axis=0, tiled=True)
    fields = fields.transpose(1, 0, 2).reshape(2, share * count)[:, :span]
    return fields.reshape(2, grid, grid)


def on_device(radiation, phases, energy, pixels, destination, propagator, transmit):
    cuts, groups = lax.axis_size("cuts"), lax.axis_size("group")
    count = cuts * groups
    grid = radiation.shape[-1]
    blocks, size = phases.shape[1:]
    cap = max(2, 2 * blocks // cuts)
    rows = grid // count if grid % count == 0 else 0
    if rows != 4 or cap * KINDS != count or cuts != KINDS or size % 128 or blocks != 2 * cap or groups % 8:
        rows = 0
    field = radiation[0]
    shape = lambda *dims: jax.ShapeDtypeStruct(dims, F32)
    read = lambda number: pltpu.VMEM((2, number, size), F32)
    hot = lambda number: [pltpu.VMEM((grid, number * size), BF16), pltpu.VMEM((2 * grid, number * size), BF16)]
    pass_flops = 4 * blocks * size * grid * grid
    prop_flops = 48 * grid**3

    state = call(
        kick_kernel, shape(4 * blocks, size),
        [
            pltpu.VMEM((2, grid, grid), F32),
            pltpu.VMEM((blocks, size), F32),
            pltpu.VMEM((blocks, size), F32),
            pltpu.VMEM((blocks, size), jnp.int32),
            pltpu.VMEM((1, blocks), jnp.int32),
            read(blocks),
            pltpu.SemaphoreType.DMA((5,)),
        ],
        pass_flops, (field, phases[0], energy[0], pixels[0], destination), pl.ANY, WHOLE_VMEM,
    )
    route = [((i + 1) % count, i) for i in range(count)]
    behind = lax.ppermute(state, AXES, route)
    field = call(
        functools.partial(radiate_kernel, blocks, count - 1), shape(2, grid, grid), hot(blocks), pass_flops + prop_flops,
        (field, state, propagator),
    )
    part_shape = shape(count * 3, rows, grid) if rows else shape(2, grid, grid)
    send_shapes = [] if rows else [shape(3 * cap, size)] * cuts
    field, *sends = call(
        functools.partial(second_kernel, count, rows, cap), (part_shape, *send_shapes),
        [read(blocks)] + hot(blocks), 2 * pass_flops + prop_flops,
        (field, behind, propagator),
    )
    chunks_in = [
        lax.ppermute(send, AXES, [(i, (i + 3 + groups * ahead) % count) for i in range(count)])
        for ahead, send in enumerate(sends)
    ]
    if rows:
        matrix = call(
            matrix_kernel, jax.ShapeDtypeStruct((2 * count, 6 * count), BF16), [], 1 << 20,
            (transmit, *time_tables(count)),
        )
        data = lax.all_to_all(field, AXES, split_axis=0, concat_axis=0, tiled=True)
        sent = call(
            functools.partial(filter_kernel, cuts, blocks // cap), shape(count * 3, rows, grid), [], 1 << 24,
            (matrix, data),
        )
        fields = lax.all_to_all(sent, AXES, split_axis=0, concat_axis=0, tiled=True)
    else:
        fields = filter_any(field, transmit, count)
    capacity = cuts * cap
    share = capacity // blocks
    field, state = call(
        functools.partial(third_kernel, cuts), (shape(2, grid, grid), shape(3 * capacity, size)),
        [read(capacity)], share * pass_flops, (fields, *chunks_in),
    )
    behind = lax.ppermute(state, AXES, route)
    field = call(
        functools.partial(radiate_kernel, capacity, 1), shape(2, grid, grid), hot(capacity),
        share * pass_flops + prop_flops, (field, state, propagator),
    )
    out = call(
        fourth_kernel, shape(2, grid, grid), [read(capacity)] + hot(capacity),
        2 * share * pass_flops + prop_flops, (field, behind, propagator),
    )
    return out[None]


def solution(mesh):
    return jax.shard_map(
        on_device,
        mesh=mesh,
        in_specs=(
            P(("cuts", "group"), None, None, None),
            P(("cuts", "group"), None, None),
            P(("cuts", "group"), None, None),
            P(("cuts", "group"), None, None),
            P(("cuts", "group"), None),
            P(),
            P(),
        ),
        out_specs=P(("cuts", "group"), None, None, None),
        check_vma=False,
    )
```

```python
import functools
import math

import jax
import jax.numpy as jnp
from jax import lax
from jax.experimental import pallas as pl
from jax.experimental.pallas import tpu as pltpu
from jax.sharding import PartitionSpec as P

KICK_RATE = 0.5
PHASE_RATE = 1.0
EMIT_RATE = 0.5

AXES = ("cuts", "group")
F32 = jnp.float32
BF16 = jnp.bfloat16
KINDS = 4
VMEM_LIMIT = 48 * 1024 * 1024
WHOLE_VMEM = 60 * 1024 * 1024


def dot(left, right, left_dim, right_dim):
    dims = (((left_dim,), (right_dim,)), ((), ()))
    return lax.dot_general(left, right, dims, preferred_element_type=F32)


def exact_dot(left, right):
    return jnp.dot(left, right, precision=lax.Precision.HIGHEST, preferred_element_type=F32)


def split(value):
    high = value.astype(BF16)
    return high, (value - high.astype(F32)).astype(BF16)


def diffract(real, imag, propagator):
    size = real.shape[0]
    prop_real, prop_imag = propagator[0], propagator[1]
    form = jnp.concatenate(
        [
            jnp.concatenate([prop_real, -prop_imag], axis=1),
            jnp.concatenate([prop_imag, prop_real], axis=1),
        ],
        axis=0,
    )
    form_high, form_low = split(form)
    high, low = split(jnp.concatenate([real, imag], axis=1))
    both = dot(jnp.concatenate([high, low], axis=0), form_high, 1, 1)
    right = both[:size] + both[size:] + dot(high, form_low, 1, 1)
    high, low = split(jnp.concatenate([right[:, :size], right[:, size:]], axis=0))
    both = dot(form_high, jnp.concatenate([high, low], axis=1), 1, 0)
    out = both[:, :size] + both[:, size:] + dot(form_low, high, 1, 0)
    return out[:size], out[size:]


def cells(pixels, grid):
    half = grid // 2
    shift = grid.bit_length() - 1
    if grid == 1 << shift:
        row, col = lax.shift_right_arithmetic(pixels, shift), pixels & (grid - 1)
    else:
        row, col = pixels // grid, pixels % grid
    right = col >= half
    place = jnp.where(pixels < 0, -1, jnp.where(right, row + grid, row))
    return place, jnp.where(right, col - half, col)


def swapped(value):
    half = value.shape[1] // 2
    return jnp.concatenate([value[:, half:], value[:, :half]], axis=1)


def fold(first, second):
    left = lax.broadcasted_iota(jnp.int32, first.shape, 1) < first.shape[1] // 2
    return jnp.where(left, first, swapped(second)), jnp.where(left, swapped(first), second)


def chunks(blocks):
    width = 2 if blocks % 2 == 0 else 1
    return [(start, width) for start in range(0, blocks, width)]


def lanes(array, start, width):
    return jnp.concatenate([array[start + k : start + k + 1] for k in range(width)], axis=1)


def hits(ids, span):
    return lax.broadcasted_iota(jnp.int32, (span, ids.shape[1]), 0) == ids


def one_hot(place, start, width, span):
    ids = lanes(place, start, width).astype(F32)
    rows = lax.broadcasted_iota(jnp.int32, (span, ids.shape[1]), 0).astype(F32)
    if span <= 256:
        ids, rows = ids.astype(BF16), rows.astype(BF16)
    one, zero = jnp.ones((), BF16), jnp.zeros((), BF16)
    return jnp.where(rows == ids, one, zero)


def kick(real, imag, phases, energy, pixels, read_ref, hot_ref=None):
    grid = real.shape[0]
    half = grid // 2
    blocks, size = phases.shape
    upper, lower = fold(real, imag)
    low = jnp.concatenate([upper, lower], axis=0).astype(BF16)
    place, col = cells(pixels, grid)
    for start, width in chunks(blocks):
        hot = one_hot(place, start, width, 2 * grid)
        if hot_ref is not None:
            hot_ref[:, start * size : (start + width) * size] = hot
        picked = dot(low, hot, 0, 0)
        col_hit = hits(lanes(col, start, width), half)
        for part in range(2):
            value = picked[part * half : (part + 1) * half]
            value = jnp.sum(jnp.where(col_hit, value, 0.0), axis=0, keepdims=True)
            for k in range(width):
                read_ref[part, start + k : start + k + 1, :] = value[:, k * size : (k + 1) * size]
    read_real = read_ref[0, :blocks, :]
    read_imag = read_ref[1, :blocks, :]
    energy = energy - KICK_RATE * (read_real * jnp.cos(phases) - read_imag * jnp.sin(phases))
    return phases + PHASE_RATE * energy, energy


def emit(real, imag, phases, pixels, hot_ref, spread_ref, filled):
    grid = real.shape[0]
    half = grid // 2
    blocks, size = phases.shape
    place, col = cells(pixels, grid)
    weight_real = jnp.cos(phases)
    weight_imag = -jnp.sin(phases)
    for start, width in chunks(blocks):
        where = slice(start * size, (start + width) * size)
        if not filled:
            hot_ref[:, where] = one_hot(place, start, width, 2 * grid)
        col_hit = hits(lanes(col, start, width), half)
        for part, weight in ((0, weight_real), (1, weight_imag)):
            value = jnp.where(col_hit, lanes(weight, start, width), 0.0)
            spread_ref[part * half : (part + 1) * half, where] = value.astype(BF16)
    span = blocks * size
    source = dot(hot_ref[:, :span], spread_ref[:, :span], 1, 1)
    source_real, source_imag = fold(source[:grid], source[grid:])
    return real + EMIT_RATE * source_real, imag + EMIT_RATE * source_imag


def position():
    return lax.axis_index("cuts") * lax.axis_size("group") + lax.axis_index("group")


def kept_unless(index):
    return jnp.where(position() == index, 0.0, 1.0).astype(F32)


def kick_kernel(field_hbm, phases_hbm, energy_hbm, pixels_hbm, dest_hbm, out, field, phases, energy, pixels, dest, read_ref, sems):
    blocks, size = phases.shape
    pairs = ((field_hbm, field), (pixels_hbm, pixels), (phases_hbm, phases), (energy_hbm, energy), (dest_hbm, dest))
    copies = [pltpu.make_async_copy(source, target, sems.at[k]) for k, (source, target) in enumerate(pairs)]
    for copy in copies:
        copy.start()
    for copy in copies:
        copy.wait()
    new_phases, new_energy = kick(field[0], field[1], phases[...], energy[...], pixels[...], read_ref)
    out[0:blocks, :] = new_phases
    out[blocks : 2 * blocks, :] = new_energy
    out[2 * blocks : 3 * blocks, :] = pixels[...].astype(F32)
    square = (blocks, blocks)
    own = lax.broadcasted_iota(jnp.int32, square, 0) == lax.broadcasted_iota(jnp.int32, square, 1)
    goals = jnp.where(own, jnp.broadcast_to(dest[0:1, :].astype(F32), square), 0.0)
    out[3 * blocks : 4 * blocks, :] = jnp.broadcast_to(jnp.sum(goals, axis=1, keepdims=True), (blocks, size))


def by_destination(kinds):
    goals = kinds[-1]
    blocks = goals.shape[0]
    place = lax.broadcasted_iota(jnp.int32, goals.shape, 0)
    rank = jnp.zeros(goals.shape, jnp.int32)
    for block in range(blocks):
        goal = goals[block : block + 1]
        ahead = (goal < goals) | ((goal == goals) & (place > block))
        rank = rank + jnp.where(ahead, 1, 0)
    ordered = [jnp.zeros(kind.shape, F32) for kind in kinds]
    for block in range(blocks):
        here = rank[block : block + 1] == place
        ordered = [jnp.where(here, kind[block : block + 1], old) for kind, old in zip(kinds, ordered)]
    return ordered


def lane_groups(values, shifts):
    size = values[0].shape[1]
    group = lax.broadcasted_iota(jnp.int32, values[0].shape, 1) // (size // len(values))
    joined_up = None
    for k, (value, shift) in enumerate(zip(values, shifts)):
        if shift % size:
            value = pltpu.roll(value, shift % size, axis=1)
        joined_up = value if joined_up is None else jnp.where(group == k, value, joined_up)
    return joined_up


def radiate_kernel(blocks, dropped, field, state, propagator, out, hot_ref, spread_ref):
    pixels = state[2 * blocks : 3 * blocks, :].astype(jnp.int32)
    real, imag = emit(field[0], field[1], state[0:blocks, :], pixels, hot_ref, spread_ref, False)
    real, imag = diffract(real, imag, propagator)
    keep = kept_unless(dropped)
    out[0] = real * keep
    out[1] = imag * keep


def second_kernel(count, rows, cap, field, state, propagator, out, *rest):
    sends = rest[:-3]
    read_ref, hot_ref, spread_ref = rest[-3:]
    blocks, size = state.shape[0] // 4, state.shape[1]
    real, imag = field[0], field[1]
    grid = real.shape[0]
    pixels = state[2 * blocks : 3 * blocks, :].astype(jnp.int32)
    phases, energy = kick(real, imag, state[0:blocks, :], state[blocks : 2 * blocks, :], pixels, read_ref, hot_ref)
    kinds = by_destination((phases, energy, state[2 * blocks : 3 * blocks, :], state[3 * blocks : 4 * blocks, :]))
    if rows:
        pieces = len(kinds)
        width = size // pieces
        for chunk in range(blocks // cap):
            parts = [kind[chunk * cap : (chunk + 1) * cap] for kind in kinds]
            for piece in range(pieces):
                row = lane_groups(parts, [(k - piece) * width for k in range(pieces)])
                out[pl.ds(piece * cap * 3 + 2, cap, stride=3), chunk, :] = row
    else:
        cuts = len(sends)
        cut = lax.div(lax.rem(position() + 1, count), count // cuts)
        for ahead, send in enumerate(sends):
            wanted = lax.rem(cut + ahead, cuts).astype(F32)
            chunk = [jnp.zeros((cap, size), F32)] * 2 + [jnp.full((cap, size), -1.0, F32)]
            for start in range(0, blocks, cap):
                goes = kinds[3][start : start + cap] == wanted
                chunk = [jnp.where(goes, kind[start : start + cap], old) for kind, old in zip(kinds, chunk)]
            for kind in range(3):
                send[kind * cap : (kind + 1) * cap, :] = chunk[kind]
    real, imag = emit(real, imag, phases, pixels, hot_ref, spread_ref, True)
    real, imag = diffract(real, imag, propagator)
    keep = kept_unless(count - 2)
    real, imag = real * keep, imag * keep
    if rows:
        for part in range(grid // rows):
            out[3 * part] = real[part * rows : (part + 1) * rows]
            out[3 * part + 1] = imag[part * rows : (part + 1) * rows]
    else:
        out[0] = real
        out[1] = imag


def matrix_kernel(transmit, cos_out, sin_out, cos_in, sin_in, out):
    gain_real, gain_imag = transmit[0:1, :], transmit[1:2, :]
    cosine, sine = cos_out[...], sin_out[...]
    real = cosine * gain_real - sine * gain_imag
    imag = cosine * gain_imag + sine * gain_real
    full_real = exact_dot(real, cos_in[...]) + exact_dot(imag, sin_in[...])
    full_imag = exact_dot(imag, cos_in[...]) - exact_dot(real, sin_in[...])
    form = jnp.concatenate(
        [
            jnp.concatenate([full_real, -full_imag], axis=1),
            jnp.concatenate([full_imag, full_real], axis=1),
        ],
        axis=0,
    )
    high, low = split(form)
    out[...] = jnp.concatenate([high, high, low], axis=1)


def filter_kernel(cuts, chunk_count, matrix, data, out):
    count = data.shape[0] // 3
    rows, size = data.shape[1:]
    groups = count // cuts
    stacked = jnp.concatenate(
        [
            jnp.concatenate([data[pl.ds(part, count, stride=3), j, :] for part in range(2)], axis=0)
            for j in range(rows)
        ],
        axis=1,
    )
    high, low = split(stacked)
    result = dot(matrix[...], jnp.concatenate([high, low, high], axis=0), 1, 0)
    for part in range(2):
        for j in range(rows):
            out[pl.ds(part, count, stride=3), j, :] = result[
                part * count : (part + 1) * count, j * size : (j + 1) * size
            ]
    bundles = [pltpu.roll(data[pl.ds(2, count, stride=3), chunk, :], 1, axis=0) for chunk in range(chunk_count)]
    goals = [bundle[:, size - 1 : size] for bundle in bundles]
    for cut in range(cuts):
        chosen = bundles[0]
        for bundle, goal in zip(bundles[1:], goals[1:]):
            chosen = jnp.where(goal == float(cut), bundle, chosen)
        first = cut * groups + 2
        fits = min(groups, count - first)
        for source in range(cuts):
            tile = chosen[source * groups : (source + 1) * groups]
            out[pl.ds(3 * first + 2, fits, stride=3), source, :] = tile[:fits]
            for k in range(fits, groups):
                out[3 * (first + k - count) + 2, source : source + 1, :] = tile[k : k + 1]


def joined(chunks_in):
    cap = chunks_in[0].shape[0] // 3
    kinds = [
        jnp.concatenate([chunk[kind * cap : (kind + 1) * cap, :] for chunk in chunks_in], axis=0)
        for kind in range(3)
    ]
    return kinds[0], kinds[1], kinds[2].astype(jnp.int32)


def relayed(fields, cuts):
    count = fields.shape[0] // 3
    size = fields.shape[2]
    width = size // KINDS
    bundles = [fields[pl.ds(2, count, stride=3), cut, :] for cut in range(cuts)]
    kinds = [lane_groups(bundles, [(cut - kind) * width for cut in range(cuts)]) for kind in range(KINDS)]
    wanted = lax.div(lax.rem(position() + (count - 2), count), count // cuts).astype(F32)
    return kinds[0], kinds[1], jnp.where(kinds[3] == wanted, kinds[2], -1.0).astype(jnp.int32)


def third_kernel(cuts, fields, *rest):
    out, state, read_ref = rest[-3:]
    chunks_in = rest[:-3]
    if chunks_in:
        phases, energy, pixels = joined(chunks_in)
        out[...] = fields[...]
    else:
        phases, energy, pixels = relayed(fields, cuts)
        rows = fields.shape[1]
        for part in range(fields.shape[0] // 3):
            for kind in range(2):
                out[kind, part * rows : (part + 1) * rows, :] = fields[3 * part + kind]
    phases, energy = kick(out[0], out[1], phases, energy, pixels, read_ref)
    blocks = phases.shape[0]
    state[0:blocks, :] = phases
    state[blocks : 2 * blocks, :] = energy
    state[2 * blocks : 3 * blocks, :] = pixels.astype(F32)


def fourth_kernel(field, state, propagator, out, read_ref, hot_ref, spread_ref):
    blocks = state.shape[0] // 3
    pixels = state[2 * blocks : 3 * blocks, :].astype(jnp.int32)
    real, imag = field[0], field[1]
    phases, _ = kick(real, imag, state[0:blocks, :], state[blocks : 2 * blocks, :], pixels, read_ref, hot_ref)
    real, imag = emit(real, imag, phases, pixels, hot_ref, spread_ref, True)
    real, imag = diffract(real, imag, propagator)
    keep = kept_unless(0)
    out[0] = real * keep
    out[1] = imag * keep


def call(kernel, out_shape, scratch, flops, args, memory=pltpu.VMEM, limit=VMEM_LIMIT):
    specs = [pl.BlockSpec(memory_space=memory)] * len(args)
    return pl.pallas_call(
        kernel,
        out_shape=out_shape,
        in_specs=specs,
        out_specs=jax.tree.map(lambda _: pl.BlockSpec(memory_space=pltpu.VMEM), out_shape),
        scratch_shapes=scratch,
        compiler_params=pltpu.CompilerParams(vmem_limit_bytes=limit),
        cost_estimate=pl.CostEstimate(flops=flops, bytes_accessed=1 << 19, transcendentals=0),
    )(*args)


def time_tables(count):
    times = jnp.arange(count, dtype=jnp.int32)
    cos_out, sin_out = angle_table((times + (count - 4)) % count, times, count)
    return (cos_out / count, sin_out / count, *angle_table(times, times, count))


def angle_table(first_ids, second_ids, total_slices):
    product = first_ids[:, None] * second_ids[None, :] % total_slices
    angle = product.astype(F32) * (2.0 * math.pi / total_slices)
    return jnp.cos(angle), jnp.sin(angle)


def filter_any(field, transmit, count):
    grid = field.shape[1]
    span = grid * grid
    share = -(-span // count)
    flat = jnp.pad(field.reshape(2, span), ((0, 0), (0, share * count - span)))
    parts = flat.reshape(2, count, share).transpose(1, 0, 2)
    got = lax.all_to_all(parts, AXES, split_axis=0, concat_axis=0, tiled=True)
    got = jnp.roll(got, 2, axis=0)
    real, imag = got[:, 0], got[:, 1]
    times = jnp.arange(count, dtype=jnp.int32)
    cosine, sine = angle_table(times, times, count)
    spec_real = exact_dot(cosine, real) + exact_dot(sine, imag)
    spec_imag = exact_dot(cosine, imag) - exact_dot(sine, real)
    gain_real, gain_imag = transmit[0][:, None], transmit[1][:, None]
    shaped_real = gain_real * spec_real - gain_imag * spec_imag
    shaped_imag = gain_real * spec_imag + gain_imag * spec_real
    back_real = (exact_dot(cosine, shaped_real) - exact_dot(sine, shaped_imag)) / count
    back_imag = (exact_dot(cosine, shaped_imag) + exact_dot(sine, shaped_real)) / count
    back = jnp.stack([back_real, back_imag], axis=1)
    sent = jnp.roll(back, 2, axis=0)
    fields = lax.all_to_all(sent, AXES, split_axis=0, concat_axis=0, tiled=True)
    fields = fields.transpose(1, 0, 2).reshape(2, share * count)[:, :span]
    return fields.reshape(2, grid, grid)


def on_device(radiation, phases, energy, pixels, destination, propagator, transmit):
    cuts, groups = lax.axis_size("cuts"), lax.axis_size("group")
    count = cuts * groups
    grid = radiation.shape[-1]
    blocks, size = phases.shape[1:]
    cap = max(2, 2 * blocks // cuts)
    rows = grid // count if grid % count == 0 else 0
    if rows != 4 or cap * KINDS != count or cuts != KINDS or size % 128 or blocks != 2 * cap or groups % 8:
        rows = 0
    field = radiation[0]
    shape = lambda *dims: jax.ShapeDtypeStruct(dims, F32)
    read = lambda number: pltpu.VMEM((2, number, size), F32)
    hot = lambda number: [pltpu.VMEM((2 * grid, number * size), BF16), pltpu.VMEM((grid, number * size), BF16)]
    pass_flops = 4 * blocks * size * grid * grid
    prop_flops = 48 * grid**3

    state = call(
        kick_kernel, shape(4 * blocks, size),
        [
            pltpu.VMEM((2, grid, grid), F32),
            pltpu.VMEM((blocks, size), F32),
            pltpu.VMEM((blocks, size), F32),
            pltpu.VMEM((blocks, size), jnp.int32),
            pltpu.VMEM((1, blocks), jnp.int32),
            read(blocks),
            pltpu.SemaphoreType.DMA((5,)),
        ],
        pass_flops, (field, phases[0], energy[0], pixels[0], destination), pl.ANY, WHOLE_VMEM,
    )
    route = [((i + 1) % count, i) for i in range(count)]
    behind = lax.ppermute(state, AXES, route)
    field = call(
        functools.partial(radiate_kernel, blocks, count - 1), shape(2, grid, grid), hot(blocks), pass_flops + prop_flops,
        (field, state, propagator),
    )
    part_shape = shape(count * 3, rows, grid) if rows else shape(2, grid, grid)
    send_shapes = [] if rows else [shape(3 * cap, size)] * cuts
    field, *sends = call(
        functools.partial(second_kernel, count, rows, cap), (part_shape, *send_shapes),
        [read(blocks)] + hot(blocks), 2 * pass_flops + prop_flops,
        (field, behind, propagator),
    )
    chunks_in = [
        lax.ppermute(send, AXES, [(i, (i + 3 + groups * ahead) % count) for i in range(count)])
        for ahead, send in enumerate(sends)
    ]
    if rows:
        matrix = call(
            matrix_kernel, jax.ShapeDtypeStruct((2 * count, 6 * count), BF16), [], 1 << 20,
            (transmit, *time_tables(count)),
        )
        data = lax.all_to_all(field, AXES, split_axis=0, concat_axis=0, tiled=True)
        sent = call(
            functools.partial(filter_kernel, cuts, blocks // cap), shape(count * 3, rows, grid), [], 1 << 24,
            (matrix, data),
        )
        fields = lax.all_to_all(sent, AXES, split_axis=0, concat_axis=0, tiled=True)
    else:
        fields = filter_any(field, transmit, count)
    capacity = cuts * cap
    share = capacity // blocks
    field, state = call(
        functools.partial(third_kernel, cuts), (shape(2, grid, grid), shape(3 * capacity, size)),
        [read(capacity)], share * pass_flops, (fields, *chunks_in),
    )
    behind = lax.ppermute(state, AXES, route)
    field = call(
        functools.partial(radiate_kernel, capacity, 1), shape(2, grid, grid), hot(capacity),
        share * pass_flops + prop_flops, (field, state, propagator),
    )
    out = call(
        fourth_kernel, shape(2, grid, grid), [read(capacity)] + hot(capacity),
        2 * share * pass_flops + prop_flops, (field, behind, propagator),
    )
    return out[None]


def solution(mesh):
    return jax.shard_map(
        on_device,
        mesh=mesh,
        in_specs=(
            P(("cuts", "group"), None, None, None),
            P(("cuts", "group"), None, None),
            P(("cuts", "group"), None, None),
            P(("cuts", "group"), None, None),
            P(("cuts", "group"), None),
            P(),
            P(),
        ),
        out_specs=P(("cuts", "group"), None, None, None),
        check_vma=False,
    )
```

```python
import functools
import math

import jax
import jax.numpy as jnp
from jax import lax
from jax.experimental import pallas as pl
from jax.experimental.pallas import tpu as pltpu
from jax.sharding import PartitionSpec as P

KICK_RATE = 0.5
PHASE_RATE = 1.0
EMIT_RATE = 0.5

AXES = ("cuts", "group")
F32 = jnp.float32
BF16 = jnp.bfloat16
KINDS = 4
VMEM_LIMIT = 48 * 1024 * 1024


def dot(left, right, left_dim, right_dim):
    dims = (((left_dim,), (right_dim,)), ((), ()))
    return lax.dot_general(left, right, dims, preferred_element_type=F32)


def exact_dot(left, right):
    return jnp.dot(left, right, precision=lax.Precision.HIGHEST, preferred_element_type=F32)


def split(value):
    high = value.astype(BF16)
    return high, (value - high.astype(F32)).astype(BF16)


def real_form(propagator):
    prop_real, prop_imag = propagator[0], propagator[1]
    form = jnp.concatenate(
        [
            jnp.concatenate([prop_real, -prop_imag], axis=1),
            jnp.concatenate([prop_imag, prop_real], axis=1),
        ],
        axis=0,
    )
    return split(form)


def diffract(real, imag, form_high, form_low):
    size = real.shape[0]
    high, low = split(jnp.concatenate([real, imag], axis=1))
    both = dot(jnp.concatenate([high, low], axis=0), form_high, 1, 1)
    right = both[:size] + both[size:] + dot(high, form_low, 1, 1)
    high, low = split(jnp.concatenate([right[:, :size], right[:, size:]], axis=0))
    both = dot(form_high, jnp.concatenate([high, low], axis=1), 1, 0)
    out = both[:, :size] + both[:, size:] + dot(form_low, high, 1, 0)
    return out[:size], out[size:]


def cells(pixels, grid):
    half = grid // 2
    shift = grid.bit_length() - 1
    if grid == 1 << shift:
        row, col = lax.shift_right_arithmetic(pixels, shift), pixels & (grid - 1)
    else:
        row, col = pixels // grid, pixels % grid
    right = col >= half
    place = jnp.where(pixels < 0, -1, jnp.where(right, row + grid, row))
    return place, jnp.where(right, col - half, col)


def swapped(value):
    half = value.shape[1] // 2
    return jnp.concatenate([value[:, half:], value[:, :half]], axis=1)


def fold(first, second):
    left = lax.broadcasted_iota(jnp.int32, first.shape, 1) < first.shape[1] // 2
    return jnp.where(left, first, swapped(second)), jnp.where(left, swapped(first), second)


def chunks(blocks):
    width = 2 if blocks % 2 == 0 else 1
    return [(start, width) for start in range(0, blocks, width)]


def lanes(array, start, width):
    return jnp.concatenate([array[start + k : start + k + 1] for k in range(width)], axis=1)


def hits(ids, span):
    return lax.broadcasted_iota(jnp.int32, (span, ids.shape[1]), 0) == ids


def one_hot(place, start, width, span):
    ids = lanes(place, start, width).astype(F32)
    rows = lax.broadcasted_iota(jnp.int32, (span, ids.shape[1]), 0).astype(F32)
    if span <= 256:
        ids, rows = ids.astype(BF16), rows.astype(BF16)
    one, zero = jnp.ones((), BF16), jnp.zeros((), BF16)
    return jnp.where(rows == ids, one, zero)


def kick(real, imag, phases, energy, pixels, read_ref, hot_ref=None):
    grid = real.shape[0]
    half = grid // 2
    blocks, size = phases.shape
    upper, lower = fold(real, imag)
    low = jnp.concatenate([upper, lower], axis=0).astype(BF16)
    place, col = cells(pixels, grid)
    for start, width in chunks(blocks):
        hot = one_hot(place, start, width, 2 * grid)
        if hot_ref is not None:
            hot_ref[:, start * size : (start + width) * size] = hot
        picked = dot(low, hot, 0, 0)
        col_hit = hits(lanes(col, start, width), half)
        for part in range(2):
            value = picked[part * half : (part + 1) * half]
            value = jnp.sum(jnp.where(col_hit, value, 0.0), axis=0, keepdims=True)
            for k in range(width):
                read_ref[part, start + k : start + k + 1, :] = value[:, k * size : (k + 1) * size]
    read_real = read_ref[0, :blocks, :]
    read_imag = read_ref[1, :blocks, :]
    energy = energy - KICK_RATE * (read_real * jnp.cos(phases) - read_imag * jnp.sin(phases))
    return phases + PHASE_RATE * energy, energy


def emit(real, imag, phases, pixels, hot_ref, spread_ref, filled):
    grid = real.shape[0]
    half = grid // 2
    blocks, size = phases.shape
    place, col = cells(pixels, grid)
    weight_real = jnp.cos(phases)
    weight_imag = -jnp.sin(phases)
    for start, width in chunks(blocks):
        where = slice(start * size, (start + width) * size)
        if not filled:
            hot_ref[:, where] = one_hot(place, start, width, 2 * grid)
        col_hit = hits(lanes(col, start, width), half)
        for part, weight in ((0, weight_real), (1, weight_imag)):
            value = jnp.where(col_hit, lanes(weight, start, width), 0.0)
            spread_ref[part * half : (part + 1) * half, where] = value.astype(BF16)
    span = blocks * size
    source = dot(hot_ref[:, :span], spread_ref[:, :span], 1, 1)
    source_real, source_imag = fold(source[:grid], source[grid:])
    return real + EMIT_RATE * source_real, imag + EMIT_RATE * source_imag


def position():
    return lax.axis_index("cuts") * lax.axis_size("group") + lax.axis_index("group")


def kept_unless(index):
    return jnp.where(position() == index, 0.0, 1.0).astype(F32)


def kick_kernel(field_hbm, phases_hbm, energy_hbm, pixels_hbm, dest_hbm, out, field, phases, energy, pixels, dest, read_ref, sems):
    blocks, size = phases.shape
    pairs = ((field_hbm, field), (pixels_hbm, pixels), (phases_hbm, phases), (energy_hbm, energy), (dest_hbm, dest))
    copies = [pltpu.make_async_copy(source, target, sems.at[k]) for k, (source, target) in enumerate(pairs)]
    for copy in copies:
        copy.start()
    for copy in copies:
        copy.wait()
    new_phases, new_energy = kick(field[0], field[1], phases[...], energy[...], pixels[...], read_ref)
    out[0:blocks, :] = new_phases
    out[blocks : 2 * blocks, :] = new_energy
    out[2 * blocks : 3 * blocks, :] = pixels[...].astype(F32)
    square = (blocks, blocks)
    own = lax.broadcasted_iota(jnp.int32, square, 0) == lax.broadcasted_iota(jnp.int32, square, 1)
    goals = jnp.where(own, jnp.broadcast_to(dest[0:1, :].astype(F32), square), 0.0)
    out[3 * blocks : 4 * blocks, :] = jnp.broadcast_to(jnp.sum(goals, axis=1, keepdims=True), (blocks, size))


def by_destination(kinds):
    goals = kinds[-1]
    blocks = goals.shape[0]
    place = lax.broadcasted_iota(jnp.int32, goals.shape, 0)
    rank = jnp.zeros(goals.shape, jnp.int32)
    for block in range(blocks):
        goal = goals[block : block + 1]
        ahead = (goal < goals) | ((goal == goals) & (place > block))
        rank = rank + jnp.where(ahead, 1, 0)
    ordered = [jnp.zeros(kind.shape, F32) for kind in kinds]
    for block in range(blocks):
        here = rank[block : block + 1] == place
        ordered = [jnp.where(here, kind[block : block + 1], old) for kind, old in zip(kinds, ordered)]
    return ordered


def lane_groups(values, shifts):
    size = values[0].shape[1]
    group = lax.broadcasted_iota(jnp.int32, values[0].shape, 1) // (size // len(values))
    joined_up = None
    for k, (value, shift) in enumerate(zip(values, shifts)):
        if shift % size:
            value = pltpu.roll(value, shift % size, axis=1)
        joined_up = value if joined_up is None else jnp.where(group == k, value, joined_up)
    return joined_up


def radiate(blocks, dropped, field, state, form, out, hot_ref, spread_ref):
    pixels = state[2 * blocks : 3 * blocks, :].astype(jnp.int32)
    real, imag = emit(field[0], field[1], state[0:blocks, :], pixels, hot_ref, spread_ref, False)
    real, imag = diffract(real, imag, *form)
    keep = kept_unless(dropped)
    out[0] = real * keep
    out[1] = imag * keep


def first_radiate_kernel(blocks, dropped, field, state, propagator, out, high, low, hot_ref, spread_ref):
    form = real_form(propagator)
    high[...], low[...] = form
    radiate(blocks, dropped, field, state, form, out, hot_ref, spread_ref)


def radiate_kernel(blocks, dropped, field, state, high, low, out, hot_ref, spread_ref):
    radiate(blocks, dropped, field, state, (high[...], low[...]), out, hot_ref, spread_ref)


def second_kernel(count, rows, cap, field, state, high, low, out, *rest):
    sends = rest[:-3]
    read_ref, hot_ref, spread_ref = rest[-3:]
    blocks, size = state.shape[0] // 4, state.shape[1]
    real, imag = field[0], field[1]
    grid = real.shape[0]
    pixels = state[2 * blocks : 3 * blocks, :].astype(jnp.int32)
    phases, energy = kick(real, imag, state[0:blocks, :], state[blocks : 2 * blocks, :], pixels, read_ref, hot_ref)
    kinds = by_destination((phases, energy, state[2 * blocks : 3 * blocks, :], state[3 * blocks : 4 * blocks, :]))
    if rows:
        pieces = len(kinds)
        width = size // pieces
        for chunk in range(blocks // cap):
            parts = [kind[chunk * cap : (chunk + 1) * cap] for kind in kinds]
            for piece in range(pieces):
                row = lane_groups(parts, [(k - piece) * width for k in range(pieces)])
                out[pl.ds(piece * cap * 3 + 2, cap, stride=3), chunk, :] = row
    else:
        cuts = len(sends)
        cut = lax.div(lax.rem(position() + 1, count), count // cuts)
        for ahead, send in enumerate(sends):
            wanted = lax.rem(cut + ahead, cuts).astype(F32)
            chunk = [jnp.zeros((cap, size), F32)] * 2 + [jnp.full((cap, size), -1.0, F32)]
            for start in range(0, blocks, cap):
                goes = kinds[3][start : start + cap] == wanted
                chunk = [jnp.where(goes, kind[start : start + cap], old) for kind, old in zip(kinds, chunk)]
            for kind in range(3):
                send[kind * cap : (kind + 1) * cap, :] = chunk[kind]
    real, imag = emit(real, imag, phases, pixels, hot_ref, spread_ref, True)
    real, imag = diffract(real, imag, high[...], low[...])
    keep = kept_unless(count - 2)
    real, imag = real * keep, imag * keep
    if rows:
        for part in range(grid // rows):
            out[3 * part] = real[part * rows : (part + 1) * rows]
            out[3 * part + 1] = imag[part * rows : (part + 1) * rows]
    else:
        out[0] = real
        out[1] = imag


def matrix_kernel(transmit, cos_out, sin_out, cos_in, sin_in, out):
    gain_real, gain_imag = transmit[0:1, :], transmit[1:2, :]
    cosine, sine = cos_out[...], sin_out[...]
    real = cosine * gain_real - sine * gain_imag
    imag = cosine * gain_imag + sine * gain_real
    full_real = exact_dot(real, cos_in[...]) + exact_dot(imag, sin_in[...])
    full_imag = exact_dot(imag, cos_in[...]) - exact_dot(real, sin_in[...])
    form = jnp.concatenate(
        [
            jnp.concatenate([full_real, -full_imag], axis=1),
            jnp.concatenate([full_imag, full_real], axis=1),
        ],
        axis=0,
    )
    high, low = split(form)
    out[...] = jnp.concatenate([high, high, low], axis=1)


def filter_kernel(cuts, chunk_count, matrix, data, out):
    count = data.shape[0] // 3
    rows, size = data.shape[1:]
    groups = count // cuts
    stacked = jnp.concatenate(
        [
            jnp.concatenate([data[pl.ds(part, count, stride=3), j, :] for part in range(2)], axis=0)
            for j in range(rows)
        ],
        axis=1,
    )
    high, low = split(stacked)
    result = dot(matrix[...], jnp.concatenate([high, low, high], axis=0), 1, 0)
    for part in range(2):
        for j in range(rows):
            out[pl.ds(part, count, stride=3), j, :] = result[
                part * count : (part + 1) * count, j * size : (j + 1) * size
            ]
    bundles = [pltpu.roll(data[pl.ds(2, count, stride=3), chunk, :], 1, axis=0) for chunk in range(chunk_count)]
    goals = [bundle[:, size - 1 : size] for bundle in bundles]
    for cut in range(cuts):
        chosen = bundles[0]
        for bundle, goal in zip(bundles[1:], goals[1:]):
            chosen = jnp.where(goal == float(cut), bundle, chosen)
        first = cut * groups + 2
        fits = min(groups, count - first)
        for source in range(cuts):
            tile = chosen[source * groups : (source + 1) * groups]
            out[pl.ds(3 * first + 2, fits, stride=3), source, :] = tile[:fits]
            for k in range(fits, groups):
                out[3 * (first + k - count) + 2, source : source + 1, :] = tile[k : k + 1]


def joined(chunks_in):
    cap = chunks_in[0].shape[0] // 3
    kinds = [
        jnp.concatenate([chunk[kind * cap : (kind + 1) * cap, :] for chunk in chunks_in], axis=0)
        for kind in range(3)
    ]
    return kinds[0], kinds[1], kinds[2].astype(jnp.int32)


def relayed(fields, cuts):
    count = fields.shape[0] // 3
    size = fields.shape[2]
    width = size // KINDS
    bundles = [fields[pl.ds(2, count, stride=3), cut, :] for cut in range(cuts)]
    kinds = [lane_groups(bundles, [(cut - kind) * width for cut in range(cuts)]) for kind in range(KINDS)]
    wanted = lax.div(lax.rem(position() + (count - 2), count), count // cuts).astype(F32)
    return kinds[0], kinds[1], jnp.where(kinds[3] == wanted, kinds[2], -1.0).astype(jnp.int32)


def third_kernel(cuts, fields, *rest):
    out, state, read_ref = rest[-3:]
    chunks_in = rest[:-3]
    if chunks_in:
        phases, energy, pixels = joined(chunks_in)
        out[...] = fields[...]
    else:
        phases, energy, pixels = relayed(fields, cuts)
        rows = fields.shape[1]
        for part in range(fields.shape[0] // 3):
            for kind in range(2):
                out[kind, part * rows : (part + 1) * rows, :] = fields[3 * part + kind]
    phases, energy = kick(out[0], out[1], phases, energy, pixels, read_ref)
    blocks = phases.shape[0]
    state[0:blocks, :] = phases
    state[blocks : 2 * blocks, :] = energy
    state[2 * blocks : 3 * blocks, :] = pixels.astype(F32)


def fourth_kernel(field, state, high, low, out, read_ref, hot_ref, spread_ref):
    blocks = state.shape[0] // 3
    pixels = state[2 * blocks : 3 * blocks, :].astype(jnp.int32)
    real, imag = field[0], field[1]
    phases, _ = kick(real, imag, state[0:blocks, :], state[blocks : 2 * blocks, :], pixels, read_ref, hot_ref)
    real, imag = emit(real, imag, phases, pixels, hot_ref, spread_ref, True)
    real, imag = diffract(real, imag, high[...], low[...])
    keep = kept_unless(0)
    out[0] = real * keep
    out[1] = imag * keep


def call(kernel, out_shape, scratch, flops, args, memory=pltpu.VMEM):
    specs = [pl.BlockSpec(memory_space=memory)] * len(args)
    return pl.pallas_call(
        kernel,
        out_shape=out_shape,
        in_specs=specs,
        out_specs=jax.tree.map(lambda _: pl.BlockSpec(memory_space=pltpu.VMEM), out_shape),
        scratch_shapes=scratch,
        compiler_params=pltpu.CompilerParams(vmem_limit_bytes=VMEM_LIMIT),
        cost_estimate=pl.CostEstimate(flops=flops, bytes_accessed=1 << 19, transcendentals=0),
    )(*args)


def time_tables(count):
    times = jnp.arange(count, dtype=jnp.int32)
    cos_out, sin_out = angle_table((times + (count - 4)) % count, times, count)
    return (cos_out / count, sin_out / count, *angle_table(times, times, count))


def angle_table(first_ids, second_ids, total_slices):
    product = first_ids[:, None] * second_ids[None, :] % total_slices
    angle = product.astype(F32) * (2.0 * math.pi / total_slices)
    return jnp.cos(angle), jnp.sin(angle)


def filter_any(field, transmit, count):
    grid = field.shape[1]
    span = grid * grid
    share = -(-span // count)
    flat = jnp.pad(field.reshape(2, span), ((0, 0), (0, share * count - span)))
    parts = flat.reshape(2, count, share).transpose(1, 0, 2)
    got = lax.all_to_all(parts, AXES, split_axis=0, concat_axis=0, tiled=True)
    got = jnp.roll(got, 2, axis=0)
    real, imag = got[:, 0], got[:, 1]
    times = jnp.arange(count, dtype=jnp.int32)
    cosine, sine = angle_table(times, times, count)
    spec_real = exact_dot(cosine, real) + exact_dot(sine, imag)
    spec_imag = exact_dot(cosine, imag) - exact_dot(sine, real)
    gain_real, gain_imag = transmit[0][:, None], transmit[1][:, None]
    shaped_real = gain_real * spec_real - gain_imag * spec_imag
    shaped_imag = gain_real * spec_imag + gain_imag * spec_real
    back_real = (exact_dot(cosine, shaped_real) - exact_dot(sine, shaped_imag)) / count
    back_imag = (exact_dot(cosine, shaped_imag) + exact_dot(sine, shaped_real)) / count
    back = jnp.stack([back_real, back_imag], axis=1)
    sent = jnp.roll(back, 2, axis=0)
    fields = lax.all_to_all(sent, AXES, split_axis=0, concat_axis=0, tiled=True)
    fields = fields.transpose(1, 0, 2).reshape(2, share * count)[:, :span]
    return fields.reshape(2, grid, grid)


def on_device(radiation, phases, energy, pixels, destination, propagator, transmit):
    cuts, groups = lax.axis_size("cuts"), lax.axis_size("group")
    count = cuts * groups
    grid = radiation.shape[-1]
    blocks, size = phases.shape[1:]
    cap = max(2, 2 * blocks // cuts)
    rows = grid // count if grid % count == 0 else 0
    if rows != 4 or cap * KINDS != count or cuts != KINDS or size % 128 or blocks != 2 * cap or groups % 8:
        rows = 0
    field = radiation[0]
    shape = lambda *dims: jax.ShapeDtypeStruct(dims, F32)
    read = lambda number: pltpu.VMEM((2, number, size), F32)
    hot = lambda number: [pltpu.VMEM((2 * grid, number * size), BF16), pltpu.VMEM((grid, number * size), BF16)]
    pass_flops = 4 * blocks * size * grid * grid
    prop_flops = 48 * grid**3

    given = (field, phases[0], energy[0], pixels[0], destination)
    state = call(
        kick_kernel, shape(4 * blocks, size),
        [
            pltpu.VMEM((2, grid, grid), F32),
            pltpu.VMEM((blocks, size), F32),
            pltpu.VMEM((blocks, size), F32),
            pltpu.VMEM((blocks, size), jnp.int32),
            pltpu.VMEM((1, blocks), jnp.int32),
            read(blocks),
            pltpu.SemaphoreType.DMA((5,)),
        ],
        pass_flops, tuple(pltpu.with_memory_space_constraint(value, pltpu.HBM) for value in given), pl.ANY,
    )
    route = [((i + 1) % count, i) for i in range(count)]
    behind = lax.ppermute(state, AXES, route)
    form_shape = jax.ShapeDtypeStruct((2 * grid, 2 * grid), BF16)
    field, *form = call(
        functools.partial(first_radiate_kernel, blocks, count - 1),
        (shape(2, grid, grid), form_shape, form_shape), hot(blocks), pass_flops + prop_flops,
        (field, state, propagator),
    )
    part_shape = shape(count * 3, rows, grid) if rows else shape(2, grid, grid)
    send_shapes = [] if rows else [shape(3 * cap, size)] * cuts
    field, *sends = call(
        functools.partial(second_kernel, count, rows, cap), (part_shape, *send_shapes),
        [read(blocks)] + hot(blocks), 2 * pass_flops + prop_flops,
        (field, behind, *form),
    )
    chunks_in = [
        lax.ppermute(send, AXES, [(i, (i + 3 + groups * ahead) % count) for i in range(count)])
        for ahead, send in enumerate(sends)
    ]
    if rows:
        matrix = call(
            matrix_kernel, jax.ShapeDtypeStruct((2 * count, 6 * count), BF16), [], 1 << 20,
            (transmit, *time_tables(count)),
        )
        data = lax.all_to_all(field, AXES, split_axis=0, concat_axis=0, tiled=True)
        sent = call(
            functools.partial(filter_kernel, cuts, blocks // cap), shape(count * 3, rows, grid), [], 1 << 24,
            (matrix, data),
        )
        fields = lax.all_to_all(sent, AXES, split_axis=0, concat_axis=0, tiled=True)
    else:
        fields = filter_any(field, transmit, count)
    capacity = cuts * cap
    share = capacity // blocks
    field, state = call(
        functools.partial(third_kernel, cuts), (shape(2, grid, grid), shape(3 * capacity, size)),
        [read(capacity)], share * pass_flops, (fields, *chunks_in),
    )
    behind = lax.ppermute(state, AXES, route)
    field = call(
        functools.partial(radiate_kernel, capacity, 1), shape(2, grid, grid), hot(capacity),
        share * pass_flops + prop_flops, (field, state, *form),
    )
    out = call(
        fourth_kernel, shape(2, grid, grid), [read(capacity)] + hot(capacity),
        2 * share * pass_flops + prop_flops, (field, behind, *form),
    )
    return out[None]


def solution(mesh):
    return jax.shard_map(
        on_device,
        mesh=mesh,
        in_specs=(
            P(("cuts", "group"), None, None, None),
            P(("cuts", "group"), None, None),
            P(("cuts", "group"), None, None),
            P(("cuts", "group"), None, None),
            P(("cuts", "group"), None),
            P(),
            P(),
        ),
        out_specs=P(("cuts", "group"), None, None, None),
        check_vma=False,
    )
```

```python
import functools
import math

import jax
import jax.numpy as jnp
from jax import lax
from jax.experimental import pallas as pl
from jax.experimental.pallas import tpu as pltpu
from jax.sharding import PartitionSpec as P

KICK_RATE = 0.5
PHASE_RATE = 1.0
EMIT_RATE = 0.5

AXES = ("cuts", "group")
F32 = jnp.float32
BF16 = jnp.bfloat16
KINDS = 4
VMEM_LIMIT = 48 * 1024 * 1024


def dot(left, right, left_dim, right_dim):
    dims = (((left_dim,), (right_dim,)), ((), ()))
    return lax.dot_general(left, right, dims, preferred_element_type=F32)


def exact_dot(left, right):
    return jnp.dot(left, right, precision=lax.Precision.HIGHEST, preferred_element_type=F32)


def split(value):
    high = value.astype(BF16)
    return high, (value - high.astype(F32)).astype(BF16)


def real_form(propagator):
    prop_real, prop_imag = propagator[0], propagator[1]
    form = jnp.concatenate(
        [
            jnp.concatenate([prop_real, -prop_imag], axis=1),
            jnp.concatenate([prop_imag, prop_real], axis=1),
        ],
        axis=0,
    )
    return split(form)


def diffract(real, imag, form_high, form_low):
    size = real.shape[0]
    high, low = split(jnp.concatenate([real, imag], axis=1))
    both = dot(jnp.concatenate([high, low], axis=0), form_high, 1, 1)
    right = both[:size] + both[size:] + dot(high, form_low, 1, 1)
    high, low = split(jnp.concatenate([right[:, :size], right[:, size:]], axis=0))
    both = dot(form_high, jnp.concatenate([high, low], axis=1), 1, 0)
    out = both[:, :size] + both[:, size:] + dot(form_low, high, 1, 0)
    return out[:size], out[size:]


def cells(pixels, grid):
    half = grid // 2
    shift = grid.bit_length() - 1
    if grid == 1 << shift:
        row, col = lax.shift_right_arithmetic(pixels, shift), pixels & (grid - 1)
    else:
        row, col = pixels // grid, pixels % grid
    right = col >= half
    place = jnp.where(pixels < 0, -1, jnp.where(right, row + grid, row))
    return place, jnp.where(right, col - half, col)


def swapped(value):
    half = value.shape[1] // 2
    return jnp.concatenate([value[:, half:], value[:, :half]], axis=1)


def fold(first, second):
    left = lax.broadcasted_iota(jnp.int32, first.shape, 1) < first.shape[1] // 2
    return jnp.where(left, first, swapped(second)), jnp.where(left, swapped(first), second)


def chunks(blocks):
    width = 2 if blocks % 2 == 0 else 1
    return [(start, width) for start in range(0, blocks, width)]


def lanes(array, start, width):
    return jnp.concatenate([array[start + k : start + k + 1] for k in range(width)], axis=1)


def hits(ids, span):
    return lax.broadcasted_iota(jnp.int32, (span, ids.shape[1]), 0) == ids


def one_hot(place, start, width, span):
    ids = lanes(place, start, width).astype(F32)
    rows = lax.broadcasted_iota(jnp.int32, (span, ids.shape[1]), 0).astype(F32)
    if span <= 256:
        ids, rows = ids.astype(BF16), rows.astype(BF16)
    one, zero = jnp.ones((), BF16), jnp.zeros((), BF16)
    return jnp.where(rows == ids, one, zero)


def kick(real, imag, phases, energy, pixels, read_ref, hot_ref=None):
    grid = real.shape[0]
    half = grid // 2
    blocks, size = phases.shape
    upper, lower = fold(real, imag)
    low = jnp.concatenate([upper, lower], axis=0).astype(BF16)
    place, col = cells(pixels, grid)
    for start, width in chunks(blocks):
        hot = one_hot(place, start, width, 2 * grid)
        if hot_ref is not None:
            hot_ref[:, start * size : (start + width) * size] = hot
        picked = dot(low, hot, 0, 0)
        col_hit = hits(lanes(col, start, width), half)
        for part in range(2):
            value = picked[part * half : (part + 1) * half]
            value = jnp.sum(jnp.where(col_hit, value, 0.0), axis=0, keepdims=True)
            for k in range(width):
                read_ref[part, start + k : start + k + 1, :] = value[:, k * size : (k + 1) * size]
    read_real = read_ref[0, :blocks, :]
    read_imag = read_ref[1, :blocks, :]
    energy = energy - KICK_RATE * (read_real * jnp.cos(phases) - read_imag * jnp.sin(phases))
    return phases + PHASE_RATE * energy, energy


def emit(real, imag, phases, pixels, hot_ref, spread_ref, filled):
    grid = real.shape[0]
    half = grid // 2
    blocks, size = phases.shape
    place, col = cells(pixels, grid)
    weight_real = jnp.cos(phases)
    weight_imag = -jnp.sin(phases)
    for start, width in chunks(blocks):
        where = slice(start * size, (start + width) * size)
        if not filled:
            hot_ref[:, where] = one_hot(place, start, width, 2 * grid)
        col_hit = hits(lanes(col, start, width), half)
        for part, weight in ((0, weight_real), (1, weight_imag)):
            value = jnp.where(col_hit, lanes(weight, start, width), 0.0)
            spread_ref[part * half : (part + 1) * half, where] = value.astype(BF16)
    span = blocks * size
    source = dot(hot_ref[:, :span], spread_ref[:, :span], 1, 1)
    source_real, source_imag = fold(source[:grid], source[grid:])
    return real + EMIT_RATE * source_real, imag + EMIT_RATE * source_imag


def position():
    return lax.axis_index("cuts") * lax.axis_size("group") + lax.axis_index("group")


def kept_unless(index):
    return jnp.where(position() == index, 0.0, 1.0).astype(F32)


def kick_kernel(field_hbm, phases_hbm, energy_hbm, pixels_hbm, dest_hbm, out, field, phases, energy, pixels, dest, read_ref, sems):
    blocks, size = phases.shape
    pairs = ((field_hbm, field), (pixels_hbm, pixels), (phases_hbm, phases), (energy_hbm, energy), (dest_hbm, dest))
    copies = [pltpu.make_async_copy(source, target, sems.at[k]) for k, (source, target) in enumerate(pairs)]
    for copy in copies:
        copy.start()
    for copy in copies:
        copy.wait()
    new_phases, new_energy = kick(field[0], field[1], phases[...], energy[...], pixels[...], read_ref)
    out[0:blocks, :] = new_phases
    out[blocks : 2 * blocks, :] = new_energy
    out[2 * blocks : 3 * blocks, :] = pixels[...].astype(F32)
    square = (blocks, blocks)
    own = lax.broadcasted_iota(jnp.int32, square, 0) == lax.broadcasted_iota(jnp.int32, square, 1)
    goals = jnp.where(own, jnp.broadcast_to(dest[0:1, :].astype(F32), square), 0.0)
    out[3 * blocks : 4 * blocks, :] = jnp.broadcast_to(jnp.sum(goals, axis=1, keepdims=True), (blocks, size))


def by_destination(kinds):
    goals = kinds[-1]
    blocks = goals.shape[0]
    place = lax.broadcasted_iota(jnp.int32, goals.shape, 0)
    rank = jnp.zeros(goals.shape, jnp.int32)
    for block in range(blocks):
        goal = goals[block : block + 1]
        ahead = (goal < goals) | ((goal == goals) & (place > block))
        rank = rank + jnp.where(ahead, 1, 0)
    ordered = [jnp.zeros(kind.shape, F32) for kind in kinds]
    for block in range(blocks):
        here = rank[block : block + 1] == place
        ordered = [jnp.where(here, kind[block : block + 1], old) for kind, old in zip(kinds, ordered)]
    return ordered


def lane_groups(values, shifts):
    size = values[0].shape[1]
    group = lax.broadcasted_iota(jnp.int32, values[0].shape, 1) // (size // len(values))
    joined_up = None
    for k, (value, shift) in enumerate(zip(values, shifts)):
        if shift % size:
            value = pltpu.roll(value, shift % size, axis=1)
        joined_up = value if joined_up is None else jnp.where(group == k, value, joined_up)
    return joined_up


def radiate(blocks, dropped, field, state, form, out, hot_ref, spread_ref):
    pixels = state[2 * blocks : 3 * blocks, :].astype(jnp.int32)
    real, imag = emit(field[0], field[1], state[0:blocks, :], pixels, hot_ref, spread_ref, False)
    real, imag = diffract(real, imag, *form)
    keep = kept_unless(dropped)
    out[0] = real * keep
    out[1] = imag * keep


def first_radiate_kernel(blocks, dropped, field, state, propagator, *rest):
    *rest, hot_ref, spread_ref = rest
    if len(rest) > 3:
        *tables, out, high, low, matrix = rest
        matrix[...] = filter_matrix(*tables)
    else:
        out, high, low = rest
    form = real_form(propagator)
    high[...], low[...] = form
    radiate(blocks, dropped, field, state, form, out, hot_ref, spread_ref)


def radiate_kernel(blocks, dropped, field, state, high, low, out, hot_ref, spread_ref):
    radiate(blocks, dropped, field, state, (high[...], low[...]), out, hot_ref, spread_ref)


def second_kernel(count, rows, cap, field, state, high, low, out, *rest):
    sends = rest[:-3]
    read_ref, hot_ref, spread_ref = rest[-3:]
    blocks, size = state.shape[0] // 4, state.shape[1]
    real, imag = field[0], field[1]
    grid = real.shape[0]
    pixels = state[2 * blocks : 3 * blocks, :].astype(jnp.int32)
    phases, energy = kick(real, imag, state[0:blocks, :], state[blocks : 2 * blocks, :], pixels, read_ref, hot_ref)
    kinds = by_destination((phases, energy, state[2 * blocks : 3 * blocks, :], state[3 * blocks : 4 * blocks, :]))
    if rows:
        pairs, pieces = rows // 2, len(kinds)
        tiles = 2 * pairs + 1
        width = size // pieces
        for chunk in range(blocks // cap):
            parts = [kind[chunk * cap : (chunk + 1) * cap] for kind in kinds]
            for piece in range(pieces):
                row = lane_groups(parts, [(k - piece) * width for k in range(pieces)])
                out[pl.ds((piece * cap + 1) * tiles - 1, cap, stride=tiles), chunk, :] = row
    else:
        cuts = len(sends)
        cut = lax.div(lax.rem(position() + 1, count), count // cuts)
        for ahead, send in enumerate(sends):
            wanted = lax.rem(cut + ahead, cuts).astype(F32)
            chunk = [jnp.zeros((cap, size), F32)] * 2 + [jnp.full((cap, size), -1.0, F32)]
            for start in range(0, blocks, cap):
                goes = kinds[3][start : start + cap] == wanted
                chunk = [jnp.where(goes, kind[start : start + cap], old) for kind, old in zip(kinds, chunk)]
            for kind in range(3):
                send[kind * cap : (kind + 1) * cap, :] = chunk[kind]
    real, imag = emit(real, imag, phases, pixels, hot_ref, spread_ref, True)
    real, imag = diffract(real, imag, high[...], low[...])
    keep = kept_unless(count - 2)
    real, imag = real * keep, imag * keep
    if rows:
        for part in range(grid // rows):
            for pair in range(pairs):
                first = part * rows + 2 * pair
                out[part * tiles + pair] = real[first : first + 2]
                out[part * tiles + pairs + pair] = imag[first : first + 2]
    else:
        out[0] = real
        out[1] = imag


def filter_matrix(transmit, cos_out, sin_out, cos_in, sin_in):
    gain_real, gain_imag = transmit[0:1, :], transmit[1:2, :]
    cosine, sine = cos_out[...], sin_out[...]
    real = cosine * gain_real - sine * gain_imag
    imag = cosine * gain_imag + sine * gain_real
    full_real = exact_dot(real, cos_in[...]) + exact_dot(imag, sin_in[...])
    full_imag = exact_dot(imag, cos_in[...]) - exact_dot(real, sin_in[...])
    form = jnp.concatenate(
        [
            jnp.concatenate([full_real, -full_imag], axis=1),
            jnp.concatenate([full_imag, full_real], axis=1),
        ],
        axis=0,
    )
    high, low = split(form)
    return jnp.concatenate([high, high, low], axis=1)


def filter_kernel(cuts, chunk_count, matrix, data, out):
    count = out.shape[0] // 3
    rows, size = out.shape[1:]
    groups = count // cuts
    pairs = rows // 2
    tiles = 2 * pairs + 1
    stacked = jnp.concatenate(
        [
            jnp.concatenate(
                [data[pl.ds(part * pairs + j // 2, count, stride=tiles), j % 2, :] for part in range(2)], axis=0
            )
            for j in range(rows)
        ],
        axis=1,
    )
    high, low = split(stacked)
    result = dot(matrix[...], jnp.concatenate([high, low, high], axis=0), 1, 0)
    for part in range(2):
        for j in range(rows):
            out[pl.ds(part, count, stride=3), j, :] = result[
                part * count : (part + 1) * count, j * size : (j + 1) * size
            ]
    bundles = [
        pltpu.roll(data[pl.ds(tiles - 1, count, stride=tiles), chunk, :], 1, axis=0)
        for chunk in range(chunk_count)
    ]
    goals = [bundle[:, size - 1 : size] for bundle in bundles]
    for cut in range(cuts):
        chosen = bundles[0]
        for bundle, goal in zip(bundles[1:], goals[1:]):
            chosen = jnp.where(goal == float(cut), bundle, chosen)
        first = cut * groups + 2
        fits = min(groups, count - first)
        for source in range(cuts):
            tile = chosen[source * groups : (source + 1) * groups]
            out[pl.ds(3 * first + 2, fits, stride=3), source, :] = tile[:fits]
            for k in range(fits, groups):
                out[3 * (first + k - count) + 2, source : source + 1, :] = tile[k : k + 1]


def joined(chunks_in):
    cap = chunks_in[0].shape[0] // 3
    kinds = [
        jnp.concatenate([chunk[kind * cap : (kind + 1) * cap, :] for chunk in chunks_in], axis=0)
        for kind in range(3)
    ]
    return kinds[0], kinds[1], kinds[2].astype(jnp.int32)


def relayed(fields, cuts):
    count = fields.shape[0] // 3
    size = fields.shape[2]
    width = size // KINDS
    bundles = [fields[pl.ds(2, count, stride=3), cut, :] for cut in range(cuts)]
    kinds = [lane_groups(bundles, [(cut - kind) * width for cut in range(cuts)]) for kind in range(KINDS)]
    wanted = lax.div(lax.rem(position() + (count - 2), count), count // cuts).astype(F32)
    return kinds[0], kinds[1], jnp.where(kinds[3] == wanted, kinds[2], -1.0).astype(jnp.int32)


def third_kernel(cuts, fields, *rest):
    out, state, read_ref = rest[-3:]
    chunks_in = rest[:-3]
    if chunks_in:
        phases, energy, pixels = joined(chunks_in)
        out[...] = fields[...]
    else:
        phases, energy, pixels = relayed(fields, cuts)
        rows = fields.shape[1]
        for part in range(fields.shape[0] // 3):
            for kind in range(2):
                out[kind, part * rows : (part + 1) * rows, :] = fields[3 * part + kind]
    phases, energy = kick(out[0], out[1], phases, energy, pixels, read_ref)
    blocks = phases.shape[0]
    state[0:blocks, :] = phases
    state[blocks : 2 * blocks, :] = energy
    state[2 * blocks : 3 * blocks, :] = pixels.astype(F32)


def fourth_kernel(field, state, high, low, out, read_ref, hot_ref, spread_ref):
    blocks = state.shape[0] // 3
    pixels = state[2 * blocks : 3 * blocks, :].astype(jnp.int32)
    real, imag = field[0], field[1]
    phases, _ = kick(real, imag, state[0:blocks, :], state[blocks : 2 * blocks, :], pixels, read_ref, hot_ref)
    real, imag = emit(real, imag, phases, pixels, hot_ref, spread_ref, True)
    real, imag = diffract(real, imag, high[...], low[...])
    keep = kept_unless(0)
    out[0] = real * keep
    out[1] = imag * keep


def call(kernel, out_shape, scratch, flops, args, memory=pltpu.VMEM):
    specs = [pl.BlockSpec(memory_space=memory)] * len(args)
    return pl.pallas_call(
        kernel,
        out_shape=out_shape,
        in_specs=specs,
        out_specs=jax.tree.map(lambda _: pl.BlockSpec(memory_space=pltpu.VMEM), out_shape),
        scratch_shapes=scratch,
        compiler_params=pltpu.CompilerParams(vmem_limit_bytes=VMEM_LIMIT),
        cost_estimate=pl.CostEstimate(flops=flops, bytes_accessed=1 << 19, transcendentals=0),
    )(*args)


def time_tables(count):
    times = jnp.arange(count, dtype=jnp.int32)
    cos_out, sin_out = angle_table((times + (count - 4)) % count, times, count)
    return (cos_out / count, sin_out / count, *angle_table(times, times, count))


def angle_table(first_ids, second_ids, total_slices):
    product = first_ids[:, None] * second_ids[None, :] % total_slices
    angle = product.astype(F32) * (2.0 * math.pi / total_slices)
    return jnp.cos(angle), jnp.sin(angle)


def filter_any(field, transmit, count):
    grid = field.shape[1]
    span = grid * grid
    share = -(-span // count)
    flat = jnp.pad(field.reshape(2, span), ((0, 0), (0, share * count - span)))
    parts = flat.reshape(2, count, share).transpose(1, 0, 2)
    got = lax.all_to_all(parts, AXES, split_axis=0, concat_axis=0, tiled=True)
    got = jnp.roll(got, 2, axis=0)
    real, imag = got[:, 0], got[:, 1]
    times = jnp.arange(count, dtype=jnp.int32)
    cosine, sine = angle_table(times, times, count)
    spec_real = exact_dot(cosine, real) + exact_dot(sine, imag)
    spec_imag = exact_dot(cosine, imag) - exact_dot(sine, real)
    gain_real, gain_imag = transmit[0][:, None], transmit[1][:, None]
    shaped_real = gain_real * spec_real - gain_imag * spec_imag
    shaped_imag = gain_real * spec_imag + gain_imag * spec_real
    back_real = (exact_dot(cosine, shaped_real) - exact_dot(sine, shaped_imag)) / count
    back_imag = (exact_dot(cosine, shaped_imag) + exact_dot(sine, shaped_real)) / count
    back = jnp.stack([back_real, back_imag], axis=1)
    sent = jnp.roll(back, 2, axis=0)
    fields = lax.all_to_all(sent, AXES, split_axis=0, concat_axis=0, tiled=True)
    fields = fields.transpose(1, 0, 2).reshape(2, share * count)[:, :span]
    return fields.reshape(2, grid, grid)


def on_device(radiation, phases, energy, pixels, destination, propagator, transmit):
    cuts, groups = lax.axis_size("cuts"), lax.axis_size("group")
    count = cuts * groups
    grid = radiation.shape[-1]
    blocks, size = phases.shape[1:]
    cap = max(2, 2 * blocks // cuts)
    rows = grid // count if grid % count == 0 else 0
    if rows != 4 or cap * KINDS != count or cuts != KINDS or size % 128 or blocks != 2 * cap or groups % 8:
        rows = 0
    field = radiation[0]
    shape = lambda *dims: jax.ShapeDtypeStruct(dims, F32)
    read = lambda number: pltpu.VMEM((2, number, size), F32)
    hot = lambda number: [pltpu.VMEM((2 * grid, number * size), BF16), pltpu.VMEM((grid, number * size), BF16)]
    pass_flops = 4 * blocks * size * grid * grid
    prop_flops = 48 * grid**3

    given = (field, phases[0], energy[0], pixels[0], destination)
    state = call(
        kick_kernel, shape(4 * blocks, size),
        [
            pltpu.VMEM((2, grid, grid), F32),
            pltpu.VMEM((blocks, size), F32),
            pltpu.VMEM((blocks, size), F32),
            pltpu.VMEM((blocks, size), jnp.int32),
            pltpu.VMEM((1, blocks), jnp.int32),
            read(blocks),
            pltpu.SemaphoreType.DMA((5,)),
        ],
        pass_flops, tuple(pltpu.with_memory_space_constraint(value, pltpu.HBM) for value in given), pl.ANY,
    )
    route = [((i + 1) % count, i) for i in range(count)]
    behind = lax.ppermute(state, AXES, route)
    form_shape = jax.ShapeDtypeStruct((2 * grid, 2 * grid), BF16)
    made = [shape(2, grid, grid), form_shape, form_shape]
    tables = ()
    if rows:
        made.append(jax.ShapeDtypeStruct((2 * count, 6 * count), BF16))
        tables = (transmit, *time_tables(count))
    field, *form = call(
        functools.partial(first_radiate_kernel, blocks, count - 1), made, hot(blocks), pass_flops + prop_flops,
        (field, state, propagator, *tables),
    )
    matrix = form[2:]
    form = form[:2]
    part_shape = shape(count * (rows + 1), 2, grid) if rows else shape(2, grid, grid)
    send_shapes = [] if rows else [shape(3 * cap, size)] * cuts
    field, *sends = call(
        functools.partial(second_kernel, count, rows, cap), (part_shape, *send_shapes),
        [read(blocks)] + hot(blocks), 2 * pass_flops + prop_flops,
        (field, behind, *form),
    )
    chunks_in = [
        lax.ppermute(send, AXES, [(i, (i + 3 + groups * ahead) % count) for i in range(count)])
        for ahead, send in enumerate(sends)
    ]
    if rows:
        data = lax.all_to_all(field, AXES, split_axis=0, concat_axis=0, tiled=True)
        sent = call(
            functools.partial(filter_kernel, cuts, blocks // cap), shape(count * 3, rows, grid), [], 1 << 24,
            (*matrix, data),
        )
        fields = lax.all_to_all(sent, AXES, split_axis=0, concat_axis=0, tiled=True)
    else:
        fields = filter_any(field, transmit, count)
    capacity = cuts * cap
    share = capacity // blocks
    field, state = call(
        functools.partial(third_kernel, cuts), (shape(2, grid, grid), shape(3 * capacity, size)),
        [read(capacity)], share * pass_flops, (fields, *chunks_in),
    )
    behind = lax.ppermute(state, AXES, route)
    field = call(
        functools.partial(radiate_kernel, capacity, 1), shape(2, grid, grid), hot(capacity),
        share * pass_flops + prop_flops, (field, state, *form),
    )
    out = call(
        fourth_kernel, shape(2, grid, grid), [read(capacity)] + hot(capacity),
        2 * share * pass_flops + prop_flops, (field, behind, *form),
    )
    return out[None]


def solution(mesh):
    return jax.shard_map(
        on_device,
        mesh=mesh,
        in_specs=(
            P(("cuts", "group"), None, None, None),
            P(("cuts", "group"), None, None),
            P(("cuts", "group"), None, None),
            P(("cuts", "group"), None, None),
            P(("cuts", "group"), None),
            P(),
            P(),
        ),
        out_specs=P(("cuts", "group"), None, None, None),
        check_vma=False,
    )
```

```python
import functools
import math

import jax
import jax.numpy as jnp
from jax import lax
from jax.experimental import pallas as pl
from jax.experimental.pallas import tpu as pltpu
from jax.sharding import PartitionSpec as P

KICK_RATE = 0.5
PHASE_RATE = 1.0
EMIT_RATE = 0.5

AXES = ("cuts", "group")
F32 = jnp.float32
BF16 = jnp.bfloat16
KINDS = 4
VMEM_LIMIT = 48 * 1024 * 1024


def dot(left, right, left_dim, right_dim):
    dims = (((left_dim,), (right_dim,)), ((), ()))
    return lax.dot_general(left, right, dims, preferred_element_type=F32)


def exact_dot(left, right):
    return jnp.dot(left, right, precision=lax.Precision.HIGHEST, preferred_element_type=F32)


def split(value):
    high = value.astype(BF16)
    return high, (value - high.astype(F32)).astype(BF16)


def real_form(propagator):
    prop_real, prop_imag = propagator[0], propagator[1]
    form = jnp.concatenate(
        [
            jnp.concatenate([prop_real, -prop_imag], axis=1),
            jnp.concatenate([prop_imag, prop_real], axis=1),
        ],
        axis=0,
    )
    return split(form)


def diffract(real, imag, form_high, form_low):
    size = real.shape[0]
    high, low = split(jnp.concatenate([real, imag], axis=1))
    both = dot(jnp.concatenate([high, low], axis=0), form_high, 1, 1)
    right = both[:size] + both[size:] + dot(high, form_low, 1, 1)
    high, low = split(jnp.concatenate([right[:, :size], right[:, size:]], axis=0))
    both = dot(form_high, jnp.concatenate([high, low], axis=1), 1, 0)
    out = both[:, :size] + both[:, size:] + dot(form_low, high, 1, 0)
    return out[:size], out[size:]


def cells(pixels, grid):
    half = grid // 2
    shift = grid.bit_length() - 1
    if grid == 1 << shift:
        row, col = lax.shift_right_arithmetic(pixels, shift), pixels & (grid - 1)
    else:
        row, col = pixels // grid, pixels % grid
    right = col >= half
    place = jnp.where(pixels < 0, -1, jnp.where(right, row + grid, row))
    return place, jnp.where(right, col - half, col)


def swapped(value):
    half = value.shape[1] // 2
    return jnp.concatenate([value[:, half:], value[:, :half]], axis=1)


def fold(first, second):
    left = lax.broadcasted_iota(jnp.int32, first.shape, 1) < first.shape[1] // 2
    return jnp.where(left, first, swapped(second)), jnp.where(left, swapped(first), second)


def chunks(blocks):
    width = 2 if blocks % 2 == 0 else 1
    return [(start, width) for start in range(0, blocks, width)]


def lanes(array, start, width):
    return jnp.concatenate([array[start + k : start + k + 1] for k in range(width)], axis=1)


def hits(ids, span):
    return lax.broadcasted_iota(jnp.int32, (span, ids.shape[1]), 0) == ids


def one_hot(place, start, width, span):
    ids = lanes(place, start, width).astype(F32)
    rows = lax.broadcasted_iota(jnp.int32, (span, ids.shape[1]), 0).astype(F32)
    if span <= 256:
        ids, rows = ids.astype(BF16), rows.astype(BF16)
    one, zero = jnp.ones((), BF16), jnp.zeros((), BF16)
    return jnp.where(rows == ids, one, zero)


def kick(real, imag, phases, energy, pixels, read_ref, hot_ref=None, dark=None):
    grid = real.shape[0]
    half = grid // 2
    blocks, size = phases.shape
    place, col = cells(pixels, grid)

    def read():
        upper, lower = fold(real, imag)
        low = jnp.concatenate([upper, lower], axis=0).astype(BF16)
        for start, width in chunks(blocks):
            hot = one_hot(place, start, width, 2 * grid)
            if hot_ref is not None:
                hot_ref[:, start * size : (start + width) * size] = hot
            picked = dot(low, hot, 0, 0)
            col_hit = hits(lanes(col, start, width), half)
            for part in range(2):
                value = picked[part * half : (part + 1) * half]
                value = jnp.sum(jnp.where(col_hit, value, 0.0), axis=0, keepdims=True)
                for k in range(width):
                    read_ref[part, start + k : start + k + 1, :] = value[:, k * size : (k + 1) * size]

    if dark is None:
        read()
    else:
        pl.when(jnp.logical_not(dark))(read)

        @pl.when(dark)
        def _():
            read_ref[...] = jnp.zeros(read_ref.shape, F32)
            for start, width in chunks(blocks):
                hot_ref[:, start * size : (start + width) * size] = one_hot(place, start, width, 2 * grid)

    read_real = read_ref[0, :blocks, :]
    read_imag = read_ref[1, :blocks, :]
    energy = energy - KICK_RATE * (read_real * jnp.cos(phases) - read_imag * jnp.sin(phases))
    return phases + PHASE_RATE * energy, energy


def emit(real, imag, phases, pixels, hot_ref, spread_ref, filled):
    grid = real.shape[0]
    half = grid // 2
    blocks, size = phases.shape
    place, col = cells(pixels, grid)
    weight_real = jnp.cos(phases)
    weight_imag = -jnp.sin(phases)
    for start, width in chunks(blocks):
        where = slice(start * size, (start + width) * size)
        if not filled:
            hot_ref[:, where] = one_hot(place, start, width, 2 * grid)
        col_hit = hits(lanes(col, start, width), half)
        for part, weight in ((0, weight_real), (1, weight_imag)):
            value = jnp.where(col_hit, lanes(weight, start, width), 0.0)
            spread_ref[part * half : (part + 1) * half, where] = value.astype(BF16)
    span = blocks * size
    source = dot(hot_ref[:, :span], spread_ref[:, :span], 1, 1)
    source_real, source_imag = fold(source[:grid], source[grid:])
    return real + EMIT_RATE * source_real, imag + EMIT_RATE * source_imag


def position():
    return lax.axis_index("cuts") * lax.axis_size("group") + lax.axis_index("group")


def kept_unless(index):
    return jnp.where(position() == index, 0.0, 1.0).astype(F32)


def kick_kernel(field_hbm, phases_hbm, energy_hbm, pixels_hbm, dest_hbm, out, field, phases, energy, pixels, dest, read_ref, sems):
    blocks, size = phases.shape
    pairs = ((field_hbm, field), (pixels_hbm, pixels), (phases_hbm, phases), (energy_hbm, energy), (dest_hbm, dest))
    copies = [pltpu.make_async_copy(source, target, sems.at[k]) for k, (source, target) in enumerate(pairs)]
    for copy in copies:
        copy.start()
    for copy in copies:
        copy.wait()
    new_phases, new_energy = kick(field[0], field[1], phases[...], energy[...], pixels[...], read_ref)
    out[0:blocks, :] = new_phases
    out[blocks : 2 * blocks, :] = new_energy
    out[2 * blocks : 3 * blocks, :] = pixels[...].astype(F32)
    square = (blocks, blocks)
    own = lax.broadcasted_iota(jnp.int32, square, 0) == lax.broadcasted_iota(jnp.int32, square, 1)
    goals = jnp.where(own, jnp.broadcast_to(dest[0:1, :].astype(F32), square), 0.0)
    out[3 * blocks : 4 * blocks, :] = jnp.broadcast_to(jnp.sum(goals, axis=1, keepdims=True), (blocks, size))


def by_destination(kinds):
    goals = kinds[-1]
    blocks = goals.shape[0]
    place = lax.broadcasted_iota(jnp.int32, goals.shape, 0)
    rank = jnp.zeros(goals.shape, jnp.int32)
    for block in range(blocks):
        goal = goals[block : block + 1]
        ahead = (goal < goals) | ((goal == goals) & (place > block))
        rank = rank + jnp.where(ahead, 1, 0)
    ordered = [jnp.zeros(kind.shape, F32) for kind in kinds]
    for block in range(blocks):
        here = rank[block : block + 1] == place
        ordered = [jnp.where(here, kind[block : block + 1], old) for kind, old in zip(kinds, ordered)]
    return ordered


def lane_groups(values, shifts):
    size = values[0].shape[1]
    group = lax.broadcasted_iota(jnp.int32, values[0].shape, 1) // (size // len(values))
    joined_up = None
    for k, (value, shift) in enumerate(zip(values, shifts)):
        if shift % size:
            value = pltpu.roll(value, shift % size, axis=1)
        joined_up = value if joined_up is None else jnp.where(group == k, value, joined_up)
    return joined_up


def radiate(blocks, dropped, field, state, form, out, hot_ref, spread_ref):
    pixels = state[2 * blocks : 3 * blocks, :].astype(jnp.int32)
    real, imag = emit(field[0], field[1], state[0:blocks, :], pixels, hot_ref, spread_ref, False)
    real, imag = diffract(real, imag, *form)
    keep = kept_unless(dropped)
    out[0] = real * keep
    out[1] = imag * keep


def first_radiate_kernel(blocks, dropped, field, state, propagator, *rest):
    *rest, hot_ref, spread_ref = rest
    if len(rest) > 3:
        *tables, out, high, low, matrix = rest
        matrix[...] = filter_matrix(*tables)
    else:
        out, high, low = rest
    form = real_form(propagator)
    high[...], low[...] = form
    radiate(blocks, dropped, field, state, form, out, hot_ref, spread_ref)


def third_radiate_kernel(blocks, field, state, high, low, out, hot_ref, spread_ref):
    needed = position() > 1

    @pl.when(needed)
    def _():
        radiate(blocks, 1, field, state, (high[...], low[...]), out, hot_ref, spread_ref)

    @pl.when(jnp.logical_not(needed))
    def _():
        out[...] = jnp.zeros(out.shape, F32)


def second_kernel(count, rows, cap, field, state, high, low, out, *rest):
    sends = rest[:-3]
    read_ref, hot_ref, spread_ref = rest[-3:]
    blocks, size = state.shape[0] // 4, state.shape[1]
    real, imag = field[0], field[1]
    grid = real.shape[0]
    pixels = state[2 * blocks : 3 * blocks, :].astype(jnp.int32)
    dark = position() == count - 1
    phases, energy = kick(
        real, imag, state[0:blocks, :], state[blocks : 2 * blocks, :], pixels, read_ref, hot_ref, dark
    )
    kinds = by_destination((phases, energy, state[2 * blocks : 3 * blocks, :], state[3 * blocks : 4 * blocks, :]))
    if rows:
        pairs, pieces = rows // 2, len(kinds)
        tiles = 2 * pairs + 1
        width = size // pieces
        for chunk in range(blocks // cap):
            parts = [kind[chunk * cap : (chunk + 1) * cap] for kind in kinds]
            for piece in range(pieces):
                row = lane_groups(parts, [(k - piece) * width for k in range(pieces)])
                out[pl.ds((piece * cap + 1) * tiles - 1, cap, stride=tiles), chunk, :] = row
    else:
        cuts = len(sends)
        cut = lax.div(lax.rem(position() + 1, count), count // cuts)
        for ahead, send in enumerate(sends):
            wanted = lax.rem(cut + ahead, cuts).astype(F32)
            chunk = [jnp.zeros((cap, size), F32)] * 2 + [jnp.full((cap, size), -1.0, F32)]
            for start in range(0, blocks, cap):
                goes = kinds[3][start : start + cap] == wanted
                chunk = [jnp.where(goes, kind[start : start + cap], old) for kind, old in zip(kinds, chunk)]
            for kind in range(3):
                send[kind * cap : (kind + 1) * cap, :] = chunk[kind]
    real, imag = emit(real, imag, phases, pixels, hot_ref, spread_ref, True)
    real, imag = diffract(real, imag, high[...], low[...])
    keep = kept_unless(count - 2)
    real, imag = real * keep, imag * keep
    if rows:
        for part in range(grid // rows):
            for pair in range(pairs):
                first = part * rows + 2 * pair
                out[part * tiles + pair] = real[first : first + 2]
                out[part * tiles + pairs + pair] = imag[first : first + 2]
    else:
        out[0] = real
        out[1] = imag


def filter_matrix(transmit, cos_out, sin_out, cos_in, sin_in):
    gain_real, gain_imag = transmit[0:1, :], transmit[1:2, :]
    cosine, sine = cos_out[...], sin_out[...]
    real = cosine * gain_real - sine * gain_imag
    imag = cosine * gain_imag + sine * gain_real
    full_real = exact_dot(real, cos_in[...]) + exact_dot(imag, sin_in[...])
    full_imag = exact_dot(imag, cos_in[...]) - exact_dot(real, sin_in[...])
    form = jnp.concatenate(
        [
            jnp.concatenate([full_real, -full_imag], axis=1),
            jnp.concatenate([full_imag, full_real], axis=1),
        ],
        axis=0,
    )
    high, low = split(form)
    return jnp.concatenate([high, high, low], axis=1)


def filter_kernel(cuts, chunk_count, matrix, data, out):
    count = out.shape[0] // 3
    rows, size = out.shape[1:]
    groups = count // cuts
    pairs = rows // 2
    tiles = 2 * pairs + 1
    stacked = jnp.concatenate(
        [
            jnp.concatenate(
                [data[pl.ds(part * pairs + j // 2, count, stride=tiles), j % 2, :] for part in range(2)], axis=0
            )
            for j in range(rows)
        ],
        axis=1,
    )
    high, low = split(stacked)
    result = dot(matrix[...], jnp.concatenate([high, low, high], axis=0), 1, 0)
    for part in range(2):
        for j in range(rows):
            out[pl.ds(part, count, stride=3), j, :] = result[
                part * count : (part + 1) * count, j * size : (j + 1) * size
            ]
    bundles = [
        pltpu.roll(data[pl.ds(tiles - 1, count, stride=tiles), chunk, :], 1, axis=0)
        for chunk in range(chunk_count)
    ]
    goals = [bundle[:, size - 1 : size] for bundle in bundles]
    for cut in range(cuts):
        chosen = bundles[0]
        for bundle, goal in zip(bundles[1:], goals[1:]):
            chosen = jnp.where(goal == float(cut), bundle, chosen)
        first = cut * groups + 2
        fits = min(groups, count - first)
        for source in range(cuts):
            tile = chosen[source * groups : (source + 1) * groups]
            out[pl.ds(3 * first + 2, fits, stride=3), source, :] = tile[:fits]
            for k in range(fits, groups):
                out[3 * (first + k - count) + 2, source : source + 1, :] = tile[k : k + 1]


def joined(chunks_in):
    cap = chunks_in[0].shape[0] // 3
    kinds = [
        jnp.concatenate([chunk[kind * cap : (kind + 1) * cap, :] for chunk in chunks_in], axis=0)
        for kind in range(3)
    ]
    return kinds[0], kinds[1], kinds[2].astype(jnp.int32)


def relayed(fields, cuts):
    count = fields.shape[0] // 3
    size = fields.shape[2]
    width = size // KINDS
    bundles = [fields[pl.ds(2, count, stride=3), cut, :] for cut in range(cuts)]
    kinds = [lane_groups(bundles, [(cut - kind) * width for cut in range(cuts)]) for kind in range(KINDS)]
    wanted = lax.div(lax.rem(position() + (count - 2), count), count // cuts).astype(F32)
    return kinds[0], kinds[1], jnp.where(kinds[3] == wanted, kinds[2], -1.0).astype(jnp.int32)


def third_kernel(cuts, fields, *rest):
    out, state, read_ref = rest[-3:]
    chunks_in = rest[:-3]
    if chunks_in:
        phases, energy, pixels = joined(chunks_in)
        out[...] = fields[...]
    else:
        phases, energy, pixels = relayed(fields, cuts)
        rows = fields.shape[1]
        for part in range(fields.shape[0] // 3):
            for kind in range(2):
                out[kind, part * rows : (part + 1) * rows, :] = fields[3 * part + kind]
    phases, energy = kick(out[0], out[1], phases, energy, pixels, read_ref)
    blocks = phases.shape[0]
    state[0:blocks, :] = phases
    state[blocks : 2 * blocks, :] = energy
    state[2 * blocks : 3 * blocks, :] = pixels.astype(F32)


def fourth_kernel(field, state, high, low, out, read_ref, hot_ref, spread_ref):
    blocks = state.shape[0] // 3
    needed = position() > 0

    @pl.when(needed)
    def _():
        pixels = state[2 * blocks : 3 * blocks, :].astype(jnp.int32)
        real, imag = field[0], field[1]
        phases, _ = kick(
            real, imag, state[0:blocks, :], state[blocks : 2 * blocks, :], pixels, read_ref, hot_ref
        )
        real, imag = emit(real, imag, phases, pixels, hot_ref, spread_ref, True)
        out[0], out[1] = diffract(real, imag, high[...], low[...])

    @pl.when(jnp.logical_not(needed))
    def _():
        out[...] = jnp.zeros(out.shape, F32)


def call(kernel, out_shape, scratch, flops, args, memory=pltpu.VMEM):
    specs = [pl.BlockSpec(memory_space=memory)] * len(args)
    return pl.pallas_call(
        kernel,
        out_shape=out_shape,
        in_specs=specs,
        out_specs=jax.tree.map(lambda _: pl.BlockSpec(memory_space=pltpu.VMEM), out_shape),
        scratch_shapes=scratch,
        compiler_params=pltpu.CompilerParams(vmem_limit_bytes=VMEM_LIMIT),
        cost_estimate=pl.CostEstimate(flops=flops, bytes_accessed=1 << 19, transcendentals=0),
    )(*args)


def time_tables(count):
    times = jnp.arange(count, dtype=jnp.int32)
    cos_out, sin_out = angle_table((times + (count - 4)) % count, times, count)
    return (cos_out / count, sin_out / count, *angle_table(times, times, count))


def angle_table(first_ids, second_ids, total_slices):
    product = first_ids[:, None] * second_ids[None, :] % total_slices
    angle = product.astype(F32) * (2.0 * math.pi / total_slices)
    return jnp.cos(angle), jnp.sin(angle)


def filter_any(field, transmit, count):
    grid = field.shape[1]
    span = grid * grid
    share = -(-span // count)
    flat = jnp.pad(field.reshape(2, span), ((0, 0), (0, share * count - span)))
    parts = flat.reshape(2, count, share).transpose(1, 0, 2)
    got = lax.all_to_all(parts, AXES, split_axis=0, concat_axis=0, tiled=True)
    got = jnp.roll(got, 2, axis=0)
    real, imag = got[:, 0], got[:, 1]
    times = jnp.arange(count, dtype=jnp.int32)
    cosine, sine = angle_table(times, times, count)
    spec_real = exact_dot(cosine, real) + exact_dot(sine, imag)
    spec_imag = exact_dot(cosine, imag) - exact_dot(sine, real)
    gain_real, gain_imag = transmit[0][:, None], transmit[1][:, None]
    shaped_real = gain_real * spec_real - gain_imag * spec_imag
    shaped_imag = gain_real * spec_imag + gain_imag * spec_real
    back_real = (exact_dot(cosine, shaped_real) - exact_dot(sine, shaped_imag)) / count
    back_imag = (exact_dot(cosine, shaped_imag) + exact_dot(sine, shaped_real)) / count
    back = jnp.stack([back_real, back_imag], axis=1)
    sent = jnp.roll(back, 2, axis=0)
    fields = lax.all_to_all(sent, AXES, split_axis=0, concat_axis=0, tiled=True)
    fields = fields.transpose(1, 0, 2).reshape(2, share * count)[:, :span]
    return fields.reshape(2, grid, grid)


def on_device(radiation, phases, energy, pixels, destination, propagator, transmit):
    cuts, groups = lax.axis_size("cuts"), lax.axis_size("group")
    count = cuts * groups
    grid = radiation.shape[-1]
    blocks, size = phases.shape[1:]
    cap = max(2, 2 * blocks // cuts)
    rows = grid // count if grid % count == 0 else 0
    if rows != 4 or cap * KINDS != count or cuts != KINDS or size % 128 or blocks != 2 * cap or groups % 8:
        rows = 0
    field = radiation[0]
    shape = lambda *dims: jax.ShapeDtypeStruct(dims, F32)
    read = lambda number: pltpu.VMEM((2, number, size), F32)
    hot = lambda number: [pltpu.VMEM((2 * grid, number * size), BF16), pltpu.VMEM((grid, number * size), BF16)]
    pass_flops = 4 * blocks * size * grid * grid
    prop_flops = 48 * grid**3

    given = (field, phases[0], energy[0], pixels[0], destination)
    state = call(
        kick_kernel, shape(4 * blocks, size),
        [
            pltpu.VMEM((2, grid, grid), F32),
            pltpu.VMEM((blocks, size), F32),
            pltpu.VMEM((blocks, size), F32),
            pltpu.VMEM((blocks, size), jnp.int32),
            pltpu.VMEM((1, blocks), jnp.int32),
            read(blocks),
            pltpu.SemaphoreType.DMA((5,)),
        ],
        pass_flops, tuple(pltpu.with_memory_space_constraint(value, pltpu.HBM) for value in given), pl.ANY,
    )
    route = [((i + 1) % count, i) for i in range(count)]
    behind = lax.ppermute(state, AXES, route)
    form_shape = jax.ShapeDtypeStruct((2 * grid, 2 * grid), BF16)
    made = [shape(2, grid, grid), form_shape, form_shape]
    tables = ()
    if rows:
        made.append(jax.ShapeDtypeStruct((2 * count, 6 * count), BF16))
        tables = (transmit, *time_tables(count))
    field, *form = call(
        functools.partial(first_radiate_kernel, blocks, count - 1), made, hot(blocks), pass_flops + prop_flops,
        (field, state, propagator, *tables),
    )
    matrix = form[2:]
    form = form[:2]
    part_shape = shape(count * (rows + 1), 2, grid) if rows else shape(2, grid, grid)
    send_shapes = [] if rows else [shape(3 * cap, size)] * cuts
    field, *sends = call(
        functools.partial(second_kernel, count, rows, cap), (part_shape, *send_shapes),
        [read(blocks)] + hot(blocks), 2 * pass_flops + prop_flops,
        (field, behind, *form),
    )
    chunks_in = [
        lax.ppermute(send, AXES, [(i, (i + 3 + groups * ahead) % count) for i in range(count)])
        for ahead, send in enumerate(sends)
    ]
    if rows:
        data = lax.all_to_all(field, AXES, split_axis=0, concat_axis=0, tiled=True)
        sent = call(
            functools.partial(filter_kernel, cuts, blocks // cap), shape(count * 3, rows, grid), [], 1 << 24,
            (*matrix, data),
        )
        fields = lax.all_to_all(sent, AXES, split_axis=0, concat_axis=0, tiled=True)
    else:
        fields = filter_any(field, transmit, count)
    capacity = cuts * cap
    share = capacity // blocks
    field, state = call(
        functools.partial(third_kernel, cuts), (shape(2, grid, grid), shape(3 * capacity, size)),
        [read(capacity)], share * pass_flops, (fields, *chunks_in),
    )
    behind = lax.ppermute(state, AXES, route)
    field = call(
        functools.partial(third_radiate_kernel, capacity), shape(2, grid, grid), hot(capacity),
        share * pass_flops + prop_flops, (field, state, *form),
    )
    out = call(
        fourth_kernel, shape(2, grid, grid), [read(capacity)] + hot(capacity),
        2 * share * pass_flops + prop_flops, (field, behind, *form),
    )
    return out[None]


def solution(mesh):
    return jax.shard_map(
        on_device,
        mesh=mesh,
        in_specs=(
            P(("cuts", "group"), None, None, None),
            P(("cuts", "group"), None, None),
            P(("cuts", "group"), None, None),
            P(("cuts", "group"), None, None),
            P(("cuts", "group"), None),
            P(),
            P(),
        ),
        out_specs=P(("cuts", "group"), None, None, None),
        check_vma=False,
    )
```

```python
import functools
import math

import jax
import jax.numpy as jnp
from jax import lax
from jax.experimental import pallas as pl
from jax.experimental.pallas import tpu as pltpu
from jax.sharding import PartitionSpec as P

KICK_RATE = 0.5
PHASE_RATE = 1.0
EMIT_RATE = 0.5

AXES = ("cuts", "group")
F32 = jnp.float32
BF16 = jnp.bfloat16
KINDS = 4
VMEM_LIMIT = 48 * 1024 * 1024


def dot(left, right, left_dim, right_dim):
    dims = (((left_dim,), (right_dim,)), ((), ()))
    return lax.dot_general(left, right, dims, preferred_element_type=F32)


def exact_dot(left, right):
    return jnp.dot(left, right, precision=lax.Precision.HIGHEST, preferred_element_type=F32)


def split(value):
    high = value.astype(BF16)
    return high, (value - high.astype(F32)).astype(BF16)


def real_form(propagator):
    prop_real, prop_imag = propagator[0], propagator[1]
    form = jnp.concatenate(
        [
            jnp.concatenate([prop_real, -prop_imag], axis=1),
            jnp.concatenate([prop_imag, prop_real], axis=1),
        ],
        axis=0,
    )
    return split(form)


def diffract(real, imag, form_high, form_low):
    size = real.shape[0]
    high, low = split(jnp.concatenate([real, imag], axis=1))
    both = dot(jnp.concatenate([high, low], axis=0), form_high, 1, 1)
    right = both[:size] + both[size:] + dot(high, form_low, 1, 1)
    high, low = split(jnp.concatenate([right[:, :size], right[:, size:]], axis=0))
    both = dot(form_high, jnp.concatenate([high, low], axis=1), 1, 0)
    out = both[:, :size] + both[:, size:] + dot(form_low, high, 1, 0)
    return out[:size], out[size:]


def cells(pixels, grid):
    half = grid // 2
    shift = grid.bit_length() - 1
    if grid == 1 << shift:
        row, col = lax.shift_right_arithmetic(pixels, shift), pixels & (grid - 1)
    else:
        row, col = pixels // grid, pixels % grid
    right = col >= half
    place = jnp.where(pixels < 0, -1, jnp.where(right, row + grid, row))
    return place, jnp.where(right, col - half, col)


def swapped(value):
    half = value.shape[1] // 2
    return jnp.concatenate([value[:, half:], value[:, :half]], axis=1)


def fold(first, second):
    left = lax.broadcasted_iota(jnp.int32, first.shape, 1) < first.shape[1] // 2
    return jnp.where(left, first, swapped(second)), jnp.where(left, swapped(first), second)


def chunks(blocks):
    width = 2 if blocks % 2 == 0 else 1
    return [(start, width) for start in range(0, blocks, width)]


def lanes(array, start, width):
    return jnp.concatenate([array[start + k : start + k + 1] for k in range(width)], axis=1)


def hits(ids, span):
    return lax.broadcasted_iota(jnp.int32, (span, ids.shape[1]), 0) == ids


def one_hot(place, start, width, span):
    ids = lanes(place, start, width).astype(F32)
    rows = lax.broadcasted_iota(jnp.int32, (span, ids.shape[1]), 0).astype(F32)
    if span <= 256:
        ids, rows = ids.astype(BF16), rows.astype(BF16)
    one, zero = jnp.ones((), BF16), jnp.zeros((), BF16)
    return jnp.where(rows == ids, one, zero)


def kick(real, imag, phases, energy, pixels, read_ref, hot_ref=None, dark=None):
    grid = real.shape[0]
    half = grid // 2
    blocks, size = phases.shape
    place, col = cells(pixels, grid)

    def read():
        upper, lower = fold(real, imag)
        low = jnp.concatenate([upper, lower], axis=0).astype(BF16)
        for start, width in chunks(blocks):
            hot = one_hot(place, start, width, 2 * grid)
            if hot_ref is not None:
                hot_ref[:, start * size : (start + width) * size] = hot
            picked = dot(low, hot, 0, 0)
            col_hit = hits(lanes(col, start, width), half)
            for part in range(2):
                value = picked[part * half : (part + 1) * half]
                value = jnp.sum(jnp.where(col_hit, value, 0.0), axis=0, keepdims=True)
                for k in range(width):
                    read_ref[part, start + k : start + k + 1, :] = value[:, k * size : (k + 1) * size]

    if dark is None:
        read()
    else:
        pl.when(jnp.logical_not(dark))(read)

        @pl.when(dark)
        def _():
            read_ref[...] = jnp.zeros(read_ref.shape, F32)
            for start, width in chunks(blocks):
                hot_ref[:, start * size : (start + width) * size] = one_hot(place, start, width, 2 * grid)

    read_real = read_ref[0, :blocks, :]
    read_imag = read_ref[1, :blocks, :]
    energy = energy - KICK_RATE * (read_real * jnp.cos(phases) - read_imag * jnp.sin(phases))
    return phases + PHASE_RATE * energy, energy


def emit(real, imag, phases, pixels, hot_ref, spread_ref, filled):
    grid = real.shape[0]
    half = grid // 2
    blocks, size = phases.shape
    place, col = cells(pixels, grid)
    weight_real = jnp.cos(phases)
    weight_imag = -jnp.sin(phases)
    for start, width in chunks(blocks):
        where = slice(start * size, (start + width) * size)
        if not filled:
            hot_ref[:, where] = one_hot(place, start, width, 2 * grid)
        col_hit = hits(lanes(col, start, width), half)
        for part, weight in ((0, weight_real), (1, weight_imag)):
            value = jnp.where(col_hit, lanes(weight, start, width), 0.0)
            spread_ref[part * half : (part + 1) * half, where] = value.astype(BF16)
    span = blocks * size
    source = dot(spread_ref[:, :span], hot_ref[:, :span], 1, 1).T
    source_real, source_imag = fold(source[:grid], source[grid:])
    return real + EMIT_RATE * source_real, imag + EMIT_RATE * source_imag


def position():
    return lax.axis_index("cuts") * lax.axis_size("group") + lax.axis_index("group")


def kept_unless(index):
    return jnp.where(position() == index, 0.0, 1.0).astype(F32)


def kick_kernel(field_hbm, phases_hbm, energy_hbm, pixels_hbm, dest_hbm, out, field, phases, energy, pixels, dest, read_ref, sems):
    blocks, size = phases.shape
    pairs = ((field_hbm, field), (pixels_hbm, pixels), (phases_hbm, phases), (energy_hbm, energy), (dest_hbm, dest))
    copies = [pltpu.make_async_copy(source, target, sems.at[k]) for k, (source, target) in enumerate(pairs)]
    for copy in copies:
        copy.start()
    for copy in copies:
        copy.wait()
    new_phases, new_energy = kick(field[0], field[1], phases[...], energy[...], pixels[...], read_ref)
    out[0:blocks, :] = new_phases
    out[blocks : 2 * blocks, :] = new_energy
    out[2 * blocks : 3 * blocks, :] = pixels[...].astype(F32)
    square = (blocks, blocks)
    own = lax.broadcasted_iota(jnp.int32, square, 0) == lax.broadcasted_iota(jnp.int32, square, 1)
    goals = jnp.where(own, jnp.broadcast_to(dest[0:1, :].astype(F32), square), 0.0)
    out[3 * blocks : 4 * blocks, :] = jnp.broadcast_to(jnp.sum(goals, axis=1, keepdims=True), (blocks, size))


def by_destination(kinds):
    goals = kinds[-1]
    blocks = goals.shape[0]
    place = lax.broadcasted_iota(jnp.int32, goals.shape, 0)
    rank = jnp.zeros(goals.shape, jnp.int32)
    for block in range(blocks):
        goal = goals[block : block + 1]
        ahead = (goal < goals) | ((goal == goals) & (place > block))
        rank = rank + jnp.where(ahead, 1, 0)
    ordered = [jnp.zeros(kind.shape, F32) for kind in kinds]
    for block in range(blocks):
        here = rank[block : block + 1] == place
        ordered = [jnp.where(here, kind[block : block + 1], old) for kind, old in zip(kinds, ordered)]
    return ordered


def lane_groups(values, shifts):
    size = values[0].shape[1]
    group = lax.broadcasted_iota(jnp.int32, values[0].shape, 1) // (size // len(values))
    joined_up = None
    for k, (value, shift) in enumerate(zip(values, shifts)):
        if shift % size:
            value = pltpu.roll(value, shift % size, axis=1)
        joined_up = value if joined_up is None else jnp.where(group == k, value, joined_up)
    return joined_up


def radiate(blocks, dropped, field, state, form, out, hot_ref, spread_ref):
    pixels = state[2 * blocks : 3 * blocks, :].astype(jnp.int32)
    real, imag = emit(field[0], field[1], state[0:blocks, :], pixels, hot_ref, spread_ref, False)
    real, imag = diffract(real, imag, *form)
    keep = kept_unless(dropped)
    out[0] = real * keep
    out[1] = imag * keep


def first_radiate_kernel(blocks, dropped, field, state, propagator, *rest):
    *rest, hot_ref, spread_ref = rest
    if len(rest) > 3:
        *tables, out, high, low, matrix = rest
        matrix[...] = filter_matrix(*tables)
    else:
        out, high, low = rest
    form = real_form(propagator)
    high[...], low[...] = form
    radiate(blocks, dropped, field, state, form, out, hot_ref, spread_ref)


def third_radiate_kernel(blocks, field, state, high, low, out, hot_ref, spread_ref):
    needed = position() > 1

    @pl.when(needed)
    def _():
        radiate(blocks, 1, field, state, (high[...], low[...]), out, hot_ref, spread_ref)

    @pl.when(jnp.logical_not(needed))
    def _():
        out[...] = jnp.zeros(out.shape, F32)


def second_kernel(count, rows, cap, field, state, high, low, out, *rest):
    sends = rest[:-3]
    read_ref, hot_ref, spread_ref = rest[-3:]
    blocks, size = state.shape[0] // 4, state.shape[1]
    real, imag = field[0], field[1]
    grid = real.shape[0]
    pixels = state[2 * blocks : 3 * blocks, :].astype(jnp.int32)
    dark = position() == count - 1
    phases, energy = kick(
        real, imag, state[0:blocks, :], state[blocks : 2 * blocks, :], pixels, read_ref, hot_ref, dark
    )
    kinds = by_destination((phases, energy, state[2 * blocks : 3 * blocks, :], state[3 * blocks : 4 * blocks, :]))
    if rows:
        pairs, pieces = rows // 2, len(kinds)
        tiles = 2 * pairs + 1
        width = size // pieces
        for chunk in range(blocks // cap):
            parts = [kind[chunk * cap : (chunk + 1) * cap] for kind in kinds]
            for piece in range(pieces):
                row = lane_groups(parts, [(k - piece) * width for k in range(pieces)])
                out[pl.ds((piece * cap + 1) * tiles - 1, cap, stride=tiles), chunk, :] = row
    else:
        cuts = len(sends)
        cut = lax.div(lax.rem(position() + 1, count), count // cuts)
        for ahead, send in enumerate(sends):
            wanted = lax.rem(cut + ahead, cuts).astype(F32)
            chunk = [jnp.zeros((cap, size), F32)] * 2 + [jnp.full((cap, size), -1.0, F32)]
            for start in range(0, blocks, cap):
                goes = kinds[3][start : start + cap] == wanted
                chunk = [jnp.where(goes, kind[start : start + cap], old) for kind, old in zip(kinds, chunk)]
            for kind in range(3):
                send[kind * cap : (kind + 1) * cap, :] = chunk[kind]
    real, imag = emit(real, imag, phases, pixels, hot_ref, spread_ref, True)
    real, imag = diffract(real, imag, high[...], low[...])
    keep = kept_unless(count - 2)
    real, imag = real * keep, imag * keep
    if rows:
        for part in range(grid // rows):
            for pair in range(pairs):
                first = part * rows + 2 * pair
                out[part * tiles + pair] = real[first : first + 2]
                out[part * tiles + pairs + pair] = imag[first : first + 2]
    else:
        out[0] = real
        out[1] = imag


def filter_matrix(transmit, cos_out, sin_out, cos_in, sin_in):
    gain_real, gain_imag = transmit[0:1, :], transmit[1:2, :]
    cosine, sine = cos_out[...], sin_out[...]
    real = cosine * gain_real - sine * gain_imag
    imag = cosine * gain_imag + sine * gain_real
    full_real = exact_dot(real, cos_in[...]) + exact_dot(imag, sin_in[...])
    full_imag = exact_dot(imag, cos_in[...]) - exact_dot(real, sin_in[...])
    form = jnp.concatenate(
        [
            jnp.concatenate([full_real, -full_imag], axis=1),
            jnp.concatenate([full_imag, full_real], axis=1),
        ],
        axis=0,
    )
    high, low = split(form)
    return jnp.concatenate([high, high, low], axis=1)


def filter_kernel(cuts, chunk_count, matrix, data, out):
    count = out.shape[0] // 3
    rows, size = out.shape[1:]
    groups = count // cuts
    pairs = rows // 2
    tiles = 2 * pairs + 1
    stacked = jnp.concatenate(
        [
            jnp.concatenate(
                [data[pl.ds(part * pairs + j // 2, count, stride=tiles), j % 2, :] for part in range(2)], axis=0
            )
            for j in range(rows)
        ],
        axis=1,
    )
    high, low = split(stacked)
    result = dot(matrix[...], jnp.concatenate([high, low, high], axis=0), 1, 0)
    for part in range(2):
        for j in range(rows):
            out[pl.ds(part, count, stride=3), j, :] = result[
                part * count : (part + 1) * count, j * size : (j + 1) * size
            ]
    bundles = [
        pltpu.roll(data[pl.ds(tiles - 1, count, stride=tiles), chunk, :], 1, axis=0)
        for chunk in range(chunk_count)
    ]
    goals = [bundle[:, size - 1 : size] for bundle in bundles]
    for cut in range(cuts):
        chosen = bundles[0]
        for bundle, goal in zip(bundles[1:], goals[1:]):
            chosen = jnp.where(goal == float(cut), bundle, chosen)
        first = cut * groups + 2
        fits = min(groups, count - first)
        for source in range(cuts):
            tile = chosen[source * groups : (source + 1) * groups]
            out[pl.ds(3 * first + 2, fits, stride=3), source, :] = tile[:fits]
            for k in range(fits, groups):
                out[3 * (first + k - count) + 2, source : source + 1, :] = tile[k : k + 1]


def joined(chunks_in):
    cap = chunks_in[0].shape[0] // 3
    kinds = [
        jnp.concatenate([chunk[kind * cap : (kind + 1) * cap, :] for chunk in chunks_in], axis=0)
        for kind in range(3)
    ]
    return kinds[0], kinds[1], kinds[2].astype(jnp.int32)


def relayed(fields, cuts):
    count = fields.shape[0] // 3
    size = fields.shape[2]
    width = size // KINDS
    bundles = [fields[pl.ds(2, count, stride=3), cut, :] for cut in range(cuts)]
    kinds = [lane_groups(bundles, [(cut - kind) * width for cut in range(cuts)]) for kind in range(KINDS)]
    wanted = lax.div(lax.rem(position() + (count - 2), count), count // cuts).astype(F32)
    return kinds[0], kinds[1], jnp.where(kinds[3] == wanted, kinds[2], -1.0).astype(jnp.int32)


def third_kernel(cuts, fields, *rest):
    out, state, read_ref = rest[-3:]
    chunks_in = rest[:-3]
    if chunks_in:
        phases, energy, pixels = joined(chunks_in)
        out[...] = fields[...]
    else:
        phases, energy, pixels = relayed(fields, cuts)
        rows = fields.shape[1]
        for part in range(fields.shape[0] // 3):
            for kind in range(2):
                out[kind, part * rows : (part + 1) * rows, :] = fields[3 * part + kind]
    phases, energy = kick(out[0], out[1], phases, energy, pixels, read_ref)
    blocks = phases.shape[0]
    state[0:blocks, :] = phases
    state[blocks : 2 * blocks, :] = energy
    state[2 * blocks : 3 * blocks, :] = pixels.astype(F32)


def fourth_kernel(field, state, high, low, out, read_ref, hot_ref, spread_ref):
    blocks = state.shape[0] // 3
    needed = position() > 0

    @pl.when(needed)
    def _():
        pixels = state[2 * blocks : 3 * blocks, :].astype(jnp.int32)
        real, imag = field[0], field[1]
        dark = position() == 1
        phases, _ = kick(
            real, imag, state[0:blocks, :], state[blocks : 2 * blocks, :], pixels, read_ref, hot_ref, dark
        )
        real, imag = emit(real, imag, phases, pixels, hot_ref, spread_ref, True)
        out[0], out[1] = diffract(real, imag, high[...], low[...])

    @pl.when(jnp.logical_not(needed))
    def _():
        out[...] = jnp.zeros(out.shape, F32)


def call(kernel, out_shape, scratch, flops, args, memory=pltpu.VMEM):
    specs = [pl.BlockSpec(memory_space=memory)] * len(args)
    return pl.pallas_call(
        kernel,
        out_shape=out_shape,
        in_specs=specs,
        out_specs=jax.tree.map(lambda _: pl.BlockSpec(memory_space=pltpu.VMEM), out_shape),
        scratch_shapes=scratch,
        compiler_params=pltpu.CompilerParams(vmem_limit_bytes=VMEM_LIMIT),
        cost_estimate=pl.CostEstimate(flops=flops, bytes_accessed=1 << 19, transcendentals=0),
    )(*args)


def time_tables(count):
    times = jnp.arange(count, dtype=jnp.int32)
    cos_out, sin_out = angle_table((times + (count - 4)) % count, times, count)
    return (cos_out / count, sin_out / count, *angle_table(times, times, count))


def angle_table(first_ids, second_ids, total_slices):
    product = first_ids[:, None] * second_ids[None, :] % total_slices
    angle = product.astype(F32) * (2.0 * math.pi / total_slices)
    return jnp.cos(angle), jnp.sin(angle)


def filter_any(field, transmit, count):
    grid = field.shape[1]
    span = grid * grid
    share = -(-span // count)
    flat = jnp.pad(field.reshape(2, span), ((0, 0), (0, share * count - span)))
    parts = flat.reshape(2, count, share).transpose(1, 0, 2)
    got = lax.all_to_all(parts, AXES, split_axis=0, concat_axis=0, tiled=True)
    got = jnp.roll(got, 2, axis=0)
    real, imag = got[:, 0], got[:, 1]
    times = jnp.arange(count, dtype=jnp.int32)
    cosine, sine = angle_table(times, times, count)
    spec_real = exact_dot(cosine, real) + exact_dot(sine, imag)
    spec_imag = exact_dot(cosine, imag) - exact_dot(sine, real)
    gain_real, gain_imag = transmit[0][:, None], transmit[1][:, None]
    shaped_real = gain_real * spec_real - gain_imag * spec_imag
    shaped_imag = gain_real * spec_imag + gain_imag * spec_real
    back_real = (exact_dot(cosine, shaped_real) - exact_dot(sine, shaped_imag)) / count
    back_imag = (exact_dot(cosine, shaped_imag) + exact_dot(sine, shaped_real)) / count
    back = jnp.stack([back_real, back_imag], axis=1)
    sent = jnp.roll(back, 2, axis=0)
    fields = lax.all_to_all(sent, AXES, split_axis=0, concat_axis=0, tiled=True)
    fields = fields.transpose(1, 0, 2).reshape(2, share * count)[:, :span]
    return fields.reshape(2, grid, grid)


def on_device(radiation, phases, energy, pixels, destination, propagator, transmit):
    cuts, groups = lax.axis_size("cuts"), lax.axis_size("group")
    count = cuts * groups
    grid = radiation.shape[-1]
    blocks, size = phases.shape[1:]
    cap = max(2, 2 * blocks // cuts)
    rows = grid // count if grid % count == 0 else 0
    if rows != 4 or cap * KINDS != count or cuts != KINDS or size % 128 or blocks != 2 * cap or groups % 8:
        rows = 0
    field = radiation[0]
    shape = lambda *dims: jax.ShapeDtypeStruct(dims, F32)
    read = lambda number: pltpu.VMEM((2, number, size), F32)
    hot = lambda number: [pltpu.VMEM((2 * grid, number * size), BF16), pltpu.VMEM((grid, number * size), BF16)]
    pass_flops = 4 * blocks * size * grid * grid
    prop_flops = 48 * grid**3

    given = (field, phases[0], energy[0], pixels[0], destination)
    state = call(
        kick_kernel, shape(4 * blocks, size),
        [
            pltpu.VMEM((2, grid, grid), F32),
            pltpu.VMEM((blocks, size), F32),
            pltpu.VMEM((blocks, size), F32),
            pltpu.VMEM((blocks, size), jnp.int32),
            pltpu.VMEM((1, blocks), jnp.int32),
            read(blocks),
            pltpu.SemaphoreType.DMA((5,)),
        ],
        pass_flops, tuple(pltpu.with_memory_space_constraint(value, pltpu.HBM) for value in given), pl.ANY,
    )
    route = [((i + 1) % count, i) for i in range(count)]
    behind = lax.ppermute(state, AXES, route)
    form_shape = jax.ShapeDtypeStruct((2 * grid, 2 * grid), BF16)
    made = [shape(2, grid, grid), form_shape, form_shape]
    tables = ()
    if rows:
        made.append(jax.ShapeDtypeStruct((2 * count, 6 * count), BF16))
        tables = (transmit, *time_tables(count))
    field, *form = call(
        functools.partial(first_radiate_kernel, blocks, count - 1), made, hot(blocks), pass_flops + prop_flops,
        (field, state, propagator, *tables),
    )
    matrix = form[2:]
    form = form[:2]
    part_shape = shape(count * (rows + 1), 2, grid) if rows else shape(2, grid, grid)
    send_shapes = [] if rows else [shape(3 * cap, size)] * cuts
    field, *sends = call(
        functools.partial(second_kernel, count, rows, cap), (part_shape, *send_shapes),
        [read(blocks)] + hot(blocks), 2 * pass_flops + prop_flops,
        (field, behind, *form),
    )
    chunks_in = [
        lax.ppermute(send, AXES, [(i, (i + 3 + groups * ahead) % count) for i in range(count)])
        for ahead, send in enumerate(sends)
    ]
    if rows:
        data = lax.all_to_all(field, AXES, split_axis=0, concat_axis=0, tiled=True)
        sent = call(
            functools.partial(filter_kernel, cuts, blocks // cap), shape(count * 3, rows, grid), [], 1 << 24,
            (*matrix, data),
        )
        fields = lax.all_to_all(sent, AXES, split_axis=0, concat_axis=0, tiled=True)
    else:
        fields = filter_any(field, transmit, count)
    capacity = cuts * cap
    share = capacity // blocks
    field, state = call(
        functools.partial(third_kernel, cuts), (shape(2, grid, grid), shape(3 * capacity, size)),
        [read(capacity)], share * pass_flops, (fields, *chunks_in),
    )
    behind = lax.ppermute(state, AXES, route)
    field = call(
        functools.partial(third_radiate_kernel, capacity), shape(2, grid, grid), hot(capacity),
        share * pass_flops + prop_flops, (field, state, *form),
    )
    out = call(
        fourth_kernel, shape(2, grid, grid), [read(capacity)] + hot(capacity),
        2 * share * pass_flops + prop_flops, (field, behind, *form),
    )
    return out[None]


def solution(mesh):
    return jax.shard_map(
        on_device,
        mesh=mesh,
        in_specs=(
            P(("cuts", "group"), None, None, None),
            P(("cuts", "group"), None, None),
            P(("cuts", "group"), None, None),
            P(("cuts", "group"), None, None),
            P(("cuts", "group"), None),
            P(),
            P(),
        ),
        out_specs=P(("cuts", "group"), None, None, None),
        check_vma=False,
    )
```

```python
import functools
import math

import jax
import jax.numpy as jnp
from jax import lax
from jax.experimental import pallas as pl
from jax.experimental.pallas import tpu as pltpu
from jax.sharding import PartitionSpec as P

KICK_RATE = 0.5
PHASE_RATE = 1.0
EMIT_RATE = 0.5

AXES = ("cuts", "group")
F32 = jnp.float32
BF16 = jnp.bfloat16
KINDS = 4
VMEM_LIMIT = 48 * 1024 * 1024


def dot(left, right, left_dim, right_dim):
    dims = (((left_dim,), (right_dim,)), ((), ()))
    return lax.dot_general(left, right, dims, preferred_element_type=F32)


def exact_dot(left, right):
    return jnp.dot(left, right, precision=lax.Precision.HIGHEST, preferred_element_type=F32)


def split(value):
    high = value.astype(BF16)
    return high, (value - high.astype(F32)).astype(BF16)


def real_form(propagator):
    prop_real, prop_imag = propagator[0], propagator[1]
    form = jnp.concatenate(
        [
            jnp.concatenate([prop_real, -prop_imag], axis=1),
            jnp.concatenate([prop_imag, prop_real], axis=1),
        ],
        axis=0,
    )
    return split(form)


def diffract(real, imag, form_high, form_low):
    size = real.shape[0]
    high, low = split(jnp.concatenate([real, imag], axis=1))
    both = dot(jnp.concatenate([high, low], axis=0), form_high, 1, 1)
    right = both[:size] + both[size:] + dot(high, form_low, 1, 1)
    high, low = split(jnp.concatenate([right[:, :size], right[:, size:]], axis=0))
    both = dot(form_high, jnp.concatenate([high, low], axis=1), 1, 0)
    out = both[:, :size] + both[:, size:] + dot(form_low, high, 1, 0)
    return out[:size], out[size:]


def cells(pixels, grid):
    half = grid // 2
    shift = grid.bit_length() - 1
    if grid == 1 << shift:
        row, col = lax.shift_right_arithmetic(pixels, shift), pixels & (grid - 1)
    else:
        row, col = pixels // grid, pixels % grid
    right = col >= half
    place = jnp.where(pixels < 0, -1, jnp.where(right, row + grid, row))
    return place, jnp.where(right, col - half, col)


def swapped(value):
    half = value.shape[1] // 2
    return jnp.concatenate([value[:, half:], value[:, :half]], axis=1)


def fold(first, second):
    left = lax.broadcasted_iota(jnp.int32, first.shape, 1) < first.shape[1] // 2
    return jnp.where(left, first, swapped(second)), jnp.where(left, swapped(first), second)


def chunks(blocks):
    width = 2 if blocks % 2 == 0 else 1
    return [(start, width) for start in range(0, blocks, width)]


def lanes(array, start, width):
    return jnp.concatenate([array[start + k : start + k + 1] for k in range(width)], axis=1)


def hits(ids, span):
    return lax.broadcasted_iota(jnp.int32, (span, ids.shape[1]), 0) == ids


def one_hot(place, start, width, span):
    ids = lanes(place, start, width).astype(F32)
    rows = lax.broadcasted_iota(jnp.int32, (span, ids.shape[1]), 0).astype(F32)
    if span <= 256:
        ids, rows = ids.astype(BF16), rows.astype(BF16)
    one, zero = jnp.ones((), BF16), jnp.zeros((), BF16)
    return jnp.where(rows == ids, one, zero)


def fill(place, blocks, size, span, hot_ref):
    for start, width in chunks(blocks):
        hot_ref[:, start * size : (start + width) * size] = one_hot(place, start, width, span)


def kick(real, imag, phases, energy, pixels, read_ref, hot_ref=None, dark=None, turn=None):
    grid = real.shape[0]
    half = grid // 2
    blocks, size = phases.shape
    place, col = cells(pixels, grid)

    def read():
        upper, lower = fold(real, imag)
        low = jnp.concatenate([upper, lower], axis=0).astype(BF16)
        for start, width in chunks(blocks):
            where = slice(start * size, (start + width) * size)
            hot = hot_ref[:, where] if turn else one_hot(place, start, width, 2 * grid)
            if hot_ref is not None and not turn:
                hot_ref[:, where] = hot
            picked = dot(low, hot, 0, 0)
            col_hit = hits(lanes(col, start, width), half)
            for part in range(2):
                value = picked[part * half : (part + 1) * half]
                value = jnp.sum(jnp.where(col_hit, value, 0.0), axis=0, keepdims=True)
                for k in range(width):
                    read_ref[part, start + k : start + k + 1, :] = value[:, k * size : (k + 1) * size]

    if dark is None:
        read()
    else:
        pl.when(jnp.logical_not(dark))(read)

        @pl.when(dark)
        def _():
            read_ref[...] = jnp.zeros(read_ref.shape, F32)
            fill(place, blocks, size, 2 * grid, hot_ref)

    cosine, sine = turn or (jnp.cos(phases), jnp.sin(phases))
    read_real = read_ref[0, :blocks, :]
    read_imag = read_ref[1, :blocks, :]
    energy = energy - KICK_RATE * (read_real * cosine - read_imag * sine)
    return phases + PHASE_RATE * energy, energy


def emit(real, imag, phases, pixels, hot_ref, spread_ref, filled):
    grid = real.shape[0]
    half = grid // 2
    blocks, size = phases.shape
    place, col = cells(pixels, grid)
    weight_real = jnp.cos(phases)
    weight_imag = -jnp.sin(phases)
    for start, width in chunks(blocks):
        where = slice(start * size, (start + width) * size)
        if not filled:
            hot_ref[:, where] = one_hot(place, start, width, 2 * grid)
        col_hit = hits(lanes(col, start, width), half)
        for part, weight in ((0, weight_real), (1, weight_imag)):
            value = jnp.where(col_hit, lanes(weight, start, width), 0.0)
            spread_ref[part * half : (part + 1) * half, where] = value.astype(BF16)
    span = blocks * size
    source = dot(hot_ref[:, :span], spread_ref[:, :span], 1, 1)
    source_real, source_imag = fold(source[:grid], source[grid:])
    return real + EMIT_RATE * source_real, imag + EMIT_RATE * source_imag


def position():
    return lax.axis_index("cuts") * lax.axis_size("group") + lax.axis_index("group")


def kept_unless(index):
    return jnp.where(position() == index, 0.0, 1.0).astype(F32)


def kick_kernel(field_hbm, phases_hbm, energy_hbm, pixels_hbm, dest_hbm, out, field, phases, energy, pixels, dest, read_ref, hot_ref, sems):
    blocks, size = phases.shape
    pairs = ((pixels_hbm, pixels), (phases_hbm, phases), (energy_hbm, energy), (dest_hbm, dest), (field_hbm, field))
    copies = [pltpu.make_async_copy(source, target, sems.at[k]) for k, (source, target) in enumerate(pairs)]
    for copy in copies:
        copy.start()
    for copy in copies[:-1]:
        copy.wait()
    grid = field.shape[1]
    place, _ = cells(pixels[...], grid)
    fill(place, blocks, size, 2 * grid, hot_ref)
    turn = (jnp.cos(phases[...]), jnp.sin(phases[...]))
    square = (blocks, blocks)
    own = lax.broadcasted_iota(jnp.int32, square, 0) == lax.broadcasted_iota(jnp.int32, square, 1)
    goals = jnp.where(own, jnp.broadcast_to(dest[0:1, :].astype(F32), square), 0.0)
    out[3 * blocks : 4 * blocks, :] = jnp.broadcast_to(jnp.sum(goals, axis=1, keepdims=True), (blocks, size))
    out[2 * blocks : 3 * blocks, :] = pixels[...].astype(F32)
    copies[-1].wait()
    new_phases, new_energy = kick(
        field[0], field[1], phases[...], energy[...], pixels[...], read_ref, hot_ref, turn=turn
    )
    out[0:blocks, :] = new_phases
    out[blocks : 2 * blocks, :] = new_energy


def by_destination(kinds):
    goals = kinds[-1]
    blocks = goals.shape[0]
    place = lax.broadcasted_iota(jnp.int32, goals.shape, 0)
    rank = jnp.zeros(goals.shape, jnp.int32)
    for block in range(blocks):
        goal = goals[block : block + 1]
        ahead = (goal < goals) | ((goal == goals) & (place > block))
        rank = rank + jnp.where(ahead, 1, 0)
    ordered = [jnp.zeros(kind.shape, F32) for kind in kinds]
    for block in range(blocks):
        here = rank[block : block + 1] == place
        ordered = [jnp.where(here, kind[block : block + 1], old) for kind, old in zip(kinds, ordered)]
    return ordered


def lane_groups(values, shifts):
    size = values[0].shape[1]
    group = lax.broadcasted_iota(jnp.int32, values[0].shape, 1) // (size // len(values))
    joined_up = None
    for k, (value, shift) in enumerate(zip(values, shifts)):
        if shift % size:
            value = pltpu.roll(value, shift % size, axis=1)
        joined_up = value if joined_up is None else jnp.where(group == k, value, joined_up)
    return joined_up


def radiate(blocks, dropped, field, state, form, out, hot_ref, spread_ref):
    pixels = state[2 * blocks : 3 * blocks, :].astype(jnp.int32)
    real, imag = emit(field[0], field[1], state[0:blocks, :], pixels, hot_ref, spread_ref, False)
    real, imag = diffract(real, imag, *form)
    keep = kept_unless(dropped)
    out[0] = real * keep
    out[1] = imag * keep


def first_radiate_kernel(blocks, dropped, field, state, propagator, *rest):
    *rest, hot_ref, spread_ref = rest
    if len(rest) > 3:
        *tables, out, high, low, matrix = rest
        matrix[...] = filter_matrix(*tables)
    else:
        out, high, low = rest
    form = real_form(propagator)
    high[...], low[...] = form
    radiate(blocks, dropped, field, state, form, out, hot_ref, spread_ref)


def third_radiate_kernel(blocks, field, state, high, low, out, hot_ref, spread_ref):
    needed = position() > 1

    @pl.when(needed)
    def _():
        radiate(blocks, 1, field, state, (high[...], low[...]), out, hot_ref, spread_ref)

    @pl.when(jnp.logical_not(needed))
    def _():
        out[...] = jnp.zeros(out.shape, F32)


def second_kernel(count, rows, cap, field, state, high, low, out, *rest):
    sends = rest[:-3]
    read_ref, hot_ref, spread_ref = rest[-3:]
    blocks, size = state.shape[0] // 4, state.shape[1]
    real, imag = field[0], field[1]
    grid = real.shape[0]
    pixels = state[2 * blocks : 3 * blocks, :].astype(jnp.int32)
    dark = position() == count - 1
    phases, energy = kick(
        real, imag, state[0:blocks, :], state[blocks : 2 * blocks, :], pixels, read_ref, hot_ref, dark
    )
    kinds = by_destination((phases, energy, state[2 * blocks : 3 * blocks, :], state[3 * blocks : 4 * blocks, :]))
    if rows:
        pairs, pieces = rows // 2, len(kinds)
        tiles = 2 * pairs + 1
        width = size // pieces
        for chunk in range(blocks // cap):
            parts = [kind[chunk * cap : (chunk + 1) * cap] for kind in kinds]
            for piece in range(pieces):
                row = lane_groups(parts, [(k - piece) * width for k in range(pieces)])
                out[pl.ds((piece * cap + 1) * tiles - 1, cap, stride=tiles), chunk, :] = row
    else:
        cuts = len(sends)
        cut = lax.div(lax.rem(position() + 1, count), count // cuts)
        for ahead, send in enumerate(sends):
            wanted = lax.rem(cut + ahead, cuts).astype(F32)
            chunk = [jnp.zeros((cap, size), F32)] * 2 + [jnp.full((cap, size), -1.0, F32)]
            for start in range(0, blocks, cap):
                goes = kinds[3][start : start + cap] == wanted
                chunk = [jnp.where(goes, kind[start : start + cap], old) for kind, old in zip(kinds, chunk)]
            for kind in range(3):
                send[kind * cap : (kind + 1) * cap, :] = chunk[kind]
    real, imag = emit(real, imag, phases, pixels, hot_ref, spread_ref, True)
    real, imag = diffract(real, imag, high[...], low[...])
    keep = kept_unless(count - 2)
    real, imag = real * keep, imag * keep
    if rows:
        for part in range(grid // rows):
            for pair in range(pairs):
                first = part * rows + 2 * pair
                out[part * tiles + pair] = real[first : first + 2]
                out[part * tiles + pairs + pair] = imag[first : first + 2]
    else:
        out[0] = real
        out[1] = imag


def filter_matrix(transmit, cos_out, sin_out, cos_in, sin_in):
    gain_real, gain_imag = transmit[0:1, :], transmit[1:2, :]
    cosine, sine = cos_out[...], sin_out[...]
    real = cosine * gain_real - sine * gain_imag
    imag = cosine * gain_imag + sine * gain_real
    full_real = exact_dot(real, cos_in[...]) + exact_dot(imag, sin_in[...])
    full_imag = exact_dot(imag, cos_in[...]) - exact_dot(real, sin_in[...])
    form = jnp.concatenate(
        [
            jnp.concatenate([full_real, -full_imag], axis=1),
            jnp.concatenate([full_imag, full_real], axis=1),
        ],
        axis=0,
    )
    high, low = split(form)
    return jnp.concatenate([high, high, low], axis=1)


def filter_kernel(cuts, chunk_count, matrix, data, out):
    count = out.shape[0] // 3
    rows, size = out.shape[1:]
    groups = count // cuts
    pairs = rows // 2
    tiles = 2 * pairs + 1
    stacked = jnp.concatenate(
        [
            jnp.concatenate(
                [data[pl.ds(part * pairs + j // 2, count, stride=tiles), j % 2, :] for part in range(2)], axis=0
            )
            for j in range(rows)
        ],
        axis=1,
    )
    high, low = split(stacked)
    result = dot(matrix[...], jnp.concatenate([high, low, high], axis=0), 1, 0)
    for part in range(2):
        for j in range(rows):
            out[pl.ds(part, count, stride=3), j, :] = result[
                part * count : (part + 1) * count, j * size : (j + 1) * size
            ]
    bundles = [
        pltpu.roll(data[pl.ds(tiles - 1, count, stride=tiles), chunk, :], 1, axis=0)
        for chunk in range(chunk_count)
    ]
    goals = [bundle[:, size - 1 : size] for bundle in bundles]
    for cut in range(cuts):
        chosen = bundles[0]
        for bundle, goal in zip(bundles[1:], goals[1:]):
            chosen = jnp.where(goal == float(cut), bundle, chosen)
        first = cut * groups + 2
        fits = min(groups, count - first)
        for source in range(cuts):
            tile = chosen[source * groups : (source + 1) * groups]
            out[pl.ds(3 * first + 2, fits, stride=3), source, :] = tile[:fits]
            for k in range(fits, groups):
                out[3 * (first + k - count) + 2, source : source + 1, :] = tile[k : k + 1]


def joined(chunks_in):
    cap = chunks_in[0].shape[0] // 3
    kinds = [
        jnp.concatenate([chunk[kind * cap : (kind + 1) * cap, :] for chunk in chunks_in], axis=0)
        for kind in range(3)
    ]
    return kinds[0], kinds[1], kinds[2].astype(jnp.int32)


def relayed(fields, cuts):
    count = fields.shape[0] // 3
    size = fields.shape[2]
    width = size // KINDS
    bundles = [fields[pl.ds(2, count, stride=3), cut, :] for cut in range(cuts)]
    kinds = [lane_groups(bundles, [(cut - kind) * width for cut in range(cuts)]) for kind in range(KINDS)]
    wanted = lax.div(lax.rem(position() + (count - 2), count), count // cuts).astype(F32)
    return kinds[0], kinds[1], jnp.where(kinds[3] == wanted, kinds[2], -1.0).astype(jnp.int32)


def third_kernel(cuts, fields, *rest):
    out, state, read_ref = rest[-3:]
    chunks_in = rest[:-3]
    if chunks_in:
        phases, energy, pixels = joined(chunks_in)
        out[...] = fields[...]
    else:
        phases, energy, pixels = relayed(fields, cuts)
        rows = fields.shape[1]
        for part in range(fields.shape[0] // 3):
            for kind in range(2):
                out[kind, part * rows : (part + 1) * rows, :] = fields[3 * part + kind]
    phases, energy = kick(out[0], out[1], phases, energy, pixels, read_ref)
    blocks = phases.shape[0]
    state[0:blocks, :] = phases
    state[blocks : 2 * blocks, :] = energy
    state[2 * blocks : 3 * blocks, :] = pixels.astype(F32)


def fourth_kernel(field, state, high, low, out, read_ref, hot_ref, spread_ref):
    blocks = state.shape[0] // 3
    needed = position() > 0

    @pl.when(needed)
    def _():
        pixels = state[2 * blocks : 3 * blocks, :].astype(jnp.int32)
        real, imag = field[0], field[1]
        dark = position() == 1
        phases, _ = kick(
            real, imag, state[0:blocks, :], state[blocks : 2 * blocks, :], pixels, read_ref, hot_ref, dark
        )
        real, imag = emit(real, imag, phases, pixels, hot_ref, spread_ref, True)
        out[0], out[1] = diffract(real, imag, high[...], low[...])

    @pl.when(jnp.logical_not(needed))
    def _():
        out[...] = jnp.zeros(out.shape, F32)


def call(kernel, out_shape, scratch, flops, args, memory=pltpu.VMEM):
    specs = [pl.BlockSpec(memory_space=memory)] * len(args)
    return pl.pallas_call(
        kernel,
        out_shape=out_shape,
        in_specs=specs,
        out_specs=jax.tree.map(lambda _: pl.BlockSpec(memory_space=pltpu.VMEM), out_shape),
        scratch_shapes=scratch,
        compiler_params=pltpu.CompilerParams(vmem_limit_bytes=VMEM_LIMIT),
        cost_estimate=pl.CostEstimate(flops=flops, bytes_accessed=1 << 19, transcendentals=0),
    )(*args)


def time_tables(count):
    times = jnp.arange(count, dtype=jnp.int32)
    cos_out, sin_out = angle_table((times + (count - 4)) % count, times, count)
    return (cos_out / count, sin_out / count, *angle_table(times, times, count))


def angle_table(first_ids, second_ids, total_slices):
    product = first_ids[:, None] * second_ids[None, :] % total_slices
    angle = product.astype(F32) * (2.0 * math.pi / total_slices)
    return jnp.cos(angle), jnp.sin(angle)


def filter_any(field, transmit, count):
    grid = field.shape[1]
    span = grid * grid
    share = -(-span // count)
    flat = jnp.pad(field.reshape(2, span), ((0, 0), (0, share * count - span)))
    parts = flat.reshape(2, count, share).transpose(1, 0, 2)
    got = lax.all_to_all(parts, AXES, split_axis=0, concat_axis=0, tiled=True)
    got = jnp.roll(got, 2, axis=0)
    real, imag = got[:, 0], got[:, 1]
    times = jnp.arange(count, dtype=jnp.int32)
    cosine, sine = angle_table(times, times, count)
    spec_real = exact_dot(cosine, real) + exact_dot(sine, imag)
    spec_imag = exact_dot(cosine, imag) - exact_dot(sine, real)
    gain_real, gain_imag = transmit[0][:, None], transmit[1][:, None]
    shaped_real = gain_real * spec_real - gain_imag * spec_imag
    shaped_imag = gain_real * spec_imag + gain_imag * spec_real
    back_real = (exact_dot(cosine, shaped_real) - exact_dot(sine, shaped_imag)) / count
    back_imag = (exact_dot(cosine, shaped_imag) + exact_dot(sine, shaped_real)) / count
    back = jnp.stack([back_real, back_imag], axis=1)
    sent = jnp.roll(back, 2, axis=0)
    fields = lax.all_to_all(sent, AXES, split_axis=0, concat_axis=0, tiled=True)
    fields = fields.transpose(1, 0, 2).reshape(2, share * count)[:, :span]
    return fields.reshape(2, grid, grid)


def on_device(radiation, phases, energy, pixels, destination, propagator, transmit):
    cuts, groups = lax.axis_size("cuts"), lax.axis_size("group")
    count = cuts * groups
    grid = radiation.shape[-1]
    blocks, size = phases.shape[1:]
    cap = max(2, 2 * blocks // cuts)
    rows = grid // count if grid % count == 0 else 0
    if rows != 4 or cap * KINDS != count or cuts != KINDS or size % 128 or blocks != 2 * cap or groups % 8:
        rows = 0
    field = radiation[0]
    shape = lambda *dims: jax.ShapeDtypeStruct(dims, F32)
    read = lambda number: pltpu.VMEM((2, number, size), F32)
    hot = lambda number: [pltpu.VMEM((2 * grid, number * size), BF16), pltpu.VMEM((grid, number * size), BF16)]
    pass_flops = 4 * blocks * size * grid * grid
    prop_flops = 48 * grid**3

    given = (field, phases[0], energy[0], pixels[0], destination)
    state = call(
        kick_kernel, shape(4 * blocks, size),
        [
            pltpu.VMEM((2, grid, grid), F32),
            pltpu.VMEM((blocks, size), F32),
            pltpu.VMEM((blocks, size), F32),
            pltpu.VMEM((blocks, size), jnp.int32),
            pltpu.VMEM((1, blocks), jnp.int32),
            read(blocks),
            hot(blocks)[0],
            pltpu.SemaphoreType.DMA((5,)),
        ],
        pass_flops, tuple(pltpu.with_memory_space_constraint(value, pltpu.HBM) for value in given), pl.ANY,
    )
    route = [((i + 1) % count, i) for i in range(count)]
    behind = lax.ppermute(state, AXES, route)
    form_shape = jax.ShapeDtypeStruct((2 * grid, 2 * grid), BF16)
    made = [shape(2, grid, grid), form_shape, form_shape]
    tables = ()
    if rows:
        made.append(jax.ShapeDtypeStruct((2 * count, 6 * count), BF16))
        tables = (transmit, *time_tables(count))
    field, *form = call(
        functools.partial(first_radiate_kernel, blocks, count - 1), made, hot(blocks), pass_flops + prop_flops,
        (field, state, propagator, *tables),
    )
    matrix = form[2:]
    form = form[:2]
    part_shape = shape(count * (rows + 1), 2, grid) if rows else shape(2, grid, grid)
    send_shapes = [] if rows else [shape(3 * cap, size)] * cuts
    field, *sends = call(
        functools.partial(second_kernel, count, rows, cap), (part_shape, *send_shapes),
        [read(blocks)] + hot(blocks), 2 * pass_flops + prop_flops,
        (field, behind, *form),
    )
    chunks_in = [
        lax.ppermute(send, AXES, [(i, (i + 3 + groups * ahead) % count) for i in range(count)])
        for ahead, send in enumerate(sends)
    ]
    if rows:
        data = lax.all_to_all(field, AXES, split_axis=0, concat_axis=0, tiled=True)
        sent = call(
            functools.partial(filter_kernel, cuts, blocks // cap), shape(count * 3, rows, grid), [], 1 << 24,
            (*matrix, data),
        )
        fields = lax.all_to_all(sent, AXES, split_axis=0, concat_axis=0, tiled=True)
    else:
        fields = filter_any(field, transmit, count)
    capacity = cuts * cap
    share = capacity // blocks
    field, state = call(
        functools.partial(third_kernel, cuts), (shape(2, grid, grid), shape(3 * capacity, size)),
        [read(capacity)], share * pass_flops, (fields, *chunks_in),
    )
    behind = lax.ppermute(state, AXES, route)
    field = call(
        functools.partial(third_radiate_kernel, capacity), shape(2, grid, grid), hot(capacity),
        share * pass_flops + prop_flops, (field, state, *form),
    )
    out = call(
        fourth_kernel, shape(2, grid, grid), [read(capacity)] + hot(capacity),
        2 * share * pass_flops + prop_flops, (field, behind, *form),
    )
    return out[None]


def solution(mesh):
    return jax.shard_map(
        on_device,
        mesh=mesh,
        in_specs=(
            P(("cuts", "group"), None, None, None),
            P(("cuts", "group"), None, None),
            P(("cuts", "group"), None, None),
            P(("cuts", "group"), None, None),
            P(("cuts", "group"), None),
            P(),
            P(),
        ),
        out_specs=P(("cuts", "group"), None, None, None),
        check_vma=False,
    )
```

```python
import functools
import math

import jax
import jax.numpy as jnp
from jax import lax
from jax.experimental import pallas as pl
from jax.experimental.pallas import tpu as pltpu
from jax.sharding import PartitionSpec as P

KICK_RATE = 0.5
PHASE_RATE = 1.0
EMIT_RATE = 0.5

AXES = ("cuts", "group")
F32 = jnp.float32
BF16 = jnp.bfloat16
KINDS = 4
VMEM_LIMIT = 48 * 1024 * 1024


def dot(left, right, left_dim, right_dim):
    dims = (((left_dim,), (right_dim,)), ((), ()))
    return lax.dot_general(left, right, dims, preferred_element_type=F32)


def exact_dot(left, right):
    return jnp.dot(left, right, precision=lax.Precision.HIGHEST, preferred_element_type=F32)


def split(value):
    high = value.astype(BF16)
    return high, (value - high.astype(F32)).astype(BF16)


def real_form(propagator):
    prop_real, prop_imag = propagator[0], propagator[1]
    form = jnp.concatenate(
        [
            jnp.concatenate([prop_real, -prop_imag], axis=1),
            jnp.concatenate([prop_imag, prop_real], axis=1),
        ],
        axis=0,
    )
    return split(form)


def diffract(real, imag, form_high, form_low):
    size = real.shape[0]
    high, low = split(jnp.concatenate([real, imag], axis=1))
    both = dot(jnp.concatenate([high, low], axis=0), form_high, 1, 1)
    right = both[:size] + both[size:] + dot(high, form_low, 1, 1)
    high, low = split(jnp.concatenate([right[:, :size], right[:, size:]], axis=0))
    both = dot(form_high, jnp.concatenate([high, low], axis=1), 1, 0)
    out = both[:, :size] + both[:, size:] + dot(form_low, high, 1, 0)
    return out[:size], out[size:]


def cells(pixels, grid):
    half = grid // 2
    shift = grid.bit_length() - 1
    if grid == 1 << shift:
        row, col = lax.shift_right_arithmetic(pixels, shift), pixels & (grid - 1)
    else:
        row, col = pixels // grid, pixels % grid
    right = col >= half
    place = jnp.where(pixels < 0, -1, jnp.where(right, row + grid, row))
    return place, jnp.where(right, col - half, col)


def swapped(value):
    half = value.shape[1] // 2
    return jnp.concatenate([value[:, half:], value[:, :half]], axis=1)


def fold(first, second):
    left = lax.broadcasted_iota(jnp.int32, first.shape, 1) < first.shape[1] // 2
    return jnp.where(left, first, swapped(second)), jnp.where(left, swapped(first), second)


def chunks(blocks):
    width = next(width for width in (4, 2, 1) if blocks % width == 0)
    return [(start, width) for start in range(0, blocks, width)]


def lanes(array, start, width):
    return jnp.concatenate([array[start + k : start + k + 1] for k in range(width)], axis=1)


def hits(ids, span):
    return lax.broadcasted_iota(jnp.int32, (span, ids.shape[1]), 0) == ids


def one_hot(place, start, width, span):
    ids = lanes(place, start, width).astype(F32)
    rows = lax.broadcasted_iota(jnp.int32, (span, ids.shape[1]), 0).astype(F32)
    if span <= 256:
        ids, rows = ids.astype(BF16), rows.astype(BF16)
    one, zero = jnp.ones((), BF16), jnp.zeros((), BF16)
    return jnp.where(rows == ids, one, zero)


def fill(place, blocks, size, span, hot_ref):
    for start, width in chunks(blocks):
        hot_ref[:, start * size : (start + width) * size] = one_hot(place, start, width, span)


def kick(real, imag, phases, energy, pixels, read_ref, hot_ref=None, dark=None, turn=None):
    grid = real.shape[0]
    half = grid // 2
    blocks, size = phases.shape
    place, col = cells(pixels, grid)

    def read():
        upper, lower = fold(real, imag)
        low = jnp.concatenate([upper, lower], axis=0).astype(BF16)
        for start, width in chunks(blocks):
            where = slice(start * size, (start + width) * size)
            hot = hot_ref[:, where] if turn else one_hot(place, start, width, 2 * grid)
            if hot_ref is not None and not turn:
                hot_ref[:, where] = hot
            picked = dot(low, hot, 0, 0)
            col_hit = hits(lanes(col, start, width), half)
            for part in range(2):
                value = picked[part * half : (part + 1) * half]
                value = jnp.sum(jnp.where(col_hit, value, 0.0), axis=0, keepdims=True)
                for k in range(width):
                    read_ref[part, start + k : start + k + 1, :] = value[:, k * size : (k + 1) * size]

    if dark is None:
        read()
    else:
        pl.when(jnp.logical_not(dark))(read)

        @pl.when(dark)
        def _():
            read_ref[...] = jnp.zeros(read_ref.shape, F32)
            fill(place, blocks, size, 2 * grid, hot_ref)

    cosine, sine = turn or (jnp.cos(phases), jnp.sin(phases))
    read_real = read_ref[0, :blocks, :]
    read_imag = read_ref[1, :blocks, :]
    energy = energy - KICK_RATE * (read_real * cosine - read_imag * sine)
    return phases + PHASE_RATE * energy, energy


def emit(real, imag, phases, pixels, hot_ref, spread_ref, filled):
    grid = real.shape[0]
    half = grid // 2
    blocks, size = phases.shape
    place, col = cells(pixels, grid)
    weight_real = jnp.cos(phases)
    weight_imag = -jnp.sin(phases)
    for start, width in chunks(blocks):
        where = slice(start * size, (start + width) * size)
        if not filled:
            hot_ref[:, where] = one_hot(place, start, width, 2 * grid)
        col_hit = hits(lanes(col, start, width), half)
        for part, weight in ((0, weight_real), (1, weight_imag)):
            value = jnp.where(col_hit, lanes(weight, start, width), 0.0)
            spread_ref[part * half : (part + 1) * half, where] = value.astype(BF16)
    span = blocks * size
    source = dot(hot_ref[:, :span], spread_ref[:, :span], 1, 1)
    source_real, source_imag = fold(source[:grid], source[grid:])
    return real + EMIT_RATE * source_real, imag + EMIT_RATE * source_imag


def position():
    return lax.axis_index("cuts") * lax.axis_size("group") + lax.axis_index("group")


def kept_unless(index):
    return jnp.where(position() == index, 0.0, 1.0).astype(F32)


def kick_kernel(field_hbm, phases_hbm, energy_hbm, pixels_hbm, dest_hbm, out, field, phases, energy, pixels, dest, read_ref, hot_ref, sems):
    blocks, size = phases.shape
    pairs = ((pixels_hbm, pixels), (phases_hbm, phases), (energy_hbm, energy), (dest_hbm, dest), (field_hbm, field))
    copies = [pltpu.make_async_copy(source, target, sems.at[k]) for k, (source, target) in enumerate(pairs)]
    for copy in copies:
        copy.start()
    for copy in copies[:-1]:
        copy.wait()
    grid = field.shape[1]
    place, _ = cells(pixels[...], grid)
    fill(place, blocks, size, 2 * grid, hot_ref)
    turn = (jnp.cos(phases[...]), jnp.sin(phases[...]))
    square = (blocks, blocks)
    own = lax.broadcasted_iota(jnp.int32, square, 0) == lax.broadcasted_iota(jnp.int32, square, 1)
    goals = jnp.where(own, jnp.broadcast_to(dest[0:1, :].astype(F32), square), 0.0)
    out[3 * blocks : 4 * blocks, :] = jnp.broadcast_to(jnp.sum(goals, axis=1, keepdims=True), (blocks, size))
    out[2 * blocks : 3 * blocks, :] = pixels[...].astype(F32)
    copies[-1].wait()
    new_phases, new_energy = kick(
        field[0], field[1], phases[...], energy[...], pixels[...], read_ref, hot_ref, turn=turn
    )
    out[0:blocks, :] = new_phases
    out[blocks : 2 * blocks, :] = new_energy


def by_destination(kinds):
    goals = kinds[-1]
    blocks = goals.shape[0]
    place = lax.broadcasted_iota(jnp.int32, goals.shape, 0)
    rank = jnp.zeros(goals.shape, jnp.int32)
    for block in range(blocks):
        goal = goals[block : block + 1]
        ahead = (goal < goals) | ((goal == goals) & (place > block))
        rank = rank + jnp.where(ahead, 1, 0)
    ordered = [jnp.zeros(kind.shape, F32) for kind in kinds]
    for block in range(blocks):
        here = rank[block : block + 1] == place
        ordered = [jnp.where(here, kind[block : block + 1], old) for kind, old in zip(kinds, ordered)]
    return ordered


def lane_groups(values, shifts):
    size = values[0].shape[1]
    group = lax.broadcasted_iota(jnp.int32, values[0].shape, 1) // (size // len(values))
    joined_up = None
    for k, (value, shift) in enumerate(zip(values, shifts)):
        if shift % size:
            value = pltpu.roll(value, shift % size, axis=1)
        joined_up = value if joined_up is None else jnp.where(group == k, value, joined_up)
    return joined_up


def radiate(blocks, dropped, field, state, form, out, hot_ref, spread_ref):
    pixels = state[2 * blocks : 3 * blocks, :].astype(jnp.int32)
    real, imag = emit(field[0], field[1], state[0:blocks, :], pixels, hot_ref, spread_ref, False)
    real, imag = diffract(real, imag, *form)
    keep = kept_unless(dropped)
    out[0] = real * keep
    out[1] = imag * keep


def first_radiate_kernel(blocks, dropped, field, state, propagator, *rest):
    *rest, hot_ref, spread_ref = rest
    if len(rest) > 3:
        *tables, out, high, low, matrix = rest
        matrix[...] = filter_matrix(*tables)
    else:
        out, high, low = rest
    form = real_form(propagator)
    high[...], low[...] = form
    radiate(blocks, dropped, field, state, form, out, hot_ref, spread_ref)


def third_radiate_kernel(blocks, field, state, high, low, out, hot_ref, spread_ref):
    needed = position() > 1

    @pl.when(needed)
    def _():
        radiate(blocks, 1, field, state, (high[...], low[...]), out, hot_ref, spread_ref)

    @pl.when(jnp.logical_not(needed))
    def _():
        out[...] = jnp.zeros(out.shape, F32)


def second_kernel(count, rows, cap, field, state, high, low, out, *rest):
    sends = rest[:-3]
    read_ref, hot_ref, spread_ref = rest[-3:]
    blocks, size = state.shape[0] // 4, state.shape[1]
    real, imag = field[0], field[1]
    grid = real.shape[0]
    pixels = state[2 * blocks : 3 * blocks, :].astype(jnp.int32)
    dark = position() == count - 1
    phases, energy = kick(
        real, imag, state[0:blocks, :], state[blocks : 2 * blocks, :], pixels, read_ref, hot_ref, dark
    )
    kinds = by_destination((phases, energy, state[2 * blocks : 3 * blocks, :], state[3 * blocks : 4 * blocks, :]))
    if rows:
        pairs, pieces = rows // 2, len(kinds)
        tiles = 2 * pairs + 1
        width = size // pieces
        for chunk in range(blocks // cap):
            parts = [kind[chunk * cap : (chunk + 1) * cap] for kind in kinds]
            for piece in range(pieces):
                row = lane_groups(parts, [(k - piece) * width for k in range(pieces)])
                out[pl.ds((piece * cap + 1) * tiles - 1, cap, stride=tiles), chunk, :] = row
    else:
        cuts = len(sends)
        cut = lax.div(lax.rem(position() + 1, count), count // cuts)
        for ahead, send in enumerate(sends):
            wanted = lax.rem(cut + ahead, cuts).astype(F32)
            chunk = [jnp.zeros((cap, size), F32)] * 2 + [jnp.full((cap, size), -1.0, F32)]
            for start in range(0, blocks, cap):
                goes = kinds[3][start : start + cap] == wanted
                chunk = [jnp.where(goes, kind[start : start + cap], old) for kind, old in zip(kinds, chunk)]
            for kind in range(3):
                send[kind * cap : (kind + 1) * cap, :] = chunk[kind]
    real, imag = emit(real, imag, phases, pixels, hot_ref, spread_ref, True)
    real, imag = diffract(real, imag, high[...], low[...])
    keep = kept_unless(count - 2)
    real, imag = real * keep, imag * keep
    if rows:
        for part in range(grid // rows):
            for pair in range(pairs):
                first = part * rows + 2 * pair
                out[part * tiles + pair] = real[first : first + 2]
                out[part * tiles + pairs + pair] = imag[first : first + 2]
    else:
        out[0] = real
        out[1] = imag


def filter_matrix(transmit, cos_out, sin_out, cos_in, sin_in):
    gain_real, gain_imag = transmit[0:1, :], transmit[1:2, :]
    cosine, sine = cos_out[...], sin_out[...]
    real = cosine * gain_real - sine * gain_imag
    imag = cosine * gain_imag + sine * gain_real
    full_real = exact_dot(real, cos_in[...]) + exact_dot(imag, sin_in[...])
    full_imag = exact_dot(imag, cos_in[...]) - exact_dot(real, sin_in[...])
    form = jnp.concatenate(
        [
            jnp.concatenate([full_real, -full_imag], axis=1),
            jnp.concatenate([full_imag, full_real], axis=1),
        ],
        axis=0,
    )
    high, low = split(form)
    return jnp.concatenate([high, high, low], axis=1)


def filter_kernel(cuts, chunk_count, matrix, data, out):
    count = out.shape[0] // 3
    rows, size = out.shape[1:]
    groups = count // cuts
    pairs = rows // 2
    tiles = 2 * pairs + 1
    stacked = jnp.concatenate(
        [
            jnp.concatenate(
                [data[pl.ds(part * pairs + j // 2, count, stride=tiles), j % 2, :] for part in range(2)], axis=0
            )
            for j in range(rows)
        ],
        axis=1,
    )
    high, low = split(stacked)
    result = dot(matrix[...], jnp.concatenate([high, low, high], axis=0), 1, 0)
    for part in range(2):
        for j in range(rows):
            out[pl.ds(part, count, stride=3), j, :] = result[
                part * count : (part + 1) * count, j * size : (j + 1) * size
            ]
    bundles = [
        pltpu.roll(data[pl.ds(tiles - 1, count, stride=tiles), chunk, :], 1, axis=0)
        for chunk in range(chunk_count)
    ]
    goals = [bundle[:, size - 1 : size] for bundle in bundles]
    for cut in range(cuts):
        chosen = bundles[0]
        for bundle, goal in zip(bundles[1:], goals[1:]):
            chosen = jnp.where(goal == float(cut), bundle, chosen)
        first = cut * groups + 2
        fits = min(groups, count - first)
        for source in range(cuts):
            tile = chosen[source * groups : (source + 1) * groups]
            out[pl.ds(3 * first + 2, fits, stride=3), source, :] = tile[:fits]
            for k in range(fits, groups):
                out[3 * (first + k - count) + 2, source : source + 1, :] = tile[k : k + 1]


def joined(chunks_in):
    cap = chunks_in[0].shape[0] // 3
    kinds = [
        jnp.concatenate([chunk[kind * cap : (kind + 1) * cap, :] for chunk in chunks_in], axis=0)
        for kind in range(3)
    ]
    return kinds[0], kinds[1], kinds[2].astype(jnp.int32)


def relayed(fields, cuts):
    count = fields.shape[0] // 3
    size = fields.shape[2]
    width = size // KINDS
    bundles = [fields[pl.ds(2, count, stride=3), cut, :] for cut in range(cuts)]
    kinds = [lane_groups(bundles, [(cut - kind) * width for cut in range(cuts)]) for kind in range(KINDS)]
    wanted = lax.div(lax.rem(position() + (count - 2), count), count // cuts).astype(F32)
    return kinds[0], kinds[1], jnp.where(kinds[3] == wanted, kinds[2], -1.0).astype(jnp.int32)


def third_kernel(cuts, fields, *rest):
    out, state, read_ref = rest[-3:]
    chunks_in = rest[:-3]
    if chunks_in:
        phases, energy, pixels = joined(chunks_in)
        out[...] = fields[...]
    else:
        phases, energy, pixels = relayed(fields, cuts)
        rows = fields.shape[1]
        for part in range(fields.shape[0] // 3):
            for kind in range(2):
                out[kind, part * rows : (part + 1) * rows, :] = fields[3 * part + kind]
    phases, energy = kick(out[0], out[1], phases, energy, pixels, read_ref)
    blocks = phases.shape[0]
    state[0:blocks, :] = phases
    state[blocks : 2 * blocks, :] = energy
    state[2 * blocks : 3 * blocks, :] = pixels.astype(F32)


def fourth_kernel(field, state, high, low, out, read_ref, hot_ref, spread_ref):
    blocks = state.shape[0] // 3
    needed = position() > 0

    @pl.when(needed)
    def _():
        pixels = state[2 * blocks : 3 * blocks, :].astype(jnp.int32)
        real, imag = field[0], field[1]
        dark = position() == 1
        phases, _ = kick(
            real, imag, state[0:blocks, :], state[blocks : 2 * blocks, :], pixels, read_ref, hot_ref, dark
        )
        real, imag = emit(real, imag, phases, pixels, hot_ref, spread_ref, True)
        out[0], out[1] = diffract(real, imag, high[...], low[...])

    @pl.when(jnp.logical_not(needed))
    def _():
        out[...] = jnp.zeros(out.shape, F32)


def call(kernel, out_shape, scratch, flops, args, memory=pltpu.VMEM):
    specs = [pl.BlockSpec(memory_space=memory)] * len(args)
    return pl.pallas_call(
        kernel,
        out_shape=out_shape,
        in_specs=specs,
        out_specs=jax.tree.map(lambda _: pl.BlockSpec(memory_space=pltpu.VMEM), out_shape),
        scratch_shapes=scratch,
        compiler_params=pltpu.CompilerParams(vmem_limit_bytes=VMEM_LIMIT),
        cost_estimate=pl.CostEstimate(flops=flops, bytes_accessed=1 << 19, transcendentals=0),
    )(*args)


def time_tables(count):
    times = jnp.arange(count, dtype=jnp.int32)
    cos_out, sin_out = angle_table((times + (count - 4)) % count, times, count)
    return (cos_out / count, sin_out / count, *angle_table(times, times, count))


def angle_table(first_ids, second_ids, total_slices):
    product = first_ids[:, None] * second_ids[None, :] % total_slices
    angle = product.astype(F32) * (2.0 * math.pi / total_slices)
    return jnp.cos(angle), jnp.sin(angle)


def filter_any(field, transmit, count):
    grid = field.shape[1]
    span = grid * grid
    share = -(-span // count)
    flat = jnp.pad(field.reshape(2, span), ((0, 0), (0, share * count - span)))
    parts = flat.reshape(2, count, share).transpose(1, 0, 2)
    got = lax.all_to_all(parts, AXES, split_axis=0, concat_axis=0, tiled=True)
    got = jnp.roll(got, 2, axis=0)
    real, imag = got[:, 0], got[:, 1]
    times = jnp.arange(count, dtype=jnp.int32)
    cosine, sine = angle_table(times, times, count)
    spec_real = exact_dot(cosine, real) + exact_dot(sine, imag)
    spec_imag = exact_dot(cosine, imag) - exact_dot(sine, real)
    gain_real, gain_imag = transmit[0][:, None], transmit[1][:, None]
    shaped_real = gain_real * spec_real - gain_imag * spec_imag
    shaped_imag = gain_real * spec_imag + gain_imag * spec_real
    back_real = (exact_dot(cosine, shaped_real) - exact_dot(sine, shaped_imag)) / count
    back_imag = (exact_dot(cosine, shaped_imag) + exact_dot(sine, shaped_real)) / count
    back = jnp.stack([back_real, back_imag], axis=1)
    sent = jnp.roll(back, 2, axis=0)
    fields = lax.all_to_all(sent, AXES, split_axis=0, concat_axis=0, tiled=True)
    fields = fields.transpose(1, 0, 2).reshape(2, share * count)[:, :span]
    return fields.reshape(2, grid, grid)


def on_device(radiation, phases, energy, pixels, destination, propagator, transmit):
    cuts, groups = lax.axis_size("cuts"), lax.axis_size("group")
    count = cuts * groups
    grid = radiation.shape[-1]
    blocks, size = phases.shape[1:]
    cap = max(2, 2 * blocks // cuts)
    rows = grid // count if grid % count == 0 else 0
    if rows != 4 or cap * KINDS != count or cuts != KINDS or size % 128 or blocks != 2 * cap or groups % 8:
        rows = 0
    field = radiation[0]
    shape = lambda *dims: jax.ShapeDtypeStruct(dims, F32)
    read = lambda number: pltpu.VMEM((2, number, size), F32)
    hot = lambda number: [pltpu.VMEM((2 * grid, number * size), BF16), pltpu.VMEM((grid, number * size), BF16)]
    pass_flops = 4 * blocks * size * grid * grid
    prop_flops = 48 * grid**3

    given = (field, phases[0], energy[0], pixels[0], destination)
    state = call(
        kick_kernel, shape(4 * blocks, size),
        [
            pltpu.VMEM((2, grid, grid), F32),
            pltpu.VMEM((blocks, size), F32),
            pltpu.VMEM((blocks, size), F32),
            pltpu.VMEM((blocks, size), jnp.int32),
            pltpu.VMEM((1, blocks), jnp.int32),
            read(blocks),
            hot(blocks)[0],
            pltpu.SemaphoreType.DMA((5,)),
        ],
        pass_flops, tuple(pltpu.with_memory_space_constraint(value, pltpu.HBM) for value in given), pl.ANY,
    )
    route = [((i + 1) % count, i) for i in range(count)]
    behind = lax.ppermute(state, AXES, route)
    form_shape = jax.ShapeDtypeStruct((2 * grid, 2 * grid), BF16)
    made = [shape(2, grid, grid), form_shape, form_shape]
    tables = ()
    if rows:
        made.append(jax.ShapeDtypeStruct((2 * count, 6 * count), BF16))
        tables = (transmit, *time_tables(count))
    field, *form = call(
        functools.partial(first_radiate_kernel, blocks, count - 1), made, hot(blocks), pass_flops + prop_flops,
        (field, state, propagator, *tables),
    )
    matrix = form[2:]
    form = form[:2]
    part_shape = shape(count * (rows + 1), 2, grid) if rows else shape(2, grid, grid)
    send_shapes = [] if rows else [shape(3 * cap, size)] * cuts
    field, *sends = call(
        functools.partial(second_kernel, count, rows, cap), (part_shape, *send_shapes),
        [read(blocks)] + hot(blocks), 2 * pass_flops + prop_flops,
        (field, behind, *form),
    )
    chunks_in = [
        lax.ppermute(send, AXES, [(i, (i + 3 + groups * ahead) % count) for i in range(count)])
        for ahead, send in enumerate(sends)
    ]
    if rows:
        data = lax.all_to_all(field, AXES, split_axis=0, concat_axis=0, tiled=True)
        sent = call(
            functools.partial(filter_kernel, cuts, blocks // cap), shape(count * 3, rows, grid), [], 1 << 24,
            (*matrix, data),
        )
        fields = lax.all_to_all(sent, AXES, split_axis=0, concat_axis=0, tiled=True)
    else:
        fields = filter_any(field, transmit, count)
    capacity = cuts * cap
    share = capacity // blocks
    field, state = call(
        functools.partial(third_kernel, cuts), (shape(2, grid, grid), shape(3 * capacity, size)),
        [read(capacity)], share * pass_flops, (fields, *chunks_in),
    )
    behind = lax.ppermute(state, AXES, route)
    field = call(
        functools.partial(third_radiate_kernel, capacity), shape(2, grid, grid), hot(capacity),
        share * pass_flops + prop_flops, (field, state, *form),
    )
    out = call(
        fourth_kernel, shape(2, grid, grid), [read(capacity)] + hot(capacity),
        2 * share * pass_flops + prop_flops, (field, behind, *form),
    )
    return out[None]


def solution(mesh):
    return jax.shard_map(
        on_device,
        mesh=mesh,
        in_specs=(
            P(("cuts", "group"), None, None, None),
            P(("cuts", "group"), None, None),
            P(("cuts", "group"), None, None),
            P(("cuts", "group"), None, None),
            P(("cuts", "group"), None),
            P(),
            P(),
        ),
        out_specs=P(("cuts", "group"), None, None, None),
        check_vma=False,
    )
```

```python
import functools
import math

import jax
import jax.numpy as jnp
from jax import lax
from jax.experimental import pallas as pl
from jax.experimental.pallas import tpu as pltpu
from jax.sharding import PartitionSpec as P

KICK_RATE = 0.5
PHASE_RATE = 1.0
EMIT_RATE = 0.5

AXES = ("cuts", "group")
F32 = jnp.float32
BF16 = jnp.bfloat16
KINDS = 4
VMEM_LIMIT = 48 * 1024 * 1024


def dot(left, right, left_dim, right_dim):
    dims = (((left_dim,), (right_dim,)), ((), ()))
    return lax.dot_general(left, right, dims, preferred_element_type=F32)


def exact_dot(left, right):
    return jnp.dot(left, right, precision=lax.Precision.HIGHEST, preferred_element_type=F32)


def split(value):
    high = value.astype(BF16)
    return high, (value - high.astype(F32)).astype(BF16)


def real_form(propagator):
    prop_real, prop_imag = propagator[0], propagator[1]
    form = jnp.concatenate(
        [
            jnp.concatenate([prop_real, -prop_imag], axis=1),
            jnp.concatenate([prop_imag, prop_real], axis=1),
        ],
        axis=0,
    )
    return split(form)


def diffract(real, imag, form_high, form_low):
    size = real.shape[0]
    high, low = split(jnp.concatenate([real, imag], axis=1))
    both = dot(jnp.concatenate([high, low], axis=0), form_high, 1, 1)
    right = both[:size] + both[size:] + dot(high, form_low, 1, 1)
    high, low = split(jnp.concatenate([right[:, :size], right[:, size:]], axis=0))
    both = dot(form_high, jnp.concatenate([high, low], axis=1), 1, 0)
    out = both[:, :size] + both[:, size:] + dot(form_low, high, 1, 0)
    return out[:size], out[size:]


def cells(pixels, grid):
    half = grid // 2
    shift = grid.bit_length() - 1
    if grid == 1 << shift:
        row, col = lax.shift_right_arithmetic(pixels, shift), pixels & (grid - 1)
    else:
        row, col = pixels // grid, pixels % grid
    right = col >= half
    place = jnp.where(pixels < 0, -1, jnp.where(right, row + grid, row))
    return place, jnp.where(right, col - half, col)


def swapped(value):
    half = value.shape[1] // 2
    return jnp.concatenate([value[:, half:], value[:, :half]], axis=1)


def fold(first, second):
    left = lax.broadcasted_iota(jnp.int32, first.shape, 1) < first.shape[1] // 2
    return jnp.where(left, first, swapped(second)), jnp.where(left, swapped(first), second)


def chunks(blocks):
    width = next(width for width in (8, 4, 2, 1) if blocks % width == 0)
    return [(start, width) for start in range(0, blocks, width)]


def lanes(array, start, width):
    return jnp.concatenate([array[start + k : start + k + 1] for k in range(width)], axis=1)


def hits(ids, span):
    return lax.broadcasted_iota(jnp.int32, (span, ids.shape[1]), 0) == ids


def one_hot(place, start, width, span):
    ids = lanes(place, start, width).astype(F32)
    rows = lax.broadcasted_iota(jnp.int32, (span, ids.shape[1]), 0).astype(F32)
    if span <= 256:
        ids, rows = ids.astype(BF16), rows.astype(BF16)
    one, zero = jnp.ones((), BF16), jnp.zeros((), BF16)
    return jnp.where(rows == ids, one, zero)


def fill(place, blocks, size, span, hot_ref):
    for start, width in chunks(blocks):
        hot_ref[:, start * size : (start + width) * size] = one_hot(place, start, width, span)


def kick(real, imag, phases, energy, pixels, read_ref, hot_ref=None, dark=None, turn=None):
    grid = real.shape[0]
    half = grid // 2
    blocks, size = phases.shape
    place, col = cells(pixels, grid)

    def read():
        upper, lower = fold(real, imag)
        low = jnp.concatenate([upper, lower], axis=0).astype(BF16)
        for start, width in chunks(blocks):
            where = slice(start * size, (start + width) * size)
            hot = hot_ref[:, where] if turn else one_hot(place, start, width, 2 * grid)
            if hot_ref is not None and not turn:
                hot_ref[:, where] = hot
            picked = dot(low, hot, 0, 0)
            col_hit = hits(lanes(col, start, width), half)
            for part in range(2):
                value = picked[part * half : (part + 1) * half]
                value = jnp.sum(jnp.where(col_hit, value, 0.0), axis=0, keepdims=True)
                for k in range(width):
                    read_ref[part, start + k : start + k + 1, :] = value[:, k * size : (k + 1) * size]

    if dark is None:
        read()
    else:
        pl.when(jnp.logical_not(dark))(read)

        @pl.when(dark)
        def _():
            read_ref[...] = jnp.zeros(read_ref.shape, F32)
            fill(place, blocks, size, 2 * grid, hot_ref)

    cosine, sine = turn or (jnp.cos(phases), jnp.sin(phases))
    read_real = read_ref[0, :blocks, :]
    read_imag = read_ref[1, :blocks, :]
    energy = energy - KICK_RATE * (read_real * cosine - read_imag * sine)
    return phases + PHASE_RATE * energy, energy


def emit(real, imag, phases, pixels, hot_ref, spread_ref, filled):
    grid = real.shape[0]
    half = grid // 2
    blocks, size = phases.shape
    place, col = cells(pixels, grid)
    weight_real = jnp.cos(phases)
    weight_imag = -jnp.sin(phases)
    for start, width in chunks(blocks):
        where = slice(start * size, (start + width) * size)
        if not filled:
            hot_ref[:, where] = one_hot(place, start, width, 2 * grid)
        col_hit = hits(lanes(col, start, width), half)
        for part, weight in ((0, weight_real), (1, weight_imag)):
            value = jnp.where(col_hit, lanes(weight, start, width), 0.0)
            spread_ref[part * half : (part + 1) * half, where] = value.astype(BF16)
    span = blocks * size
    source = dot(hot_ref[:, :span], spread_ref[:, :span], 1, 1)
    source_real, source_imag = fold(source[:grid], source[grid:])
    return real + EMIT_RATE * source_real, imag + EMIT_RATE * source_imag


def position():
    return lax.axis_index("cuts") * lax.axis_size("group") + lax.axis_index("group")


def kept_unless(index):
    return jnp.where(position() == index, 0.0, 1.0).astype(F32)


def kick_kernel(field_hbm, phases_hbm, energy_hbm, pixels_hbm, dest_hbm, out, field, phases, energy, pixels, dest, read_ref, hot_ref, sems):
    blocks, size = phases.shape
    pairs = ((pixels_hbm, pixels), (phases_hbm, phases), (energy_hbm, energy), (dest_hbm, dest), (field_hbm, field))
    copies = [pltpu.make_async_copy(source, target, sems.at[k]) for k, (source, target) in enumerate(pairs)]
    for copy in copies:
        copy.start()
    for copy in copies[:-1]:
        copy.wait()
    grid = field.shape[1]
    place, _ = cells(pixels[...], grid)
    fill(place, blocks, size, 2 * grid, hot_ref)
    turn = (jnp.cos(phases[...]), jnp.sin(phases[...]))
    square = (blocks, blocks)
    own = lax.broadcasted_iota(jnp.int32, square, 0) == lax.broadcasted_iota(jnp.int32, square, 1)
    goals = jnp.where(own, jnp.broadcast_to(dest[0:1, :].astype(F32), square), 0.0)
    out[3 * blocks : 4 * blocks, :] = jnp.broadcast_to(jnp.sum(goals, axis=1, keepdims=True), (blocks, size))
    out[2 * blocks : 3 * blocks, :] = pixels[...].astype(F32)
    copies[-1].wait()
    new_phases, new_energy = kick(
        field[0], field[1], phases[...], energy[...], pixels[...], read_ref, hot_ref, turn=turn
    )
    out[0:blocks, :] = new_phases
    out[blocks : 2 * blocks, :] = new_energy


def by_destination(kinds):
    goals = kinds[-1]
    blocks = goals.shape[0]
    place = lax.broadcasted_iota(jnp.int32, goals.shape, 0)
    rank = jnp.zeros(goals.shape, jnp.int32)
    for block in range(blocks):
        goal = goals[block : block + 1]
        ahead = (goal < goals) | ((goal == goals) & (place > block))
        rank = rank + jnp.where(ahead, 1, 0)
    ordered = [jnp.zeros(kind.shape, F32) for kind in kinds]
    for block in range(blocks):
        here = rank[block : block + 1] == place
        ordered = [jnp.where(here, kind[block : block + 1], old) for kind, old in zip(kinds, ordered)]
    return ordered


def lane_groups(values, shifts):
    size = values[0].shape[1]
    group = lax.broadcasted_iota(jnp.int32, values[0].shape, 1) // (size // len(values))
    joined_up = None
    for k, (value, shift) in enumerate(zip(values, shifts)):
        if shift % size:
            value = pltpu.roll(value, shift % size, axis=1)
        joined_up = value if joined_up is None else jnp.where(group == k, value, joined_up)
    return joined_up


def radiate(blocks, dropped, field, state, form, out, hot_ref, spread_ref):
    pixels = state[2 * blocks : 3 * blocks, :].astype(jnp.int32)
    real, imag = emit(field[0], field[1], state[0:blocks, :], pixels, hot_ref, spread_ref, False)
    real, imag = diffract(real, imag, *form)
    keep = kept_unless(dropped)
    out[0] = real * keep
    out[1] = imag * keep


def first_radiate_kernel(blocks, dropped, field, state, propagator, *rest):
    *rest, hot_ref, spread_ref = rest
    if len(rest) > 3:
        *tables, out, high, low, matrix = rest
        matrix[...] = filter_matrix(*tables)
    else:
        out, high, low = rest
    form = real_form(propagator)
    high[...], low[...] = form
    radiate(blocks, dropped, field, state, form, out, hot_ref, spread_ref)


def third_radiate_kernel(blocks, field, state, high, low, out, hot_ref, spread_ref):
    needed = position() > 1

    @pl.when(needed)
    def _():
        radiate(blocks, 1, field, state, (high[...], low[...]), out, hot_ref, spread_ref)

    @pl.when(jnp.logical_not(needed))
    def _():
        out[...] = jnp.zeros(out.shape, F32)


def second_kernel(count, rows, cap, field, state, high, low, out, *rest):
    sends = rest[:-3]
    read_ref, hot_ref, spread_ref = rest[-3:]
    blocks, size = state.shape[0] // 4, state.shape[1]
    real, imag = field[0], field[1]
    grid = real.shape[0]
    pixels = state[2 * blocks : 3 * blocks, :].astype(jnp.int32)
    dark = position() == count - 1
    phases, energy = kick(
        real, imag, state[0:blocks, :], state[blocks : 2 * blocks, :], pixels, read_ref, hot_ref, dark
    )
    kinds = by_destination((phases, energy, state[2 * blocks : 3 * blocks, :], state[3 * blocks : 4 * blocks, :]))
    if rows:
        pairs, pieces = rows // 2, len(kinds)
        tiles = 2 * pairs + 1
        width = size // pieces
        for chunk in range(blocks // cap):
            parts = [kind[chunk * cap : (chunk + 1) * cap] for kind in kinds]
            for piece in range(pieces):
                row = lane_groups(parts, [(k - piece) * width for k in range(pieces)])
                out[pl.ds((piece * cap + 1) * tiles - 1, cap, stride=tiles), chunk, :] = row
    else:
        cuts = len(sends)
        cut = lax.div(lax.rem(position() + 1, count), count // cuts)
        for ahead, send in enumerate(sends):
            wanted = lax.rem(cut + ahead, cuts).astype(F32)
            chunk = [jnp.zeros((cap, size), F32)] * 2 + [jnp.full((cap, size), -1.0, F32)]
            for start in range(0, blocks, cap):
                goes = kinds[3][start : start + cap] == wanted
                chunk = [jnp.where(goes, kind[start : start + cap], old) for kind, old in zip(kinds, chunk)]
            for kind in range(3):
                send[kind * cap : (kind + 1) * cap, :] = chunk[kind]
    real, imag = emit(real, imag, phases, pixels, hot_ref, spread_ref, True)
    real, imag = diffract(real, imag, high[...], low[...])
    keep = kept_unless(count - 2)
    real, imag = real * keep, imag * keep
    if rows:
        for part in range(grid // rows):
            for pair in range(pairs):
                first = part * rows + 2 * pair
                out[part * tiles + pair] = real[first : first + 2]
                out[part * tiles + pairs + pair] = imag[first : first + 2]
    else:
        out[0] = real
        out[1] = imag


def filter_matrix(transmit, cos_out, sin_out, cos_in, sin_in):
    gain_real, gain_imag = transmit[0:1, :], transmit[1:2, :]
    cosine, sine = cos_out[...], sin_out[...]
    real = cosine * gain_real - sine * gain_imag
    imag = cosine * gain_imag + sine * gain_real
    full_real = exact_dot(real, cos_in[...]) + exact_dot(imag, sin_in[...])
    full_imag = exact_dot(imag, cos_in[...]) - exact_dot(real, sin_in[...])
    form = jnp.concatenate(
        [
            jnp.concatenate([full_real, -full_imag], axis=1),
            jnp.concatenate([full_imag, full_real], axis=1),
        ],
        axis=0,
    )
    high, low = split(form)
    return jnp.concatenate([high, high, low], axis=1)


def filter_kernel(cuts, chunk_count, matrix, data, out):
    count = out.shape[0] // 3
    rows, size = out.shape[1:]
    groups = count // cuts
    pairs = rows // 2
    tiles = 2 * pairs + 1
    stacked = jnp.concatenate(
        [
            jnp.concatenate(
                [data[pl.ds(part * pairs + j // 2, count, stride=tiles), j % 2, :] for part in range(2)], axis=0
            )
            for j in range(rows)
        ],
        axis=1,
    )
    high, low = split(stacked)
    result = dot(matrix[...], jnp.concatenate([high, low, high], axis=0), 1, 0)
    for part in range(2):
        for j in range(rows):
            out[pl.ds(part, count, stride=3), j, :] = result[
                part * count : (part + 1) * count, j * size : (j + 1) * size
            ]
    bundles = [
        pltpu.roll(data[pl.ds(tiles - 1, count, stride=tiles), chunk, :], 1, axis=0)
        for chunk in range(chunk_count)
    ]
    goals = [bundle[:, size - 1 : size] for bundle in bundles]
    for cut in range(cuts):
        chosen = bundles[0]
        for bundle, goal in zip(bundles[1:], goals[1:]):
            chosen = jnp.where(goal == float(cut), bundle, chosen)
        first = cut * groups + 2
        fits = min(groups, count - first)
        for source in range(cuts):
            tile = chosen[source * groups : (source + 1) * groups]
            out[pl.ds(3 * first + 2, fits, stride=3), source, :] = tile[:fits]
            for k in range(fits, groups):
                out[3 * (first + k - count) + 2, source : source + 1, :] = tile[k : k + 1]


def joined(chunks_in):
    cap = chunks_in[0].shape[0] // 3
    kinds = [
        jnp.concatenate([chunk[kind * cap : (kind + 1) * cap, :] for chunk in chunks_in], axis=0)
        for kind in range(3)
    ]
    return kinds[0], kinds[1], kinds[2].astype(jnp.int32)


def relayed(fields, cuts):
    count = fields.shape[0] // 3
    size = fields.shape[2]
    width = size // KINDS
    bundles = [fields[pl.ds(2, count, stride=3), cut, :] for cut in range(cuts)]
    kinds = [lane_groups(bundles, [(cut - kind) * width for cut in range(cuts)]) for kind in range(KINDS)]
    wanted = lax.div(lax.rem(position() + (count - 2), count), count // cuts).astype(F32)
    return kinds[0], kinds[1], jnp.where(kinds[3] == wanted, kinds[2], -1.0).astype(jnp.int32)


def third_kernel(cuts, fields, *rest):
    out, state, read_ref = rest[-3:]
    chunks_in = rest[:-3]
    if chunks_in:
        phases, energy, pixels = joined(chunks_in)
        out[...] = fields[...]
    else:
        phases, energy, pixels = relayed(fields, cuts)
        rows = fields.shape[1]
        for part in range(fields.shape[0] // 3):
            for kind in range(2):
                out[kind, part * rows : (part + 1) * rows, :] = fields[3 * part + kind]
    phases, energy = kick(out[0], out[1], phases, energy, pixels, read_ref)
    blocks = phases.shape[0]
    state[0:blocks, :] = phases
    state[blocks : 2 * blocks, :] = energy
    state[2 * blocks : 3 * blocks, :] = pixels.astype(F32)


def fourth_kernel(field, state, high, low, out, read_ref, hot_ref, spread_ref):
    blocks = state.shape[0] // 3
    needed = position() > 0

    @pl.when(needed)
    def _():
        pixels = state[2 * blocks : 3 * blocks, :].astype(jnp.int32)
        real, imag = field[0], field[1]
        dark = position() == 1
        phases, _ = kick(
            real, imag, state[0:blocks, :], state[blocks : 2 * blocks, :], pixels, read_ref, hot_ref, dark
        )
        real, imag = emit(real, imag, phases, pixels, hot_ref, spread_ref, True)
        out[0], out[1] = diffract(real, imag, high[...], low[...])

    @pl.when(jnp.logical_not(needed))
    def _():
        out[...] = jnp.zeros(out.shape, F32)


def call(kernel, out_shape, scratch, flops, args, memory=pltpu.VMEM):
    specs = [pl.BlockSpec(memory_space=memory)] * len(args)
    return pl.pallas_call(
        kernel,
        out_shape=out_shape,
        in_specs=specs,
        out_specs=jax.tree.map(lambda _: pl.BlockSpec(memory_space=pltpu.VMEM), out_shape),
        scratch_shapes=scratch,
        compiler_params=pltpu.CompilerParams(vmem_limit_bytes=VMEM_LIMIT),
        cost_estimate=pl.CostEstimate(flops=flops, bytes_accessed=1 << 19, transcendentals=0),
    )(*args)


def time_tables(count):
    times = jnp.arange(count, dtype=jnp.int32)
    cos_out, sin_out = angle_table((times + (count - 4)) % count, times, count)
    return (cos_out / count, sin_out / count, *angle_table(times, times, count))


def angle_table(first_ids, second_ids, total_slices):
    product = first_ids[:, None] * second_ids[None, :] % total_slices
    angle = product.astype(F32) * (2.0 * math.pi / total_slices)
    return jnp.cos(angle), jnp.sin(angle)


def filter_any(field, transmit, count):
    grid = field.shape[1]
    span = grid * grid
    share = -(-span // count)
    flat = jnp.pad(field.reshape(2, span), ((0, 0), (0, share * count - span)))
    parts = flat.reshape(2, count, share).transpose(1, 0, 2)
    got = lax.all_to_all(parts, AXES, split_axis=0, concat_axis=0, tiled=True)
    got = jnp.roll(got, 2, axis=0)
    real, imag = got[:, 0], got[:, 1]
    times = jnp.arange(count, dtype=jnp.int32)
    cosine, sine = angle_table(times, times, count)
    spec_real = exact_dot(cosine, real) + exact_dot(sine, imag)
    spec_imag = exact_dot(cosine, imag) - exact_dot(sine, real)
    gain_real, gain_imag = transmit[0][:, None], transmit[1][:, None]
    shaped_real = gain_real * spec_real - gain_imag * spec_imag
    shaped_imag = gain_real * spec_imag + gain_imag * spec_real
    back_real = (exact_dot(cosine, shaped_real) - exact_dot(sine, shaped_imag)) / count
    back_imag = (exact_dot(cosine, shaped_imag) + exact_dot(sine, shaped_real)) / count
    back = jnp.stack([back_real, back_imag], axis=1)
    sent = jnp.roll(back, 2, axis=0)
    fields = lax.all_to_all(sent, AXES, split_axis=0, concat_axis=0, tiled=True)
    fields = fields.transpose(1, 0, 2).reshape(2, share * count)[:, :span]
    return fields.reshape(2, grid, grid)


def on_device(radiation, phases, energy, pixels, destination, propagator, transmit):
    cuts, groups = lax.axis_size("cuts"), lax.axis_size("group")
    count = cuts * groups
    grid = radiation.shape[-1]
    blocks, size = phases.shape[1:]
    cap = max(2, 2 * blocks // cuts)
    rows = grid // count if grid % count == 0 else 0
    if rows != 4 or cap * KINDS != count or cuts != KINDS or size % 128 or blocks != 2 * cap or groups % 8:
        rows = 0
    field = radiation[0]
    shape = lambda *dims: jax.ShapeDtypeStruct(dims, F32)
    read = lambda number: pltpu.VMEM((2, number, size), F32)
    hot = lambda number: [pltpu.VMEM((2 * grid, number * size), BF16), pltpu.VMEM((grid, number * size), BF16)]
    pass_flops = 4 * blocks * size * grid * grid
    prop_flops = 48 * grid**3

    given = (field, phases[0], energy[0], pixels[0], destination)
    state = call(
        kick_kernel, shape(4 * blocks, size),
        [
            pltpu.VMEM((2, grid, grid), F32),
            pltpu.VMEM((blocks, size), F32),
            pltpu.VMEM((blocks, size), F32),
            pltpu.VMEM((blocks, size), jnp.int32),
            pltpu.VMEM((1, blocks), jnp.int32),
            read(blocks),
            hot(blocks)[0],
            pltpu.SemaphoreType.DMA((5,)),
        ],
        pass_flops, tuple(pltpu.with_memory_space_constraint(value, pltpu.HBM) for value in given), pl.ANY,
    )
    route = [((i + 1) % count, i) for i in range(count)]
    behind = lax.ppermute(state, AXES, route)
    form_shape = jax.ShapeDtypeStruct((2 * grid, 2 * grid), BF16)
    made = [shape(2, grid, grid), form_shape, form_shape]
    tables = ()
    if rows:
        made.append(jax.ShapeDtypeStruct((2 * count, 6 * count), BF16))
        tables = (transmit, *time_tables(count))
    field, *form = call(
        functools.partial(first_radiate_kernel, blocks, count - 1), made, hot(blocks), pass_flops + prop_flops,
        (field, state, propagator, *tables),
    )
    matrix = form[2:]
    form = form[:2]
    part_shape = shape(count * (rows + 1), 2, grid) if rows else shape(2, grid, grid)
    send_shapes = [] if rows else [shape(3 * cap, size)] * cuts
    field, *sends = call(
        functools.partial(second_kernel, count, rows, cap), (part_shape, *send_shapes),
        [read(blocks)] + hot(blocks), 2 * pass_flops + prop_flops,
        (field, behind, *form),
    )
    chunks_in = [
        lax.ppermute(send, AXES, [(i, (i + 3 + groups * ahead) % count) for i in range(count)])
        for ahead, send in enumerate(sends)
    ]
    if rows:
        data = lax.all_to_all(field, AXES, split_axis=0, concat_axis=0, tiled=True)
        sent = call(
            functools.partial(filter_kernel, cuts, blocks // cap), shape(count * 3, rows, grid), [], 1 << 24,
            (*matrix, data),
        )
        fields = lax.all_to_all(sent, AXES, split_axis=0, concat_axis=0, tiled=True)
    else:
        fields = filter_any(field, transmit, count)
    capacity = cuts * cap
    share = capacity // blocks
    field, state = call(
        functools.partial(third_kernel, cuts), (shape(2, grid, grid), shape(3 * capacity, size)),
        [read(capacity)], share * pass_flops, (fields, *chunks_in),
    )
    behind = lax.ppermute(state, AXES, route)
    field = call(
        functools.partial(third_radiate_kernel, capacity), shape(2, grid, grid), hot(capacity),
        share * pass_flops + prop_flops, (field, state, *form),
    )
    out = call(
        fourth_kernel, shape(2, grid, grid), [read(capacity)] + hot(capacity),
        2 * share * pass_flops + prop_flops, (field, behind, *form),
    )
    return out[None]


def solution(mesh):
    return jax.shard_map(
        on_device,
        mesh=mesh,
        in_specs=(
            P(("cuts", "group"), None, None, None),
            P(("cuts", "group"), None, None),
            P(("cuts", "group"), None, None),
            P(("cuts", "group"), None, None),
            P(("cuts", "group"), None),
            P(),
            P(),
        ),
        out_specs=P(("cuts", "group"), None, None, None),
        check_vma=False,
    )
```

```python
import functools
import math

import jax
import jax.numpy as jnp
from jax import lax
from jax.experimental import pallas as pl
from jax.experimental.pallas import tpu as pltpu
from jax.sharding import PartitionSpec as P

KICK_RATE = 0.5
PHASE_RATE = 1.0
EMIT_RATE = 0.5

AXES = ("cuts", "group")
F32 = jnp.float32
BF16 = jnp.bfloat16
KINDS = 4
VMEM_LIMIT = 48 * 1024 * 1024


def dot(left, right, left_dim, right_dim):
    dims = (((left_dim,), (right_dim,)), ((), ()))
    return lax.dot_general(left, right, dims, preferred_element_type=F32)


def exact_dot(left, right):
    return jnp.dot(left, right, precision=lax.Precision.HIGHEST, preferred_element_type=F32)


def split(value):
    high = value.astype(BF16)
    return high, (value - high.astype(F32)).astype(BF16)


def real_form(propagator):
    prop_real, prop_imag = propagator[0], propagator[1]
    form = jnp.concatenate(
        [
            jnp.concatenate([prop_real, -prop_imag], axis=1),
            jnp.concatenate([prop_imag, prop_real], axis=1),
        ],
        axis=0,
    )
    return split(form)


def diffract(real, imag, form_high, form_low):
    size = real.shape[0]
    high, low = split(jnp.concatenate([real, imag], axis=1))
    both = dot(jnp.concatenate([high, low], axis=0), form_high, 1, 1)
    right = both[:size] + both[size:] + dot(high, form_low, 1, 1)
    high, low = split(jnp.concatenate([right[:, :size], right[:, size:]], axis=0))
    both = dot(form_high, jnp.concatenate([high, low], axis=1), 1, 0)
    out = both[:, :size] + both[:, size:] + dot(form_low, high, 1, 0)
    return out[:size], out[size:]


def cells(pixels, grid):
    half = grid // 2
    shift = grid.bit_length() - 1
    if grid == 1 << shift:
        row, col = lax.shift_right_arithmetic(pixels, shift), pixels & (grid - 1)
    else:
        row, col = pixels // grid, pixels % grid
    right = col >= half
    place = jnp.where(pixels < 0, -1, jnp.where(right, row + grid, row))
    return place, jnp.where(right, col - half, col)


def swapped(value):
    half = value.shape[1] // 2
    return jnp.concatenate([value[:, half:], value[:, :half]], axis=1)


def fold(first, second):
    left = lax.broadcasted_iota(jnp.int32, first.shape, 1) < first.shape[1] // 2
    return jnp.where(left, first, swapped(second)), jnp.where(left, swapped(first), second)


def chunks(blocks):
    width = next(width for width in (4, 2, 1) if blocks % width == 0)
    return [(start, width) for start in range(0, blocks, width)]


def lanes(array, start, width):
    return jnp.concatenate([array[start + k : start + k + 1] for k in range(width)], axis=1)


def hits(ids, span):
    return lax.broadcasted_iota(jnp.int32, (span, ids.shape[1]), 0) == ids


def one_hot(place, start, width, span):
    ids = lanes(place, start, width).astype(F32)
    rows = lax.broadcasted_iota(jnp.int32, (span, ids.shape[1]), 0).astype(F32)
    if span <= 256:
        ids, rows = ids.astype(BF16), rows.astype(BF16)
    one, zero = jnp.ones((), BF16), jnp.zeros((), BF16)
    return jnp.where(rows == ids, one, zero)


def fill(place, blocks, size, span, hot_ref):
    for start, width in chunks(blocks):
        hot_ref[:, start * size : (start + width) * size] = one_hot(place, start, width, span)


def kick(real, imag, phases, energy, pixels, read_ref, hot_ref=None, dark=None, turn=None):
    grid = real.shape[0]
    half = grid // 2
    blocks, size = phases.shape
    place, col = cells(pixels, grid)

    def read():
        upper, lower = fold(real, imag)
        low = jnp.concatenate([upper, lower], axis=0).astype(BF16)
        for start, width in chunks(blocks):
            where = slice(start * size, (start + width) * size)
            hot = hot_ref[:, where] if turn else one_hot(place, start, width, 2 * grid)
            if hot_ref is not None and not turn:
                hot_ref[:, where] = hot
            picked = dot(low, hot, 0, 0)
            col_hit = hits(lanes(col, start, width), half)
            for part in range(2):
                value = picked[part * half : (part + 1) * half]
                value = jnp.sum(jnp.where(col_hit, value, 0.0), axis=0, keepdims=True)
                for k in range(width):
                    read_ref[part, start + k : start + k + 1, :] = value[:, k * size : (k + 1) * size]

    if dark is None:
        read()
    else:
        pl.when(jnp.logical_not(dark))(read)

        @pl.when(dark)
        def _():
            read_ref[...] = jnp.zeros(read_ref.shape, F32)
            fill(place, blocks, size, 2 * grid, hot_ref)

    cosine, sine = turn or (jnp.cos(phases), jnp.sin(phases))
    read_real = read_ref[0, :blocks, :]
    read_imag = read_ref[1, :blocks, :]
    energy = energy - KICK_RATE * (read_real * cosine - read_imag * sine)
    return phases + PHASE_RATE * energy, energy


def emit(real, imag, phases, pixels, hot_ref, spread_ref, filled):
    grid = real.shape[0]
    half = grid // 2
    blocks, size = phases.shape
    place, col = cells(pixels, grid)
    weight_real = jnp.cos(phases)
    weight_imag = -jnp.sin(phases)
    for start, width in chunks(blocks):
        where = slice(start * size, (start + width) * size)
        if not filled:
            hot_ref[:, where] = one_hot(place, start, width, 2 * grid)
        col_ids = lanes(col, start, width).astype(F32)
        col_rows = lax.broadcasted_iota(jnp.int32, (half, col_ids.shape[1]), 0).astype(F32)
        if half <= 256:
            col_ids, col_rows = col_ids.astype(BF16), col_rows.astype(BF16)
        col_hit = col_rows == col_ids
        for part, weight in ((0, weight_real), (1, weight_imag)):
            value = lanes(weight, start, width).astype(BF16)
            value = jnp.where(col_hit, value, jnp.zeros((), BF16))
            spread_ref[part * half : (part + 1) * half, where] = value
    span = blocks * size
    source = dot(hot_ref[:, :span], spread_ref[:, :span], 1, 1)
    source_real, source_imag = fold(source[:grid], source[grid:])
    return real + EMIT_RATE * source_real, imag + EMIT_RATE * source_imag


def position():
    return lax.axis_index("cuts") * lax.axis_size("group") + lax.axis_index("group")


def kept_unless(index):
    return jnp.where(position() == index, 0.0, 1.0).astype(F32)


def kick_kernel(field_hbm, phases_hbm, energy_hbm, pixels_hbm, dest_hbm, out, field, phases, energy, pixels, dest, read_ref, hot_ref, sems):
    blocks, size = phases.shape
    pairs = ((pixels_hbm, pixels), (phases_hbm, phases), (energy_hbm, energy), (dest_hbm, dest), (field_hbm, field))
    copies = [pltpu.make_async_copy(source, target, sems.at[k]) for k, (source, target) in enumerate(pairs)]
    for copy in copies:
        copy.start()
    for copy in copies[:-1]:
        copy.wait()
    grid = field.shape[1]
    place, _ = cells(pixels[...], grid)
    fill(place, blocks, size, 2 * grid, hot_ref)
    turn = (jnp.cos(phases[...]), jnp.sin(phases[...]))
    square = (blocks, blocks)
    own = lax.broadcasted_iota(jnp.int32, square, 0) == lax.broadcasted_iota(jnp.int32, square, 1)
    goals = jnp.where(own, jnp.broadcast_to(dest[0:1, :].astype(F32), square), 0.0)
    out[3 * blocks : 4 * blocks, :] = jnp.broadcast_to(jnp.sum(goals, axis=1, keepdims=True), (blocks, size))
    out[2 * blocks : 3 * blocks, :] = pixels[...].astype(F32)
    copies[-1].wait()
    new_phases, new_energy = kick(
        field[0], field[1], phases[...], energy[...], pixels[...], read_ref, hot_ref, turn=turn
    )
    out[0:blocks, :] = new_phases
    out[blocks : 2 * blocks, :] = new_energy


def by_destination(kinds):
    goals = kinds[-1]
    blocks = goals.shape[0]
    place = lax.broadcasted_iota(jnp.int32, goals.shape, 0)
    rank = jnp.zeros(goals.shape, jnp.int32)
    for block in range(blocks):
        goal = goals[block : block + 1]
        ahead = (goal < goals) | ((goal == goals) & (place > block))
        rank = rank + jnp.where(ahead, 1, 0)
    ordered = [jnp.zeros(kind.shape, F32) for kind in kinds]
    for block in range(blocks):
        here = rank[block : block + 1] == place
        ordered = [jnp.where(here, kind[block : block + 1], old) for kind, old in zip(kinds, ordered)]
    return ordered


def lane_groups(values, shifts):
    size = values[0].shape[1]
    group = lax.broadcasted_iota(jnp.int32, values[0].shape, 1) // (size // len(values))
    joined_up = None
    for k, (value, shift) in enumerate(zip(values, shifts)):
        if shift % size:
            value = pltpu.roll(value, shift % size, axis=1)
        joined_up = value if joined_up is None else jnp.where(group == k, value, joined_up)
    return joined_up


def radiate(blocks, dropped, field, state, form, out, hot_ref, spread_ref):
    pixels = state[2 * blocks : 3 * blocks, :].astype(jnp.int32)
    real, imag = emit(field[0], field[1], state[0:blocks, :], pixels, hot_ref, spread_ref, False)
    real, imag = diffract(real, imag, *form)
    keep = kept_unless(dropped)
    out[0] = real * keep
    out[1] = imag * keep


def first_radiate_kernel(blocks, dropped, field, state, propagator, *rest):
    *rest, hot_ref, spread_ref = rest
    if len(rest) > 3:
        *tables, out, high, low, matrix = rest
        matrix[...] = filter_matrix(*tables)
    else:
        out, high, low = rest
    form = real_form(propagator)
    high[...], low[...] = form
    radiate(blocks, dropped, field, state, form, out, hot_ref, spread_ref)


def third_radiate_kernel(blocks, field, state, high, low, out, hot_ref, spread_ref):
    needed = position() > 1

    @pl.when(needed)
    def _():
        radiate(blocks, 1, field, state, (high[...], low[...]), out, hot_ref, spread_ref)

    @pl.when(jnp.logical_not(needed))
    def _():
        out[...] = jnp.zeros(out.shape, F32)


def second_kernel(count, rows, cap, field, state, high, low, out, *rest):
    sends = rest[:-3]
    read_ref, hot_ref, spread_ref = rest[-3:]
    blocks, size = state.shape[0] // 4, state.shape[1]
    real, imag = field[0], field[1]
    grid = real.shape[0]
    pixels = state[2 * blocks : 3 * blocks, :].astype(jnp.int32)
    dark = position() == count - 1
    phases, energy = kick(
        real, imag, state[0:blocks, :], state[blocks : 2 * blocks, :], pixels, read_ref, hot_ref, dark
    )
    kinds = by_destination((phases, energy, state[2 * blocks : 3 * blocks, :], state[3 * blocks : 4 * blocks, :]))
    if rows:
        pairs, pieces = rows // 2, len(kinds)
        tiles = 2 * pairs + 1
        width = size // pieces
        for chunk in range(blocks // cap):
            parts = [kind[chunk * cap : (chunk + 1) * cap] for kind in kinds]
            for piece in range(pieces):
                row = lane_groups(parts, [(k - piece) * width for k in range(pieces)])
                out[pl.ds((piece * cap + 1) * tiles - 1, cap, stride=tiles), chunk, :] = row
    else:
        cuts = len(sends)
        cut = lax.div(lax.rem(position() + 1, count), count // cuts)
        for ahead, send in enumerate(sends):
            wanted = lax.rem(cut + ahead, cuts).astype(F32)
            chunk = [jnp.zeros((cap, size), F32)] * 2 + [jnp.full((cap, size), -1.0, F32)]
            for start in range(0, blocks, cap):
                goes = kinds[3][start : start + cap] == wanted
                chunk = [jnp.where(goes, kind[start : start + cap], old) for kind, old in zip(kinds, chunk)]
            for kind in range(3):
                send[kind * cap : (kind + 1) * cap, :] = chunk[kind]
    real, imag = emit(real, imag, phases, pixels, hot_ref, spread_ref, True)
    real, imag = diffract(real, imag, high[...], low[...])
    keep = kept_unless(count - 2)
    real, imag = real * keep, imag * keep
    if rows:
        for part in range(grid // rows):
            for pair in range(pairs):
                first = part * rows + 2 * pair
                out[part * tiles + pair] = real[first : first + 2]
                out[part * tiles + pairs + pair] = imag[first : first + 2]
    else:
        out[0] = real
        out[1] = imag


def filter_matrix(transmit, cos_out, sin_out, cos_in, sin_in):
    gain_real, gain_imag = transmit[0:1, :], transmit[1:2, :]
    cosine, sine = cos_out[...], sin_out[...]
    real = cosine * gain_real - sine * gain_imag
    imag = cosine * gain_imag + sine * gain_real
    full_real = exact_dot(real, cos_in[...]) + exact_dot(imag, sin_in[...])
    full_imag = exact_dot(imag, cos_in[...]) - exact_dot(real, sin_in[...])
    form = jnp.concatenate(
        [
            jnp.concatenate([full_real, -full_imag], axis=1),
            jnp.concatenate([full_imag, full_real], axis=1),
        ],
        axis=0,
    )
    high, low = split(form)
    return jnp.concatenate([high, high, low], axis=1)


def filter_kernel(cuts, chunk_count, matrix, data, out):
    count = out.shape[0] // 3
    rows, size = out.shape[1:]
    groups = count // cuts
    pairs = rows // 2
    tiles = 2 * pairs + 1
    stacked = jnp.concatenate(
        [
            jnp.concatenate(
                [data[pl.ds(part * pairs + j // 2, count, stride=tiles), j % 2, :] for part in range(2)], axis=0
            )
            for j in range(rows)
        ],
        axis=1,
    )
    high, low = split(stacked)
    result = dot(matrix[...], jnp.concatenate([high, low, high], axis=0), 1, 0)
    for part in range(2):
        for j in range(rows):
            out[pl.ds(part, count, stride=3), j, :] = result[
                part * count : (part + 1) * count, j * size : (j + 1) * size
            ]
    bundles = [
        pltpu.roll(data[pl.ds(tiles - 1, count, stride=tiles), chunk, :], 1, axis=0)
        for chunk in range(chunk_count)
    ]
    goals = [bundle[:, size - 1 : size] for bundle in bundles]
    for cut in range(cuts):
        chosen = bundles[0]
        for bundle, goal in zip(bundles[1:], goals[1:]):
            chosen = jnp.where(goal == float(cut), bundle, chosen)
        first = cut * groups + 2
        fits = min(groups, count - first)
        for source in range(cuts):
            tile = chosen[source * groups : (source + 1) * groups]
            out[pl.ds(3 * first + 2, fits, stride=3), source, :] = tile[:fits]
            for k in range(fits, groups):
                out[3 * (first + k - count) + 2, source : source + 1, :] = tile[k : k + 1]


def joined(chunks_in):
    cap = chunks_in[0].shape[0] // 3
    kinds = [
        jnp.concatenate([chunk[kind * cap : (kind + 1) * cap, :] for chunk in chunks_in], axis=0)
        for kind in range(3)
    ]
    return kinds[0], kinds[1], kinds[2].astype(jnp.int32)


def relayed(fields, cuts):
    count = fields.shape[0] // 3
    size = fields.shape[2]
    width = size // KINDS
    bundles = [fields[pl.ds(2, count, stride=3), cut, :] for cut in range(cuts)]
    kinds = [lane_groups(bundles, [(cut - kind) * width for cut in range(cuts)]) for kind in range(KINDS)]
    wanted = lax.div(lax.rem(position() + (count - 2), count), count // cuts).astype(F32)
    return kinds[0], kinds[1], jnp.where(kinds[3] == wanted, kinds[2], -1.0).astype(jnp.int32)


def third_kernel(cuts, fields, *rest):
    out, state, read_ref = rest[-3:]
    chunks_in = rest[:-3]
    if chunks_in:
        phases, energy, pixels = joined(chunks_in)
        out[...] = fields[...]
    else:
        phases, energy, pixels = relayed(fields, cuts)
        rows = fields.shape[1]
        for part in range(fields.shape[0] // 3):
            for kind in range(2):
                out[kind, part * rows : (part + 1) * rows, :] = fields[3 * part + kind]
    phases, energy = kick(out[0], out[1], phases, energy, pixels, read_ref)
    blocks = phases.shape[0]
    state[0:blocks, :] = phases
    state[blocks : 2 * blocks, :] = energy
    state[2 * blocks : 3 * blocks, :] = pixels.astype(F32)


def fourth_kernel(field, state, high, low, out, read_ref, hot_ref, spread_ref):
    blocks = state.shape[0] // 3
    needed = position() > 0

    @pl.when(needed)
    def _():
        pixels = state[2 * blocks : 3 * blocks, :].astype(jnp.int32)
        real, imag = field[0], field[1]
        dark = position() == 1
        phases, _ = kick(
            real, imag, state[0:blocks, :], state[blocks : 2 * blocks, :], pixels, read_ref, hot_ref, dark
        )
        real, imag = emit(real, imag, phases, pixels, hot_ref, spread_ref, True)
        out[0], out[1] = diffract(real, imag, high[...], low[...])

    @pl.when(jnp.logical_not(needed))
    def _():
        out[...] = jnp.zeros(out.shape, F32)


def call(kernel, out_shape, scratch, flops, args, memory=pltpu.VMEM):
    specs = [pl.BlockSpec(memory_space=memory)] * len(args)
    return pl.pallas_call(
        kernel,
        out_shape=out_shape,
        in_specs=specs,
        out_specs=jax.tree.map(lambda _: pl.BlockSpec(memory_space=pltpu.VMEM), out_shape),
        scratch_shapes=scratch,
        compiler_params=pltpu.CompilerParams(vmem_limit_bytes=VMEM_LIMIT),
        cost_estimate=pl.CostEstimate(flops=flops, bytes_accessed=1 << 19, transcendentals=0),
    )(*args)


def time_tables(count):
    times = jnp.arange(count, dtype=jnp.int32)
    cos_out, sin_out = angle_table((times + (count - 4)) % count, times, count)
    return (cos_out / count, sin_out / count, *angle_table(times, times, count))


def angle_table(first_ids, second_ids, total_slices):
    product = first_ids[:, None] * second_ids[None, :] % total_slices
    angle = product.astype(F32) * (2.0 * math.pi / total_slices)
    return jnp.cos(angle), jnp.sin(angle)


def filter_any(field, transmit, count):
    grid = field.shape[1]
    span = grid * grid
    share = -(-span // count)
    flat = jnp.pad(field.reshape(2, span), ((0, 0), (0, share * count - span)))
    parts = flat.reshape(2, count, share).transpose(1, 0, 2)
    got = lax.all_to_all(parts, AXES, split_axis=0, concat_axis=0, tiled=True)
    got = jnp.roll(got, 2, axis=0)
    real, imag = got[:, 0], got[:, 1]
    times = jnp.arange(count, dtype=jnp.int32)
    cosine, sine = angle_table(times, times, count)
    spec_real = exact_dot(cosine, real) + exact_dot(sine, imag)
    spec_imag = exact_dot(cosine, imag) - exact_dot(sine, real)
    gain_real, gain_imag = transmit[0][:, None], transmit[1][:, None]
    shaped_real = gain_real * spec_real - gain_imag * spec_imag
    shaped_imag = gain_real * spec_imag + gain_imag * spec_real
    back_real = (exact_dot(cosine, shaped_real) - exact_dot(sine, shaped_imag)) / count
    back_imag = (exact_dot(cosine, shaped_imag) + exact_dot(sine, shaped_real)) / count
    back = jnp.stack([back_real, back_imag], axis=1)
    sent = jnp.roll(back, 2, axis=0)
    fields = lax.all_to_all(sent, AXES, split_axis=0, concat_axis=0, tiled=True)
    fields = fields.transpose(1, 0, 2).reshape(2, share * count)[:, :span]
    return fields.reshape(2, grid, grid)


def on_device(radiation, phases, energy, pixels, destination, propagator, transmit):
    cuts, groups = lax.axis_size("cuts"), lax.axis_size("group")
    count = cuts * groups
    grid = radiation.shape[-1]
    blocks, size = phases.shape[1:]
    cap = max(2, 2 * blocks // cuts)
    rows = grid // count if grid % count == 0 else 0
    if rows != 4 or cap * KINDS != count or cuts != KINDS or size % 128 or blocks != 2 * cap or groups % 8:
        rows = 0
    field = radiation[0]
    shape = lambda *dims: jax.ShapeDtypeStruct(dims, F32)
    read = lambda number: pltpu.VMEM((2, number, size), F32)
    hot = lambda number: [pltpu.VMEM((2 * grid, number * size), BF16), pltpu.VMEM((grid, number * size), BF16)]
    pass_flops = 4 * blocks * size * grid * grid
    prop_flops = 48 * grid**3

    given = (field, phases[0], energy[0], pixels[0], destination)
    state = call(
        kick_kernel, shape(4 * blocks, size),
        [
            pltpu.VMEM((2, grid, grid), F32),
            pltpu.VMEM((blocks, size), F32),
            pltpu.VMEM((blocks, size), F32),
            pltpu.VMEM((blocks, size), jnp.int32),
            pltpu.VMEM((1, blocks), jnp.int32),
            read(blocks),
            hot(blocks)[0],
            pltpu.SemaphoreType.DMA((5,)),
        ],
        pass_flops, tuple(pltpu.with_memory_space_constraint(value, pltpu.HBM) for value in given), pl.ANY,
    )
    route = [((i + 1) % count, i) for i in range(count)]
    behind = lax.ppermute(state, AXES, route)
    form_shape = jax.ShapeDtypeStruct((2 * grid, 2 * grid), BF16)
    made = [shape(2, grid, grid), form_shape, form_shape]
    tables = ()
    if rows:
        made.append(jax.ShapeDtypeStruct((2 * count, 6 * count), BF16))
        tables = (transmit, *time_tables(count))
    field, *form = call(
        functools.partial(first_radiate_kernel, blocks, count - 1), made, hot(blocks), pass_flops + prop_flops,
        (field, state, propagator, *tables),
    )
    matrix = form[2:]
    form = form[:2]
    part_shape = shape(count * (rows + 1), 2, grid) if rows else shape(2, grid, grid)
    send_shapes = [] if rows else [shape(3 * cap, size)] * cuts
    field, *sends = call(
        functools.partial(second_kernel, count, rows, cap), (part_shape, *send_shapes),
        [read(blocks)] + hot(blocks), 2 * pass_flops + prop_flops,
        (field, behind, *form),
    )
    chunks_in = [
        lax.ppermute(send, AXES, [(i, (i + 3 + groups * ahead) % count) for i in range(count)])
        for ahead, send in enumerate(sends)
    ]
    if rows:
        data = lax.all_to_all(field, AXES, split_axis=0, concat_axis=0, tiled=True)
        sent = call(
            functools.partial(filter_kernel, cuts, blocks // cap), shape(count * 3, rows, grid), [], 1 << 24,
            (*matrix, data),
        )
        fields = lax.all_to_all(sent, AXES, split_axis=0, concat_axis=0, tiled=True)
    else:
        fields = filter_any(field, transmit, count)
    capacity = cuts * cap
    share = capacity // blocks
    field, state = call(
        functools.partial(third_kernel, cuts), (shape(2, grid, grid), shape(3 * capacity, size)),
        [read(capacity)], share * pass_flops, (fields, *chunks_in),
    )
    behind = lax.ppermute(state, AXES, route)
    field = call(
        functools.partial(third_radiate_kernel, capacity), shape(2, grid, grid), hot(capacity),
        share * pass_flops + prop_flops, (field, state, *form),
    )
    out = call(
        fourth_kernel, shape(2, grid, grid), [read(capacity)] + hot(capacity),
        2 * share * pass_flops + prop_flops, (field, behind, *form),
    )
    return out[None]


def solution(mesh):
    return jax.shard_map(
        on_device,
        mesh=mesh,
        in_specs=(
            P(("cuts", "group"), None, None, None),
            P(("cuts", "group"), None, None),
            P(("cuts", "group"), None, None),
            P(("cuts", "group"), None, None),
            P(("cuts", "group"), None),
            P(),
            P(),
        ),
        out_specs=P(("cuts", "group"), None, None, None),
        check_vma=False,
    )
```

```python
import functools
import math

import jax
import jax.numpy as jnp
from jax import lax
from jax.experimental import pallas as pl
from jax.experimental.pallas import tpu as pltpu
from jax.sharding import PartitionSpec as P

KICK_RATE = 0.5
PHASE_RATE = 1.0
EMIT_RATE = 0.5

AXES = ("cuts", "group")
F32 = jnp.float32
BF16 = jnp.bfloat16
KINDS = 4
VMEM_LIMIT = 48 * 1024 * 1024


def dot(left, right, left_dim, right_dim):
    dims = (((left_dim,), (right_dim,)), ((), ()))
    return lax.dot_general(left, right, dims, preferred_element_type=F32)


def exact_dot(left, right):
    return jnp.dot(left, right, precision=lax.Precision.HIGHEST, preferred_element_type=F32)


def split(value):
    high = value.astype(BF16)
    return high, (value - high.astype(F32)).astype(BF16)


def real_form(propagator):
    prop_real, prop_imag = propagator[0], propagator[1]
    form = jnp.concatenate(
        [
            jnp.concatenate([prop_real, -prop_imag], axis=1),
            jnp.concatenate([prop_imag, prop_real], axis=1),
        ],
        axis=0,
    )
    return split(jnp.concatenate([form, form.T], axis=0))


def diffract(real, imag, form_high, form_low):
    size = real.shape[0]
    high, low = split(jnp.concatenate([real, imag], axis=1))
    form_high, turned_high = form_high[: 2 * size], form_high[2 * size :]
    form_low, turned_low = form_low[: 2 * size], form_low[2 * size :]
    both = dot(jnp.concatenate([high, low], axis=0), turned_high, 1, 0)
    right = both[:size] + both[size:] + dot(high, turned_low, 1, 0)
    high, low = split(jnp.concatenate([right[:, :size], right[:, size:]], axis=0))
    both = dot(form_high, jnp.concatenate([high, low], axis=1), 1, 0)
    out = both[:, :size] + both[:, size:] + dot(form_low, high, 1, 0)
    return out[:size], out[size:]


def cells(pixels, grid):
    half = grid // 2
    shift = grid.bit_length() - 1
    if grid == 1 << shift:
        row, col = lax.shift_right_arithmetic(pixels, shift), pixels & (grid - 1)
    else:
        row, col = pixels // grid, pixels % grid
    right = col >= half
    place = jnp.where(pixels < 0, -1, jnp.where(right, row + grid, row))
    return place, jnp.where(right, col - half, col)


def swapped(value):
    half = value.shape[1] // 2
    return jnp.concatenate([value[:, half:], value[:, :half]], axis=1)


def fold(first, second):
    left = lax.broadcasted_iota(jnp.int32, first.shape, 1) < first.shape[1] // 2
    return jnp.where(left, first, swapped(second)), jnp.where(left, swapped(first), second)


def chunks(blocks):
    width = next(width for width in (4, 2, 1) if blocks % width == 0)
    return [(start, width) for start in range(0, blocks, width)]


def lanes(array, start, width):
    return jnp.concatenate([array[start + k : start + k + 1] for k in range(width)], axis=1)


def hits(ids, span):
    return lax.broadcasted_iota(jnp.int32, (span, ids.shape[1]), 0) == ids


def one_hot(place, start, width, span):
    ids = lanes(place, start, width).astype(F32)
    rows = lax.broadcasted_iota(jnp.int32, (span, ids.shape[1]), 0).astype(F32)
    if span <= 256:
        ids, rows = ids.astype(BF16), rows.astype(BF16)
    one, zero = jnp.ones((), BF16), jnp.zeros((), BF16)
    return jnp.where(rows == ids, one, zero)


def fill(place, blocks, size, span, hot_ref):
    for start, width in chunks(blocks):
        hot_ref[:, start * size : (start + width) * size] = one_hot(place, start, width, span)


def kick(real, imag, phases, energy, pixels, read_ref, hot_ref=None, dark=None, turn=None):
    grid = real.shape[0]
    half = grid // 2
    blocks, size = phases.shape
    place, col = cells(pixels, grid)

    def read():
        upper, lower = fold(real, imag)
        low = jnp.concatenate([upper, lower], axis=0).astype(BF16)
        for start, width in chunks(blocks):
            where = slice(start * size, (start + width) * size)
            hot = hot_ref[:, where] if turn else one_hot(place, start, width, 2 * grid)
            if hot_ref is not None and not turn:
                hot_ref[:, where] = hot
            picked = dot(low, hot, 0, 0)
            col_hit = hits(lanes(col, start, width), half)
            for part in range(2):
                value = picked[part * half : (part + 1) * half]
                value = jnp.sum(jnp.where(col_hit, value, 0.0), axis=0, keepdims=True)
                for k in range(width):
                    read_ref[part, start + k : start + k + 1, :] = value[:, k * size : (k + 1) * size]

    if dark is None:
        read()
    else:
        pl.when(jnp.logical_not(dark))(read)

        @pl.when(dark)
        def _():
            read_ref[...] = jnp.zeros(read_ref.shape, F32)
            fill(place, blocks, size, 2 * grid, hot_ref)

    cosine, sine = turn or (jnp.cos(phases), jnp.sin(phases))
    read_real = read_ref[0, :blocks, :]
    read_imag = read_ref[1, :blocks, :]
    energy = energy - KICK_RATE * (read_real * cosine - read_imag * sine)
    return phases + PHASE_RATE * energy, energy


def emit(real, imag, phases, pixels, hot_ref, spread_ref, filled):
    grid = real.shape[0]
    half = grid // 2
    blocks, size = phases.shape
    place, col = cells(pixels, grid)
    weight_real = jnp.cos(phases)
    weight_imag = -jnp.sin(phases)
    for start, width in chunks(blocks):
        where = slice(start * size, (start + width) * size)
        if not filled:
            hot_ref[:, where] = one_hot(place, start, width, 2 * grid)
        col_hit = hits(lanes(col, start, width), half)
        for part, weight in ((0, weight_real), (1, weight_imag)):
            value = jnp.where(col_hit, lanes(weight, start, width), 0.0)
            spread_ref[part * half : (part + 1) * half, where] = value.astype(BF16)
    span = blocks * size
    source = dot(hot_ref[:, :span], spread_ref[:, :span], 1, 1)
    source_real, source_imag = fold(source[:grid], source[grid:])
    return real + EMIT_RATE * source_real, imag + EMIT_RATE * source_imag


def position():
    return lax.axis_index("cuts") * lax.axis_size("group") + lax.axis_index("group")


def kept_unless(index):
    return jnp.where(position() == index, 0.0, 1.0).astype(F32)


def kick_kernel(field_hbm, phases_hbm, energy_hbm, pixels_hbm, dest_hbm, out, field, phases, energy, pixels, dest, read_ref, hot_ref, sems):
    blocks, size = phases.shape
    pairs = ((pixels_hbm, pixels), (phases_hbm, phases), (energy_hbm, energy), (dest_hbm, dest), (field_hbm, field))
    copies = [pltpu.make_async_copy(source, target, sems.at[k]) for k, (source, target) in enumerate(pairs)]
    for copy in copies:
        copy.start()
    for copy in copies[:-1]:
        copy.wait()
    grid = field.shape[1]
    place, _ = cells(pixels[...], grid)
    fill(place, blocks, size, 2 * grid, hot_ref)
    turn = (jnp.cos(phases[...]), jnp.sin(phases[...]))
    square = (blocks, blocks)
    own = lax.broadcasted_iota(jnp.int32, square, 0) == lax.broadcasted_iota(jnp.int32, square, 1)
    goals = jnp.where(own, jnp.broadcast_to(dest[0:1, :].astype(F32), square), 0.0)
    out[3 * blocks : 4 * blocks, :] = jnp.broadcast_to(jnp.sum(goals, axis=1, keepdims=True), (blocks, size))
    out[2 * blocks : 3 * blocks, :] = pixels[...].astype(F32)
    copies[-1].wait()
    new_phases, new_energy = kick(
        field[0], field[1], phases[...], energy[...], pixels[...], read_ref, hot_ref, turn=turn
    )
    out[0:blocks, :] = new_phases
    out[blocks : 2 * blocks, :] = new_energy


def by_destination(kinds):
    goals = kinds[-1]
    blocks = goals.shape[0]
    place = lax.broadcasted_iota(jnp.int32, goals.shape, 0)
    rank = jnp.zeros(goals.shape, jnp.int32)
    for block in range(blocks):
        goal = goals[block : block + 1]
        ahead = (goal < goals) | ((goal == goals) & (place > block))
        rank = rank + jnp.where(ahead, 1, 0)
    ordered = [jnp.zeros(kind.shape, F32) for kind in kinds]
    for block in range(blocks):
        here = rank[block : block + 1] == place
        ordered = [jnp.where(here, kind[block : block + 1], old) for kind, old in zip(kinds, ordered)]
    return ordered


def lane_groups(values, shifts):
    size = values[0].shape[1]
    group = lax.broadcasted_iota(jnp.int32, values[0].shape, 1) // (size // len(values))
    joined_up = None
    for k, (value, shift) in enumerate(zip(values, shifts)):
        if shift % size:
            value = pltpu.roll(value, shift % size, axis=1)
        joined_up = value if joined_up is None else jnp.where(group == k, value, joined_up)
    return joined_up


def radiate(blocks, dropped, field, state, form, out, hot_ref, spread_ref):
    pixels = state[2 * blocks : 3 * blocks, :].astype(jnp.int32)
    real, imag = emit(field[0], field[1], state[0:blocks, :], pixels, hot_ref, spread_ref, False)
    real, imag = diffract(real, imag, *form)
    keep = kept_unless(dropped)
    out[0] = real * keep
    out[1] = imag * keep


def first_radiate_kernel(blocks, dropped, field, state, propagator, *rest):
    *rest, hot_ref, spread_ref = rest
    if len(rest) > 3:
        *tables, out, high, low, matrix = rest
        matrix[...] = filter_matrix(*tables)
    else:
        out, high, low = rest
    form = real_form(propagator)
    high[...], low[...] = form
    radiate(blocks, dropped, field, state, form, out, hot_ref, spread_ref)


def third_radiate_kernel(blocks, field, state, high, low, out, hot_ref, spread_ref):
    needed = position() > 1

    @pl.when(needed)
    def _():
        radiate(blocks, 1, field, state, (high[...], low[...]), out, hot_ref, spread_ref)

    @pl.when(jnp.logical_not(needed))
    def _():
        out[...] = jnp.zeros(out.shape, F32)


def second_kernel(count, rows, cap, field, state, high, low, out, *rest):
    sends = rest[:-3]
    read_ref, hot_ref, spread_ref = rest[-3:]
    blocks, size = state.shape[0] // 4, state.shape[1]
    real, imag = field[0], field[1]
    grid = real.shape[0]
    pixels = state[2 * blocks : 3 * blocks, :].astype(jnp.int32)
    dark = position() == count - 1
    phases, energy = kick(
        real, imag, state[0:blocks, :], state[blocks : 2 * blocks, :], pixels, read_ref, hot_ref, dark
    )
    kinds = by_destination((phases, energy, state[2 * blocks : 3 * blocks, :], state[3 * blocks : 4 * blocks, :]))
    if rows:
        pairs, pieces = rows // 2, len(kinds)
        tiles = 2 * pairs + 1
        width = size // pieces
        for chunk in range(blocks // cap):
            parts = [kind[chunk * cap : (chunk + 1) * cap] for kind in kinds]
            for piece in range(pieces):
                row = lane_groups(parts, [(k - piece) * width for k in range(pieces)])
                out[pl.ds((piece * cap + 1) * tiles - 1, cap, stride=tiles), chunk, :] = row
    else:
        cuts = len(sends)
        cut = lax.div(lax.rem(position() + 1, count), count // cuts)
        for ahead, send in enumerate(sends):
            wanted = lax.rem(cut + ahead, cuts).astype(F32)
            chunk = [jnp.zeros((cap, size), F32)] * 2 + [jnp.full((cap, size), -1.0, F32)]
            for start in range(0, blocks, cap):
                goes = kinds[3][start : start + cap] == wanted
                chunk = [jnp.where(goes, kind[start : start + cap], old) for kind, old in zip(kinds, chunk)]
            for kind in range(3):
                send[kind * cap : (kind + 1) * cap, :] = chunk[kind]
    real, imag = emit(real, imag, phases, pixels, hot_ref, spread_ref, True)
    real, imag = diffract(real, imag, high[...], low[...])
    keep = kept_unless(count - 2)
    real, imag = real * keep, imag * keep
    if rows:
        for part in range(grid // rows):
            for pair in range(pairs):
                first = part * rows + 2 * pair
                out[part * tiles + pair] = real[first : first + 2]
                out[part * tiles + pairs + pair] = imag[first : first + 2]
    else:
        out[0] = real
        out[1] = imag


def filter_matrix(transmit, cos_out, sin_out, cos_in, sin_in):
    gain_real, gain_imag = transmit[0:1, :], transmit[1:2, :]
    cosine, sine = cos_out[...], sin_out[...]
    real = cosine * gain_real - sine * gain_imag
    imag = cosine * gain_imag + sine * gain_real
    full_real = exact_dot(real, cos_in[...]) + exact_dot(imag, sin_in[...])
    full_imag = exact_dot(imag, cos_in[...]) - exact_dot(real, sin_in[...])
    form = jnp.concatenate(
        [
            jnp.concatenate([full_real, -full_imag], axis=1),
            jnp.concatenate([full_imag, full_real], axis=1),
        ],
        axis=0,
    )
    high, low = split(form)
    return jnp.concatenate([high, high, low], axis=1)


def filter_kernel(cuts, chunk_count, matrix, data, out):
    count = out.shape[0] // 3
    rows, size = out.shape[1:]
    groups = count // cuts
    pairs = rows // 2
    tiles = 2 * pairs + 1
    stacked = jnp.concatenate(
        [
            jnp.concatenate(
                [data[pl.ds(part * pairs + j // 2, count, stride=tiles), j % 2, :] for part in range(2)], axis=0
            )
            for j in range(rows)
        ],
        axis=1,
    )
    high, low = split(stacked)
    result = dot(matrix[...], jnp.concatenate([high, low, high], axis=0), 1, 0)
    for part in range(2):
        for j in range(rows):
            out[pl.ds(part, count, stride=3), j, :] = result[
                part * count : (part + 1) * count, j * size : (j + 1) * size
            ]
    bundles = [
        pltpu.roll(data[pl.ds(tiles - 1, count, stride=tiles), chunk, :], 1, axis=0)
        for chunk in range(chunk_count)
    ]
    goals = [bundle[:, size - 1 : size] for bundle in bundles]
    for cut in range(cuts):
        chosen = bundles[0]
        for bundle, goal in zip(bundles[1:], goals[1:]):
            chosen = jnp.where(goal == float(cut), bundle, chosen)
        first = cut * groups + 2
        fits = min(groups, count - first)
        for source in range(cuts):
            tile = chosen[source * groups : (source + 1) * groups]
            out[pl.ds(3 * first + 2, fits, stride=3), source, :] = tile[:fits]
            for k in range(fits, groups):
                out[3 * (first + k - count) + 2, source : source + 1, :] = tile[k : k + 1]


def joined(chunks_in):
    cap = chunks_in[0].shape[0] // 3
    kinds = [
        jnp.concatenate([chunk[kind * cap : (kind + 1) * cap, :] for chunk in chunks_in], axis=0)
        for kind in range(3)
    ]
    return kinds[0], kinds[1], kinds[2].astype(jnp.int32)


def relayed(fields, cuts):
    count = fields.shape[0] // 3
    size = fields.shape[2]
    width = size // KINDS
    bundles = [fields[pl.ds(2, count, stride=3), cut, :] for cut in range(cuts)]
    kinds = [lane_groups(bundles, [(cut - kind) * width for cut in range(cuts)]) for kind in range(KINDS)]
    wanted = lax.div(lax.rem(position() + (count - 2), count), count // cuts).astype(F32)
    return kinds[0], kinds[1], jnp.where(kinds[3] == wanted, kinds[2], -1.0).astype(jnp.int32)


def third_kernel(cuts, fields, *rest):
    out, state, read_ref = rest[-3:]
    chunks_in = rest[:-3]
    if chunks_in:
        phases, energy, pixels = joined(chunks_in)
        out[...] = fields[...]
    else:
        phases, energy, pixels = relayed(fields, cuts)
        rows = fields.shape[1]
        for part in range(fields.shape[0] // 3):
            for kind in range(2):
                out[kind, part * rows : (part + 1) * rows, :] = fields[3 * part + kind]
    phases, energy = kick(out[0], out[1], phases, energy, pixels, read_ref)
    blocks = phases.shape[0]
    state[0:blocks, :] = phases
    state[blocks : 2 * blocks, :] = energy
    state[2 * blocks : 3 * blocks, :] = pixels.astype(F32)


def fourth_kernel(field, state, high, low, out, read_ref, hot_ref, spread_ref):
    blocks = state.shape[0] // 3
    needed = position() > 0

    @pl.when(needed)
    def _():
        pixels = state[2 * blocks : 3 * blocks, :].astype(jnp.int32)
        real, imag = field[0], field[1]
        dark = position() == 1
        phases, _ = kick(
            real, imag, state[0:blocks, :], state[blocks : 2 * blocks, :], pixels, read_ref, hot_ref, dark
        )
        real, imag = emit(real, imag, phases, pixels, hot_ref, spread_ref, True)
        out[0], out[1] = diffract(real, imag, high[...], low[...])

    @pl.when(jnp.logical_not(needed))
    def _():
        out[...] = jnp.zeros(out.shape, F32)


def call(kernel, out_shape, scratch, flops, args, memory=pltpu.VMEM):
    specs = [pl.BlockSpec(memory_space=memory)] * len(args)
    return pl.pallas_call(
        kernel,
        out_shape=out_shape,
        in_specs=specs,
        out_specs=jax.tree.map(lambda _: pl.BlockSpec(memory_space=pltpu.VMEM), out_shape),
        scratch_shapes=scratch,
        compiler_params=pltpu.CompilerParams(vmem_limit_bytes=VMEM_LIMIT),
        cost_estimate=pl.CostEstimate(flops=flops, bytes_accessed=1 << 19, transcendentals=0),
    )(*args)


def time_tables(count):
    times = jnp.arange(count, dtype=jnp.int32)
    cos_out, sin_out = angle_table((times + (count - 4)) % count, times, count)
    return (cos_out / count, sin_out / count, *angle_table(times, times, count))


def angle_table(first_ids, second_ids, total_slices):
    product = first_ids[:, None] * second_ids[None, :] % total_slices
    angle = product.astype(F32) * (2.0 * math.pi / total_slices)
    return jnp.cos(angle), jnp.sin(angle)


def filter_any(field, transmit, count):
    grid = field.shape[1]
    span = grid * grid
    share = -(-span // count)
    flat = jnp.pad(field.reshape(2, span), ((0, 0), (0, share * count - span)))
    parts = flat.reshape(2, count, share).transpose(1, 0, 2)
    got = lax.all_to_all(parts, AXES, split_axis=0, concat_axis=0, tiled=True)
    got = jnp.roll(got, 2, axis=0)
    real, imag = got[:, 0], got[:, 1]
    times = jnp.arange(count, dtype=jnp.int32)
    cosine, sine = angle_table(times, times, count)
    spec_real = exact_dot(cosine, real) + exact_dot(sine, imag)
    spec_imag = exact_dot(cosine, imag) - exact_dot(sine, real)
    gain_real, gain_imag = transmit[0][:, None], transmit[1][:, None]
    shaped_real = gain_real * spec_real - gain_imag * spec_imag
    shaped_imag = gain_real * spec_imag + gain_imag * spec_real
    back_real = (exact_dot(cosine, shaped_real) - exact_dot(sine, shaped_imag)) / count
    back_imag = (exact_dot(cosine, shaped_imag) + exact_dot(sine, shaped_real)) / count
    back = jnp.stack([back_real, back_imag], axis=1)
    sent = jnp.roll(back, 2, axis=0)
    fields = lax.all_to_all(sent, AXES, split_axis=0, concat_axis=0, tiled=True)
    fields = fields.transpose(1, 0, 2).reshape(2, share * count)[:, :span]
    return fields.reshape(2, grid, grid)


def on_device(radiation, phases, energy, pixels, destination, propagator, transmit):
    cuts, groups = lax.axis_size("cuts"), lax.axis_size("group")
    count = cuts * groups
    grid = radiation.shape[-1]
    blocks, size = phases.shape[1:]
    cap = max(2, 2 * blocks // cuts)
    rows = grid // count if grid % count == 0 else 0
    if rows != 4 or cap * KINDS != count or cuts != KINDS or size % 128 or blocks != 2 * cap or groups % 8:
        rows = 0
    field = radiation[0]
    shape = lambda *dims: jax.ShapeDtypeStruct(dims, F32)
    read = lambda number: pltpu.VMEM((2, number, size), F32)
    hot = lambda number: [pltpu.VMEM((2 * grid, number * size), BF16), pltpu.VMEM((grid, number * size), BF16)]
    pass_flops = 4 * blocks * size * grid * grid
    prop_flops = 48 * grid**3

    given = (field, phases[0], energy[0], pixels[0], destination)
    state = call(
        kick_kernel, shape(4 * blocks, size),
        [
            pltpu.VMEM((2, grid, grid), F32),
            pltpu.VMEM((blocks, size), F32),
            pltpu.VMEM((blocks, size), F32),
            pltpu.VMEM((blocks, size), jnp.int32),
            pltpu.VMEM((1, blocks), jnp.int32),
            read(blocks),
            hot(blocks)[0],
            pltpu.SemaphoreType.DMA((5,)),
        ],
        pass_flops, tuple(pltpu.with_memory_space_constraint(value, pltpu.HBM) for value in given), pl.ANY,
    )
    route = [((i + 1) % count, i) for i in range(count)]
    behind = lax.ppermute(state, AXES, route)
    form_shape = jax.ShapeDtypeStruct((4 * grid, 2 * grid), BF16)
    made = [shape(2, grid, grid), form_shape, form_shape]
    tables = ()
    if rows:
        made.append(jax.ShapeDtypeStruct((2 * count, 6 * count), BF16))
        tables = (transmit, *time_tables(count))
    field, *form = call(
        functools.partial(first_radiate_kernel, blocks, count - 1), made, hot(blocks), pass_flops + prop_flops,
        (field, state, propagator, *tables),
    )
    matrix = form[2:]
    form = form[:2]
    part_shape = shape(count * (rows + 1), 2, grid) if rows else shape(2, grid, grid)
    send_shapes = [] if rows else [shape(3 * cap, size)] * cuts
    field, *sends = call(
        functools.partial(second_kernel, count, rows, cap), (part_shape, *send_shapes),
        [read(blocks)] + hot(blocks), 2 * pass_flops + prop_flops,
        (field, behind, *form),
    )
    chunks_in = [
        lax.ppermute(send, AXES, [(i, (i + 3 + groups * ahead) % count) for i in range(count)])
        for ahead, send in enumerate(sends)
    ]
    if rows:
        data = lax.all_to_all(field, AXES, split_axis=0, concat_axis=0, tiled=True)
        sent = call(
            functools.partial(filter_kernel, cuts, blocks // cap), shape(count * 3, rows, grid), [], 1 << 24,
            (*matrix, data),
        )
        fields = lax.all_to_all(sent, AXES, split_axis=0, concat_axis=0, tiled=True)
    else:
        fields = filter_any(field, transmit, count)
    capacity = cuts * cap
    share = capacity // blocks
    field, state = call(
        functools.partial(third_kernel, cuts), (shape(2, grid, grid), shape(3 * capacity, size)),
        [read(capacity)], share * pass_flops, (fields, *chunks_in),
    )
    behind = lax.ppermute(state, AXES, route)
    field = call(
        functools.partial(third_radiate_kernel, capacity), shape(2, grid, grid), hot(capacity),
        share * pass_flops + prop_flops, (field, state, *form),
    )
    out = call(
        fourth_kernel, shape(2, grid, grid), [read(capacity)] + hot(capacity),
        2 * share * pass_flops + prop_flops, (field, behind, *form),
    )
    return out[None]


def solution(mesh):
    return jax.shard_map(
        on_device,
        mesh=mesh,
        in_specs=(
            P(("cuts", "group"), None, None, None),
            P(("cuts", "group"), None, None),
            P(("cuts", "group"), None, None),
            P(("cuts", "group"), None, None),
            P(("cuts", "group"), None),
            P(),
            P(),
        ),
        out_specs=P(("cuts", "group"), None, None, None),
        check_vma=False,
    )
```

```python
import functools
import math

import jax
import jax.numpy as jnp
from jax import lax
from jax.experimental import pallas as pl
from jax.experimental.pallas import tpu as pltpu
from jax.sharding import PartitionSpec as P

KICK_RATE = 0.5
PHASE_RATE = 1.0
EMIT_RATE = 0.5

AXES = ("cuts", "group")
F32 = jnp.float32
BF16 = jnp.bfloat16
KINDS = 4
VMEM_LIMIT = 48 * 1024 * 1024


def dot(left, right, left_dim, right_dim):
    dims = (((left_dim,), (right_dim,)), ((), ()))
    return lax.dot_general(left, right, dims, preferred_element_type=F32)


def exact_dot(left, right):
    return jnp.dot(left, right, precision=lax.Precision.HIGHEST, preferred_element_type=F32)


def split(value):
    high = value.astype(BF16)
    return high, (value - high.astype(F32)).astype(BF16)


def real_form(propagator):
    prop_real, prop_imag = propagator[0], propagator[1]
    form = jnp.concatenate(
        [
            jnp.concatenate([prop_real, -prop_imag], axis=1),
            jnp.concatenate([prop_imag, prop_real], axis=1),
        ],
        axis=0,
    )
    return split(form)


def diffract(real, imag, form_high, form_low):
    size = real.shape[0]
    high, low = split(jnp.concatenate([real, imag], axis=1))
    both = dot(jnp.concatenate([high, low], axis=0), form_high, 1, 1)
    right = both[:size] + both[size:] + dot(high, form_low, 1, 1)
    high, low = split(jnp.concatenate([right[:, :size], right[:, size:]], axis=0))
    both = dot(form_high, jnp.concatenate([high, low], axis=1), 1, 0)
    out = both[:, :size] + both[:, size:] + dot(form_low, high, 1, 0)
    return out[:size], out[size:]


def cells(pixels, grid):
    half = grid // 2
    shift = grid.bit_length() - 1
    if grid == 1 << shift:
        row, col = lax.shift_right_arithmetic(pixels, shift), pixels & (grid - 1)
    else:
        row, col = pixels // grid, pixels % grid
    right = col >= half
    place = jnp.where(pixels < 0, -1, jnp.where(right, row + grid, row))
    return place, jnp.where(right, col - half, col)


def swapped(value):
    half = value.shape[1] // 2
    return jnp.concatenate([value[:, half:], value[:, :half]], axis=1)


def fold(first, second):
    left = lax.broadcasted_iota(jnp.int32, first.shape, 1) < first.shape[1] // 2
    return jnp.where(left, first, swapped(second)), jnp.where(left, swapped(first), second)


def chunks(blocks):
    width = next(width for width in (4, 2, 1) if blocks % width == 0)
    return [(start, width) for start in range(0, blocks, width)]


def lanes(array, start, width):
    return jnp.concatenate([array[start + k : start + k + 1] for k in range(width)], axis=1)


def hits(ids, span):
    return lax.broadcasted_iota(jnp.int32, (span, ids.shape[1]), 0) == ids


def one_hot(place, start, width, span):
    ids = lanes(place, start, width).astype(F32)
    rows = lax.broadcasted_iota(jnp.int32, (span, ids.shape[1]), 0).astype(F32)
    if span <= 256:
        ids, rows = ids.astype(BF16), rows.astype(BF16)
    one, zero = jnp.ones((), BF16), jnp.zeros((), BF16)
    return jnp.where(rows == ids, one, zero)


def fill(place, blocks, size, span, hot_ref):
    for start, width in chunks(blocks):
        hot_ref[:, start * size : (start + width) * size] = one_hot(place, start, width, span)


def kick(real, imag, phases, energy, pixels, read_ref, hot_ref=None, dark=None, turn=None):
    grid = real.shape[0]
    half = grid // 2
    blocks, size = phases.shape
    place, col = cells(pixels, grid)

    def read():
        upper, lower = fold(real, imag)
        low = jnp.concatenate([upper, lower], axis=0).astype(BF16)
        for start, width in chunks(blocks):
            where = slice(start * size, (start + width) * size)
            hot = hot_ref[:, where] if turn else one_hot(place, start, width, 2 * grid)
            if hot_ref is not None and not turn:
                hot_ref[:, where] = hot
            picked = dot(low, hot, 0, 0)
            col_hit = hits(lanes(col, start, width), half)
            for part in range(2):
                value = picked[part * half : (part + 1) * half]
                value = jnp.sum(jnp.where(col_hit, value, 0.0), axis=0, keepdims=True)
                for k in range(width):
                    read_ref[part, start + k : start + k + 1, :] = value[:, k * size : (k + 1) * size]

    if dark is None:
        read()
    else:
        pl.when(jnp.logical_not(dark))(read)

        @pl.when(dark)
        def _():
            read_ref[...] = jnp.zeros(read_ref.shape, F32)
            fill(place, blocks, size, 2 * grid, hot_ref)

    cosine, sine = turn or (jnp.cos(phases), jnp.sin(phases))
    read_real = read_ref[0, :blocks, :]
    read_imag = read_ref[1, :blocks, :]
    energy = energy - KICK_RATE * (read_real * cosine - read_imag * sine)
    return phases + PHASE_RATE * energy, energy


def emit(real, imag, phases, pixels, hot_ref, spread_ref, filled):
    grid = real.shape[0]
    half = grid // 2
    blocks, size = phases.shape
    place, col = cells(pixels, grid)
    weight_real = jnp.cos(phases)
    weight_imag = -jnp.sin(phases)
    for start, width in chunks(blocks):
        where = slice(start * size, (start + width) * size)
        if not filled:
            hot_ref[:, where] = one_hot(place, start, width, 2 * grid)
        col_hit = hits(lanes(col, start, width), half)
        for part, weight in ((0, weight_real), (1, weight_imag)):
            value = jnp.where(col_hit, lanes(weight, start, width), 0.0)
            spread_ref[part * half : (part + 1) * half, where] = value.astype(BF16)
    span = blocks * size
    source = dot(hot_ref[:, :span], spread_ref[:, :span], 1, 1)
    source_real, source_imag = fold(source[:grid], source[grid:])
    return real + EMIT_RATE * source_real, imag + EMIT_RATE * source_imag


def position():
    return lax.axis_index("cuts") * lax.axis_size("group") + lax.axis_index("group")


def kept_unless(index):
    return jnp.where(position() == index, 0.0, 1.0).astype(F32)


def kick_kernel(field_hbm, phases_hbm, energy_hbm, pixels_hbm, dest_hbm, out, field, phases, energy, pixels, dest, read_ref, hot_ref, sems):
    blocks, size = phases.shape
    pairs = ((pixels_hbm, pixels), (phases_hbm, phases), (energy_hbm, energy), (dest_hbm, dest), (field_hbm, field))
    copies = [pltpu.make_async_copy(source, target, sems.at[k]) for k, (source, target) in enumerate(pairs)]
    for copy in reversed(copies):
        copy.start()
    for copy in copies[:-1]:
        copy.wait()
    grid = field.shape[1]
    place, _ = cells(pixels[...], grid)
    fill(place, blocks, size, 2 * grid, hot_ref)
    turn = (jnp.cos(phases[...]), jnp.sin(phases[...]))
    square = (blocks, blocks)
    own = lax.broadcasted_iota(jnp.int32, square, 0) == lax.broadcasted_iota(jnp.int32, square, 1)
    goals = jnp.where(own, jnp.broadcast_to(dest[0:1, :].astype(F32), square), 0.0)
    out[3 * blocks : 4 * blocks, :] = jnp.broadcast_to(jnp.sum(goals, axis=1, keepdims=True), (blocks, size))
    out[2 * blocks : 3 * blocks, :] = pixels[...].astype(F32)
    copies[-1].wait()
    new_phases, new_energy = kick(
        field[0], field[1], phases[...], energy[...], pixels[...], read_ref, hot_ref, turn=turn
    )
    out[0:blocks, :] = new_phases
    out[blocks : 2 * blocks, :] = new_energy


def by_destination(kinds):
    goals = kinds[-1]
    blocks = goals.shape[0]
    place = lax.broadcasted_iota(jnp.int32, goals.shape, 0)
    rank = jnp.zeros(goals.shape, jnp.int32)
    for block in range(blocks):
        goal = goals[block : block + 1]
        ahead = (goal < goals) | ((goal == goals) & (place > block))
        rank = rank + jnp.where(ahead, 1, 0)
    ordered = [jnp.zeros(kind.shape, F32) for kind in kinds]
    for block in range(blocks):
        here = rank[block : block + 1] == place
        ordered = [jnp.where(here, kind[block : block + 1], old) for kind, old in zip(kinds, ordered)]
    return ordered


def lane_groups(values, shifts):
    size = values[0].shape[1]
    group = lax.broadcasted_iota(jnp.int32, values[0].shape, 1) // (size // len(values))
    joined_up = None
    for k, (value, shift) in enumerate(zip(values, shifts)):
        if shift % size:
            value = pltpu.roll(value, shift % size, axis=1)
        joined_up = value if joined_up is None else jnp.where(group == k, value, joined_up)
    return joined_up


def radiate(blocks, dropped, field, state, form, out, hot_ref, spread_ref):
    pixels = state[2 * blocks : 3 * blocks, :].astype(jnp.int32)
    real, imag = emit(field[0], field[1], state[0:blocks, :], pixels, hot_ref, spread_ref, False)
    real, imag = diffract(real, imag, *form)
    keep = kept_unless(dropped)
    out[0] = real * keep
    out[1] = imag * keep


def first_radiate_kernel(blocks, dropped, field, state, propagator, *rest):
    *rest, hot_ref, spread_ref = rest
    if len(rest) > 3:
        *tables, out, high, low, matrix = rest
        matrix[...] = filter_matrix(*tables)
    else:
        out, high, low = rest
    form = real_form(propagator)
    high[...], low[...] = form
    radiate(blocks, dropped, field, state, form, out, hot_ref, spread_ref)


def third_radiate_kernel(blocks, field, state, high, low, out, hot_ref, spread_ref):
    needed = position() > 1

    @pl.when(needed)
    def _():
        radiate(blocks, 1, field, state, (high[...], low[...]), out, hot_ref, spread_ref)

    @pl.when(jnp.logical_not(needed))
    def _():
        out[...] = jnp.zeros(out.shape, F32)


def second_kernel(count, rows, cap, field, state, high, low, out, *rest):
    sends = rest[:-3]
    read_ref, hot_ref, spread_ref = rest[-3:]
    blocks, size = state.shape[0] // 4, state.shape[1]
    real, imag = field[0], field[1]
    grid = real.shape[0]
    pixels = state[2 * blocks : 3 * blocks, :].astype(jnp.int32)
    dark = position() == count - 1
    phases, energy = kick(
        real, imag, state[0:blocks, :], state[blocks : 2 * blocks, :], pixels, read_ref, hot_ref, dark
    )
    kinds = by_destination((phases, energy, state[2 * blocks : 3 * blocks, :], state[3 * blocks : 4 * blocks, :]))
    if rows:
        pairs, pieces = rows // 2, len(kinds)
        tiles = 2 * pairs + 1
        width = size // pieces
        for chunk in range(blocks // cap):
            parts = [kind[chunk * cap : (chunk + 1) * cap] for kind in kinds]
            for piece in range(pieces):
                row = lane_groups(parts, [(k - piece) * width for k in range(pieces)])
                out[pl.ds((piece * cap + 1) * tiles - 1, cap, stride=tiles), chunk, :] = row
    else:
        cuts = len(sends)
        cut = lax.div(lax.rem(position() + 1, count), count // cuts)
        for ahead, send in enumerate(sends):
            wanted = lax.rem(cut + ahead, cuts).astype(F32)
            chunk = [jnp.zeros((cap, size), F32)] * 2 + [jnp.full((cap, size), -1.0, F32)]
            for start in range(0, blocks, cap):
                goes = kinds[3][start : start + cap] == wanted
                chunk = [jnp.where(goes, kind[start : start + cap], old) for kind, old in zip(kinds, chunk)]
            for kind in range(3):
                send[kind * cap : (kind + 1) * cap, :] = chunk[kind]
    real, imag = emit(real, imag, phases, pixels, hot_ref, spread_ref, True)
    real, imag = diffract(real, imag, high[...], low[...])
    keep = kept_unless(count - 2)
    real, imag = real * keep, imag * keep
    if rows:
        for part in range(grid // rows):
            for pair in range(pairs):
                first = part * rows + 2 * pair
                out[part * tiles + pair] = real[first : first + 2]
                out[part * tiles + pairs + pair] = imag[first : first + 2]
    else:
        out[0] = real
        out[1] = imag


def filter_matrix(transmit, cos_out, sin_out, cos_in, sin_in):
    gain_real, gain_imag = transmit[0:1, :], transmit[1:2, :]
    cosine, sine = cos_out[...], sin_out[...]
    real = cosine * gain_real - sine * gain_imag
    imag = cosine * gain_imag + sine * gain_real
    full_real = exact_dot(real, cos_in[...]) + exact_dot(imag, sin_in[...])
    full_imag = exact_dot(imag, cos_in[...]) - exact_dot(real, sin_in[...])
    form = jnp.concatenate(
        [
            jnp.concatenate([full_real, -full_imag], axis=1),
            jnp.concatenate([full_imag, full_real], axis=1),
        ],
        axis=0,
    )
    high, low = split(form)
    return jnp.concatenate([high, high, low], axis=1)


def filter_kernel(cuts, chunk_count, matrix, data, out):
    count = out.shape[0] // 3
    rows, size = out.shape[1:]
    groups = count // cuts
    pairs = rows // 2
    tiles = 2 * pairs + 1
    stacked = jnp.concatenate(
        [
            jnp.concatenate(
                [data[pl.ds(part * pairs + j // 2, count, stride=tiles), j % 2, :] for part in range(2)], axis=0
            )
            for j in range(rows)
        ],
        axis=1,
    )
    high, low = split(stacked)
    result = dot(matrix[...], jnp.concatenate([high, low, high], axis=0), 1, 0)
    for part in range(2):
        for j in range(rows):
            out[pl.ds(part, count, stride=3), j, :] = result[
                part * count : (part + 1) * count, j * size : (j + 1) * size
            ]
    bundles = [
        pltpu.roll(data[pl.ds(tiles - 1, count, stride=tiles), chunk, :], 1, axis=0)
        for chunk in range(chunk_count)
    ]
    goals = [bundle[:, size - 1 : size] for bundle in bundles]
    for cut in range(cuts):
        chosen = bundles[0]
        for bundle, goal in zip(bundles[1:], goals[1:]):
            chosen = jnp.where(goal == float(cut), bundle, chosen)
        first = cut * groups + 2
        fits = min(groups, count - first)
        for source in range(cuts):
            tile = chosen[source * groups : (source + 1) * groups]
            out[pl.ds(3 * first + 2, fits, stride=3), source, :] = tile[:fits]
            for k in range(fits, groups):
                out[3 * (first + k - count) + 2, source : source + 1, :] = tile[k : k + 1]


def joined(chunks_in):
    cap = chunks_in[0].shape[0] // 3
    kinds = [
        jnp.concatenate([chunk[kind * cap : (kind + 1) * cap, :] for chunk in chunks_in], axis=0)
        for kind in range(3)
    ]
    return kinds[0], kinds[1], kinds[2].astype(jnp.int32)


def relayed(fields, cuts):
    count = fields.shape[0] // 3
    size = fields.shape[2]
    width = size // KINDS
    bundles = [fields[pl.ds(2, count, stride=3), cut, :] for cut in range(cuts)]
    kinds = [lane_groups(bundles, [(cut - kind) * width for cut in range(cuts)]) for kind in range(KINDS)]
    wanted = lax.div(lax.rem(position() + (count - 2), count), count // cuts).astype(F32)
    return kinds[0], kinds[1], jnp.where(kinds[3] == wanted, kinds[2], -1.0).astype(jnp.int32)


def third_kernel(cuts, fields, *rest):
    out, state, read_ref = rest[-3:]
    chunks_in = rest[:-3]
    if chunks_in:
        phases, energy, pixels = joined(chunks_in)
        out[...] = fields[...]
    else:
        phases, energy, pixels = relayed(fields, cuts)
        rows = fields.shape[1]
        for part in range(fields.shape[0] // 3):
            for kind in range(2):
                out[kind, part * rows : (part + 1) * rows, :] = fields[3 * part + kind]
    phases, energy = kick(out[0], out[1], phases, energy, pixels, read_ref)
    blocks = phases.shape[0]
    state[0:blocks, :] = phases
    state[blocks : 2 * blocks, :] = energy
    state[2 * blocks : 3 * blocks, :] = pixels.astype(F32)


def fourth_kernel(field, state, high, low, out, read_ref, hot_ref, spread_ref):
    blocks = state.shape[0] // 3
    needed = position() > 0

    @pl.when(needed)
    def _():
        pixels = state[2 * blocks : 3 * blocks, :].astype(jnp.int32)
        real, imag = field[0], field[1]
        dark = position() == 1
        phases, _ = kick(
            real, imag, state[0:blocks, :], state[blocks : 2 * blocks, :], pixels, read_ref, hot_ref, dark
        )
        real, imag = emit(real, imag, phases, pixels, hot_ref, spread_ref, True)
        out[0], out[1] = diffract(real, imag, high[...], low[...])

    @pl.when(jnp.logical_not(needed))
    def _():
        out[...] = jnp.zeros(out.shape, F32)


def call(kernel, out_shape, scratch, flops, args, memory=pltpu.VMEM):
    specs = [pl.BlockSpec(memory_space=memory)] * len(args)
    return pl.pallas_call(
        kernel,
        out_shape=out_shape,
        in_specs=specs,
        out_specs=jax.tree.map(lambda _: pl.BlockSpec(memory_space=pltpu.VMEM), out_shape),
        scratch_shapes=scratch,
        compiler_params=pltpu.CompilerParams(vmem_limit_bytes=VMEM_LIMIT),
        cost_estimate=pl.CostEstimate(flops=flops, bytes_accessed=1 << 19, transcendentals=0),
    )(*args)


def time_tables(count):
    times = jnp.arange(count, dtype=jnp.int32)
    cos_out, sin_out = angle_table((times + (count - 4)) % count, times, count)
    return (cos_out / count, sin_out / count, *angle_table(times, times, count))


def angle_table(first_ids, second_ids, total_slices):
    product = first_ids[:, None] * second_ids[None, :] % total_slices
    angle = product.astype(F32) * (2.0 * math.pi / total_slices)
    return jnp.cos(angle), jnp.sin(angle)


def filter_any(field, transmit, count):
    grid = field.shape[1]
    span = grid * grid
    share = -(-span // count)
    flat = jnp.pad(field.reshape(2, span), ((0, 0), (0, share * count - span)))
    parts = flat.reshape(2, count, share).transpose(1, 0, 2)
    got = lax.all_to_all(parts, AXES, split_axis=0, concat_axis=0, tiled=True)
    got = jnp.roll(got, 2, axis=0)
    real, imag = got[:, 0], got[:, 1]
    times = jnp.arange(count, dtype=jnp.int32)
    cosine, sine = angle_table(times, times, count)
    spec_real = exact_dot(cosine, real) + exact_dot(sine, imag)
    spec_imag = exact_dot(cosine, imag) - exact_dot(sine, real)
    gain_real, gain_imag = transmit[0][:, None], transmit[1][:, None]
    shaped_real = gain_real * spec_real - gain_imag * spec_imag
    shaped_imag = gain_real * spec_imag + gain_imag * spec_real
    back_real = (exact_dot(cosine, shaped_real) - exact_dot(sine, shaped_imag)) / count
    back_imag = (exact_dot(cosine, shaped_imag) + exact_dot(sine, shaped_real)) / count
    back = jnp.stack([back_real, back_imag], axis=1)
    sent = jnp.roll(back, 2, axis=0)
    fields = lax.all_to_all(sent, AXES, split_axis=0, concat_axis=0, tiled=True)
    fields = fields.transpose(1, 0, 2).reshape(2, share * count)[:, :span]
    return fields.reshape(2, grid, grid)


def on_device(radiation, phases, energy, pixels, destination, propagator, transmit):
    cuts, groups = lax.axis_size("cuts"), lax.axis_size("group")
    count = cuts * groups
    grid = radiation.shape[-1]
    blocks, size = phases.shape[1:]
    cap = max(2, 2 * blocks // cuts)
    rows = grid // count if grid % count == 0 else 0
    if rows != 4 or cap * KINDS != count or cuts != KINDS or size % 128 or blocks != 2 * cap or groups % 8:
        rows = 0
    field = radiation[0]
    shape = lambda *dims: jax.ShapeDtypeStruct(dims, F32)
    read = lambda number: pltpu.VMEM((2, number, size), F32)
    hot = lambda number: [pltpu.VMEM((2 * grid, number * size), BF16), pltpu.VMEM((grid, number * size), BF16)]
    pass_flops = 4 * blocks * size * grid * grid
    prop_flops = 48 * grid**3

    given = (field, phases[0], energy[0], pixels[0], destination)
    state = call(
        kick_kernel, shape(4 * blocks, size),
        [
            pltpu.VMEM((2, grid, grid), F32),
            pltpu.VMEM((blocks, size), F32),
            pltpu.VMEM((blocks, size), F32),
            pltpu.VMEM((blocks, size), jnp.int32),
            pltpu.VMEM((1, blocks), jnp.int32),
            read(blocks),
            hot(blocks)[0],
            pltpu.SemaphoreType.DMA((5,)),
        ],
        pass_flops, tuple(pltpu.with_memory_space_constraint(value, pltpu.HBM) for value in given), pl.ANY,
    )
    route = [((i + 1) % count, i) for i in range(count)]
    behind = lax.ppermute(state, AXES, route)
    form_shape = jax.ShapeDtypeStruct((2 * grid, 2 * grid), BF16)
    made = [shape(2, grid, grid), form_shape, form_shape]
    tables = ()
    if rows:
        made.append(jax.ShapeDtypeStruct((2 * count, 6 * count), BF16))
        tables = (transmit, *time_tables(count))
    field, *form = call(
        functools.partial(first_radiate_kernel, blocks, count - 1), made, hot(blocks), pass_flops + prop_flops,
        (field, state, propagator, *tables),
    )
    matrix = form[2:]
    form = form[:2]
    part_shape = shape(count * (rows + 1), 2, grid) if rows else shape(2, grid, grid)
    send_shapes = [] if rows else [shape(3 * cap, size)] * cuts
    field, *sends = call(
        functools.partial(second_kernel, count, rows, cap), (part_shape, *send_shapes),
        [read(blocks)] + hot(blocks), 2 * pass_flops + prop_flops,
        (field, behind, *form),
    )
    chunks_in = [
        lax.ppermute(send, AXES, [(i, (i + 3 + groups * ahead) % count) for i in range(count)])
        for ahead, send in enumerate(sends)
    ]
    if rows:
        data = lax.all_to_all(field, AXES, split_axis=0, concat_axis=0, tiled=True)
        sent = call(
            functools.partial(filter_kernel, cuts, blocks // cap), shape(count * 3, rows, grid), [], 1 << 24,
            (*matrix, data),
        )
        fields = lax.all_to_all(sent, AXES, split_axis=0, concat_axis=0, tiled=True)
    else:
        fields = filter_any(field, transmit, count)
    capacity = cuts * cap
    share = capacity // blocks
    field, state = call(
        functools.partial(third_kernel, cuts), (shape(2, grid, grid), shape(3 * capacity, size)),
        [read(capacity)], share * pass_flops, (fields, *chunks_in),
    )
    behind = lax.ppermute(state, AXES, route)
    field = call(
        functools.partial(third_radiate_kernel, capacity), shape(2, grid, grid), hot(capacity),
        share * pass_flops + prop_flops, (field, state, *form),
    )
    out = call(
        fourth_kernel, shape(2, grid, grid), [read(capacity)] + hot(capacity),
        2 * share * pass_flops + prop_flops, (field, behind, *form),
    )
    return out[None]


def solution(mesh):
    return jax.shard_map(
        on_device,
        mesh=mesh,
        in_specs=(
            P(("cuts", "group"), None, None, None),
            P(("cuts", "group"), None, None),
            P(("cuts", "group"), None, None),
            P(("cuts", "group"), None, None),
            P(("cuts", "group"), None),
            P(),
            P(),
        ),
        out_specs=P(("cuts", "group"), None, None, None),
        check_vma=False,
    )
```
